32 devices in a mesh: dp: 4 (over y, x), row: 4 (over z), col: 2 (over core).
Axes of the slice: x: 2, y: 2, z: 4, core: 2. Of those that a mesh axis runs over, the one named last changes fastest.
Arguments:
- outer_gate: bfloat16 [4, 8, 1024, 1024], P('dp', None, ('row', 'col')), may hold values from -6 to 6
- inner_gate: bfloat16 [4, 8, 1024, 1024], P('dp', None, ('row', 'col')), may hold values from -6 to 6
- signal: bfloat16 [4, 8, 1024, 1024], P('dp', None, ('row', 'col')), may hold values from -6 to 6
- grad_out: bfloat16 [4, 8, 1024, 1024], P('dp', None, ('row', 'col')), may hold values from -6 to 6
- filter_weight: float32 [1024, 1024], P(('row', 'col')), may hold values from -6 to 6
Outputs:
- grad_outer: bfloat16 [4, 8, 1024, 1024], P('dp', None, ('row', 'col'))
- grad_inner: bfloat16 [4, 8, 1024, 1024], P('dp', None, ('row', 'col'))
- grad_signal: bfloat16 [4, 8, 1024, 1024], P('dp', None, ('row', 'col'))
- grad_filter: float32 [1024, 1024], P(('row', 'col'))
The draws below stay inside these ranges and needn't reach their ends.
All inputs are finite; a program needn't handle non-finite values.
Results may differ from the reference program's by a relative error of at most 0.0013.
Values sent between devices are 32-bit elements; how exact they have to be, the bound alone decides.
No kernel may reach another device: no remote copies, remote signals or barrier semaphores. Data moves between devices by JAX's collectives and lax.ppermute only.
A program may use at most 192 MiB of HBM per device.

```python
import jax
import jax.numpy as jnp
from jax import lax

GRID = 1024
CH = 8
SEQS = 4


def level_of(own_key, extent, shards, least, high):
    def one(dim, blocks):
        heights = jax.random.uniform(jax.random.fold_in(jax.random.fold_in(own_key, 6), dim), (blocks,), jnp.float32, least / len(shards), high / len(shards))
        return jnp.repeat(jnp.exp(heights), extent[dim] // blocks).reshape((-1,) + (1,) * (len(extent) - dim - 1))

    factor_of = one(*shards[0])
    for cut in shards[1:]:
        factor_of = factor_of * one(*cut)
    return factor_of


def noise(stream_key, shape, scale, limit, shards=(), dtype=jnp.bfloat16):
    factor_of = level_of(stream_key, shape, shards, -0.22, 0.18) if shards else 1.0
    drawn = jax.random.normal(stream_key, shape, jnp.float32) * scale * factor_of
    return jnp.minimum(jnp.maximum(drawn, -limit), limit).astype(dtype)


def setup_inputs(seed: int = 0) -> dict:
    key_of = jax.random.split(jax.random.key(seed), 6)
    outer_gate = noise(key_of[0], (SEQS, CH, GRID, GRID), 1.0, 6.0, ((0, 4), (2, 8)))
    inner_gate = noise(key_of[1], (SEQS, CH, GRID, GRID), 1.0, 6.0, ((0, 4), (2, 8)))
    signal = noise(key_of[2], (SEQS, CH, GRID, GRID), 1.0, 6.0, ((0, 4), (2, 8)))
    grad_out = noise(key_of[3], (SEQS, CH, GRID, GRID), 1.0, 6.0, ((0, 4), (2, 8)))
    filter_weight = noise(key_of[4], (GRID, GRID), 1.0, 6.0, ((0, 8),), jnp.float32)
    return {"outer_gate": outer_gate, "inner_gate": inner_gate, "signal": signal, "grad_out": grad_out, "filter_weight": filter_weight}


def flatten_seq(array, seqs, total):
    return array.astype(jnp.float32).reshape(seqs, total)


def reference(outer_gate, inner_gate, signal, grad_out, filter_weight):
    total = GRID * GRID
    taps = filter_weight.astype(jnp.float32).reshape(total) * (1.0 / GRID)
    filt_spec = jnp.fft.fft(taps)

    def channel_grads(pieces):
        outer, inner, values, cotangent = pieces
        seqs = outer.shape[0]
        outer_f = flatten_seq(outer, seqs, total)
        inner_f = flatten_seq(inner, seqs, total)
        values_f = flatten_seq(values, seqs, total)
        grad_f = flatten_seq(cotangent, seqs, total)
        gated = inner_f * values_f
        gated_spec = jnp.fft.fft(gated, axis=-1)
        conv = jnp.real(jnp.fft.ifft(filt_spec[None, :] * gated_spec, axis=-1)).astype(jnp.float32)
        grad_outer = (grad_f * conv).astype(jnp.bfloat16)
        grad_conv = grad_f * outer_f
        conv_spec = jnp.fft.fft(grad_conv, axis=-1)
        grad_gated = jnp.real(jnp.fft.ifft(jnp.conj(filt_spec)[None, :] * conv_spec, axis=-1)).astype(jnp.float32)
        grad_inner = (grad_gated * values_f).astype(jnp.bfloat16)
        grad_signal = (grad_gated * inner_f).astype(jnp.bfloat16)
        filter_terms = jnp.real(jnp.fft.ifft(jnp.conj(gated_spec) * conv_spec, axis=-1)).astype(jnp.float32)
        shape = (seqs, GRID, GRID)
        return (grad_outer.reshape(shape), grad_inner.reshape(shape), grad_signal.reshape(shape),
                jnp.sum(filter_terms, axis=0).reshape(GRID, GRID))

    results = lax.map(channel_grads, (jnp.moveaxis(outer_gate, 1, 0), jnp.moveaxis(inner_gate, 1, 0),
                                      jnp.moveaxis(signal, 1, 0), jnp.moveaxis(grad_out, 1, 0)))
    grad_outer = jnp.moveaxis(results[0], 0, 1)
    grad_inner = jnp.moveaxis(results[1], 0, 1)
    grad_signal = jnp.moveaxis(results[2], 0, 1)
    grad_filter = jnp.sum(results[3], axis=0) * (1.0 / GRID)
    return grad_outer, grad_inner, grad_signal, grad_filter
```

```python
import functools
import math

import jax
import jax.numpy as jnp
import numpy as np
from jax import lax
from jax.experimental import pallas as pl
from jax.experimental.pallas import tpu as pltpu
from jax.sharding import PartitionSpec as P

TWO_PI = 2.0 * math.pi


def contract(form, left, right):
    return jnp.einsum(
        form, left, right, precision=lax.Precision.HIGHEST, preferred_element_type=jnp.float32
    )


def redistribute(blocks):
    return lax.all_to_all(blocks, ("row", "col"), split_axis=0, concat_axis=0, tiled=True)


def own_block():
    return lax.axis_index("row") * lax.axis_size("col") + lax.axis_index("col")


def turn_angles(first_index, second_index, total):
    product = first_index * second_index % total
    angles = product.astype(jnp.float32) * (TWO_PI / total)
    return (jnp.cos(angles), jnp.sin(angles))


def axis_dft(real, imag, sign):
    length, width = real.shape
    first = 1 << (length.bit_length() - 1) // 2
    second = length // first
    index_a = jnp.arange(first, dtype=jnp.int32)
    index_b = jnp.arange(second, dtype=jnp.int32)
    cos_a, sin_a = turn_angles(index_a[:, None], index_a[None, :], first)
    sin_a = sign * sin_a
    cos_b, sin_b = turn_angles(index_b[:, None], index_b[None, :], second)
    sin_b = sign * sin_b
    twist_cos, twist_sin = turn_angles(index_a[:, None], index_b[None, :], length)
    twist_cos = twist_cos[:, :, None]
    twist_sin = sign * twist_sin[:, :, None]
    real_three = real.reshape(first, second, width)
    step_real = contract("abm,ak->kbm", real_three, cos_a)
    step_imag = contract("abm,ak->kbm", real_three, sin_a)
    if imag is not None:
        imag_three = imag.reshape(first, second, width)
        step_real = step_real - contract("abm,ak->kbm", imag_three, sin_a)
        step_imag = step_imag + contract("abm,ak->kbm", imag_three, cos_a)
    turned_real = step_real * twist_cos - step_imag * twist_sin
    turned_imag = step_real * twist_sin + step_imag * twist_cos
    out_real = contract("kbm,bj->jkm", turned_real, cos_b) - contract(
        "kbm,bj->jkm", turned_imag, sin_b
    )
    out_imag = contract("kbm,bj->jkm", turned_real, sin_b) + contract(
        "kbm,bj->jkm", turned_imag, cos_b
    )
    return (out_real.reshape(length, width), out_imag.reshape(length, width))


def forward(stacked, order):
    count, block, grid_side = stacked.shape
    owners = grid_side // block
    total = grid_side * grid_side
    send = jnp.transpose(stacked.reshape(count, block, owners, block), (2, 1, 0, 3)).reshape(
        owners, block, count * block
    )
    columns = redistribute(send).reshape(grid_side, count * block)
    first_real, first_imag = axis_dft(columns, None, -1.0)
    first_real = first_real.reshape(grid_side, count, block)
    first_imag = first_imag.reshape(grid_side, count, block)
    col_index = own_block() * block + jnp.arange(block, dtype=jnp.int32)
    cos_turn, sin_turn = turn_angles(order[:, None, None], col_index[None, None, :], total)
    turned_real = first_real * cos_turn + first_imag * sin_turn
    turned_imag = first_imag * cos_turn - first_real * sin_turn
    send_two = jnp.concatenate([turned_real, turned_imag], axis=1).reshape(
        owners, block, 2 * count * block
    )
    gotten = redistribute(send_two).reshape(owners, block, 2 * count, block)
    flat_real = jnp.transpose(gotten[:, :, :count, :], (0, 3, 1, 2)).reshape(
        grid_side, block * count
    )
    flat_imag = jnp.transpose(gotten[:, :, count:, :], (0, 3, 1, 2)).reshape(
        grid_side, block * count
    )
    out_real, out_imag = axis_dft(flat_real, flat_imag, -1.0)
    spec_real = jnp.transpose(out_real.reshape(grid_side, block, count), (1, 2, 0))
    spec_imag = jnp.transpose(out_imag.reshape(grid_side, block, count), (1, 2, 0))
    return (spec_real, spec_imag)


def inverse(spec_real, spec_imag, order):
    block, count, grid_side = spec_real.shape
    owners = grid_side // block
    total = grid_side * grid_side
    flat_real = jnp.transpose(spec_real, (2, 0, 1)).reshape(grid_side, block * count)
    flat_imag = jnp.transpose(spec_imag, (2, 0, 1)).reshape(grid_side, block * count)
    out_real, out_imag = axis_dft(flat_real, flat_imag, 1.0)
    back_real = jnp.transpose(out_real.reshape(owners, block, block, count), (0, 2, 3, 1))
    back_imag = jnp.transpose(out_imag.reshape(owners, block, block, count), (0, 2, 3, 1))
    freq_index = lax.dynamic_slice_in_dim(order, own_block() * block, block, 0)
    col_index = (
        jnp.arange(owners, dtype=jnp.int32)[:, None] * block
        + jnp.arange(block, dtype=jnp.int32)[None, :]
    )
    cos_turn, sin_turn = turn_angles(
        freq_index[None, :, None, None], col_index[:, None, None, :], total
    )
    turned_real = back_real * cos_turn - back_imag * sin_turn
    turned_imag = back_real * sin_turn + back_imag * cos_turn
    send = jnp.concatenate([turned_real, turned_imag], axis=2).reshape(
        owners, block, 2 * count * block
    )
    gotten = redistribute(send).reshape(grid_side, 2 * count * block)
    real_part = gotten[:, : count * block]
    imag_part = gotten[:, count * block :]
    full_real, full_imag = axis_dft(real_part, imag_part, 1.0)
    values = full_real * (1.0 / total)
    returned = redistribute(values.reshape(owners, block, count * block)).reshape(
        owners, block, count, block
    )
    return jnp.transpose(returned, (2, 1, 0, 3)).reshape(count, block, grid_side)


def spread_shards(outer_gate, inner_gate, signal, grad_out, filter_weight):
    grid_side = filter_weight.shape[1]
    freq_index = jnp.arange(grid_side, dtype=jnp.int32)
    outer_f = outer_gate[0].astype(jnp.float32)
    inner_f = inner_gate[0].astype(jnp.float32)
    signal_f = signal[0].astype(jnp.float32)
    grad_f = grad_out[0].astype(jnp.float32)
    channels = inner_f.shape[0]
    gated = inner_f * signal_f
    grad_conv = grad_f * outer_f
    taps = (filter_weight * (1.0 / grid_side))[None]
    spec_real, spec_imag = forward(jnp.concatenate([gated, grad_conv], axis=0), freq_index)
    filt_real, filt_imag = forward(taps, freq_index)
    gated_real = spec_real[:, :channels]
    gated_imag = spec_imag[:, :channels]
    cot_real = spec_real[:, channels : 2 * channels]
    cot_imag = spec_imag[:, channels : 2 * channels]
    conv_real = filt_real * gated_real - filt_imag * gated_imag
    conv_imag = filt_real * gated_imag + filt_imag * gated_real
    back_real = filt_real * cot_real + filt_imag * cot_imag
    back_imag = filt_real * cot_imag - filt_imag * cot_real
    term_real = jnp.sum(gated_real * cot_real + gated_imag * cot_imag, axis=1, keepdims=True)
    term_imag = jnp.sum(gated_real * cot_imag - gated_imag * cot_real, axis=1, keepdims=True)
    values = inverse(
        jnp.concatenate([conv_real, back_real, term_real], axis=1),
        jnp.concatenate([conv_imag, back_imag, term_imag], axis=1),
        freq_index,
    )
    grad_filter = lax.psum(values[2 * channels], "dp") * (1.0 / grid_side)
    conv = values[:channels]
    grad_gated = values[channels : 2 * channels]
    grad_outer = (grad_f * conv).astype(jnp.bfloat16)[None]
    grad_inner = (grad_gated * signal_f).astype(jnp.bfloat16)[None]
    grad_signal = (grad_gated * inner_f).astype(jnp.bfloat16)[None]
    return (grad_outer, grad_inner, grad_signal, grad_filter)


VMEM_LIMIT = 40 * 1024 * 1024
ROW_PAD = 16
LANE_PAD = 128


def up_to(value, unit):
    return -(-value // unit) * unit


def high_low(table):
    high = table.astype(jnp.bfloat16)
    low = (table - high.astype(np.float64)).astype(jnp.bfloat16)
    return np.stack([high, low])


class Plan:
    def __init__(self, side):
        half = side // 2
        self.side, self.half, self.quarter = side, half, side // 4
        self.evens = up_to(half // 2 + 1, ROW_PAD)
        self.odds = half // 2
        self.rows = self.evens + self.odds
        self.even_depth = up_to(2 * self.evens, LANE_PAD)
        total = side * side
        even_k = 2 * np.arange(self.evens)
        odd_k = 2 * np.arange(self.odds) + 1
        live = (even_k <= half).astype(np.float64)
        p = np.arange(half)

        def waves(k, scale):
            angle = 2.0 * np.pi * (k[:, None] * p[None, :] % side) / side
            return np.concatenate([np.cos(angle) * scale[:, None], -np.sin(angle) * scale[:, None]])

        ones = np.ones(self.odds)
        self.into_even = high_low(waves(even_k, live))
        self.into_odd = high_low(waves(odd_k, ones))
        weight = np.where((even_k == 0) | (even_k == half), 1.0, 2.0) * live / total
        back_even = np.zeros((half, self.even_depth))
        back_even[:, : 2 * self.evens] = waves(even_k, weight).T
        self.back_even = high_low(back_even)
        self.back_odd = high_low(waves(odd_k, ones * 2.0 / total).T)
        k = np.concatenate([even_k, odd_k])
        turn = 2.0 * np.pi * (k[:, None] * np.arange(side)[None, :] % total) / total
        self.turn = np.stack([np.cos(turn), np.sin(turn)]).astype(np.float32)
        q = np.arange(self.quarter)
        mixes = []
        for r in range(4):
            angle = 2.0 * np.pi * (q[:, None] * (4 * q[None, :] + r) % side) / side
            cos, sin = np.cos(angle), np.sin(angle)
            mixes.append(np.block([[cos, -sin], [sin, cos]]))
        self.mix = high_low(np.stack(mixes))
        self.row_tile = next(t for t in (176, 264, 16, 8) if self.rows % t == 0)


def split_terms(values):
    high = values.astype(jnp.bfloat16)
    return high, (values - high.astype(jnp.float32)).astype(jnp.bfloat16)


def dot_in(table, rows, high, low):
    dot = functools.partial(jnp.dot, preferred_element_type=jnp.float32)
    first, second = table[0, rows], table[1, rows]
    return dot(first, high) + (dot(first, low) + dot(second, high))


def block_views(plan, owners, me, blocks, values):
    size = plan.side // owners
    for step in range(owners):
        at = pl.multiple_of((me[0] ^ step) * size, size)
        yield blocks[step], values.at[pl.ds(at, size)]


def tile_views(plan, grid, me, tiles, values):
    parts, rows, cols = grid
    height, width = plan.side // (rows * cols), plan.side // parts
    for part in range(parts):
        for row in range(rows):
            for col in range(cols):
                place = values.at[pl.ds((row * cols + col) * height, height), pl.ds(part * width, width)]
                yield tiles[0].at[part * cols + col, row], place


def copy_all(pairs, sems):
    copies = [pltpu.make_async_copy(source, to, sems.at[i]) for i, (source, to) in enumerate(pairs)]
    for copy in copies:
        copy.start()
    for copy in copies:
        copy.wait()


def forward_kernel(plan, views, count, me, *refs):
    blocks = refs[:count]
    into_even, into_odd, turn, mix, spec, values, mid, sems = refs[count:]
    side, half, quarter = plan.side, plan.half, plan.quarter
    copy_all(views(me, blocks, values), sems)

    @pl.loop(0, side // quarter)
    def columns(tile):
        cols = pl.ds(pl.multiple_of(tile * quarter, quarter), quarter)
        top, bottom = values[pl.ds(0, half), cols], values[pl.ds(half, half), cols]
        for first, count, table, part in (
            (0, plan.evens, into_even, top + bottom),
            (plan.evens, plan.odds, into_odd, top - bottom),
        ):
            out = dot_in(table, slice(None), *split_terms(part))
            real, imag = out[:count], out[count:]
            rows = pl.ds(first, count)
            cos, sin = turn[0, rows, cols], turn[1, rows, cols]
            mid[0, rows, cols] = real * cos + imag * sin
            mid[1, rows, cols] = imag * cos - real * sin

    @pl.loop(0, plan.rows // plan.row_tile)
    def rows_loop(tile):
        rows = pl.ds(pl.multiple_of(tile * plan.row_tile, plan.row_tile), plan.row_tile)
        real = [mid[0, rows, pl.ds(j * quarter, quarter)] for j in range(4)]
        imag = [mid[1, rows, pl.ds(j * quarter, quarter)] for j in range(4)]
        sum_r, sum_i = real[0] + real[2], imag[0] + imag[2]
        dif_r, dif_i = real[0] - real[2], imag[0] - imag[2]
        two_r, two_i = real[1] + real[3], imag[1] + imag[3]
        odd_r, odd_i = real[1] - real[3], imag[1] - imag[3]
        turns = (
            (sum_r + two_r, sum_i + two_i),
            (dif_r + odd_i, dif_i - odd_r),
            (sum_r - two_r, sum_i - two_i),
            (dif_r - odd_i, dif_i + odd_r),
        )
        dot = functools.partial(jnp.dot, preferred_element_type=jnp.float32)
        for r, pair in enumerate(turns):
            high, low = split_terms(jnp.concatenate(pair, axis=1))
            out = dot(high, mix[0, r]) + (dot(low, mix[0, r]) + dot(high, mix[1, r]))
            cols = pl.ds(r * quarter, quarter)
            spec[0, rows, cols] = out[:, :quarter]
            spec[1, rows, cols] = out[:, quarter:]


def inverse_kernel(plan, views, count, conjugate, me, left, right, back_even, back_odd, turn, mix, *refs):
    blocks = refs[:count]
    values, mid, sems = refs[count:]
    side, half, quarter = plan.side, plan.half, plan.quarter

    @pl.loop(0, plan.rows // plan.row_tile)
    def rows_loop(tile):
        rows = pl.ds(pl.multiple_of(tile * plan.row_tile, plan.row_tile), plan.row_tile)
        real, imag = [], []
        for r in range(4):
            cols = pl.ds(r * quarter, quarter)
            left_r, left_i = left[0, rows, cols], left[1, rows, cols]
            right_r, right_i = right[0, rows, cols], right[1, rows, cols]
            if conjugate:
                left_i = -left_i
            pair = (left_r * right_r - left_i * right_i, left_r * right_i + left_i * right_r)
            high, low = split_terms(jnp.concatenate(pair, axis=1))

            def dot(part, table):
                return lax.dot_general(
                    part, table, (((1,), (1,)), ((), ())), preferred_element_type=jnp.float32
                )

            out = dot(high, mix[0, r]) + (dot(low, mix[0, r]) + dot(high, mix[1, r]))
            real.append(out[:, :quarter])
            imag.append(out[:, quarter:])
        sum_r, sum_i = real[0] + real[2], imag[0] + imag[2]
        dif_r, dif_i = real[0] - real[2], imag[0] - imag[2]
        two_r, two_i = real[1] + real[3], imag[1] + imag[3]
        odd_r, odd_i = real[1] - real[3], imag[1] - imag[3]
        turns = (
            (sum_r + two_r, sum_i + two_i),
            (dif_r - odd_i, dif_i + odd_r),
            (sum_r - two_r, sum_i - two_i),
            (dif_r + odd_i, dif_i - odd_r),
        )
        for j, (got_r, got_i) in enumerate(turns):
            cols = pl.ds(j * quarter, quarter)
            cos, sin = turn[0, rows, cols], turn[1, rows, cols]
            mid[0, rows, cols] = got_r * cos - got_i * sin
            mid[1, rows, cols] = got_r * sin + got_i * cos

    @pl.loop(0, side // quarter)
    def columns(tile):
        cols = pl.ds(pl.multiple_of(tile * quarter, quarter), quarter)
        even = [mid[0, pl.ds(0, plan.evens), cols], mid[1, pl.ds(0, plan.evens), cols]]
        if plan.even_depth > 2 * plan.evens:
            even.append(jnp.zeros((plan.even_depth - 2 * plan.evens, quarter), jnp.float32))
        odd = [mid[0, pl.ds(plan.evens, plan.odds), cols], mid[1, pl.ds(plan.evens, plan.odds), cols]]
        from_even = dot_in(back_even, slice(None), *split_terms(jnp.concatenate(even)))
        from_odd = dot_in(back_odd, slice(None), *split_terms(jnp.concatenate(odd)))
        values[pl.ds(0, half), cols] = from_even + from_odd
        values[pl.ds(half, half), cols] = from_even - from_odd

    copy_all(((to, source) for source, to in views(me, blocks, values)), sems)


def smem():
    return pl.BlockSpec(memory_space=pltpu.SMEM)


def vmem():
    return pl.BlockSpec(memory_space=pltpu.VMEM)


def anywhere():
    return pl.BlockSpec(memory_space=pl.ANY)


def kernel_cost(plan):
    return pl.CostEstimate(flops=plan.side**2, bytes_accessed=plan.side**2, transcendentals=0)


def to_spectrum(plan, me, blocks, views, copies):
    count = len(blocks)
    shape = (2, plan.rows, plan.side)
    return pl.pallas_call(
        functools.partial(forward_kernel, plan, views, count),
        out_shape=jax.ShapeDtypeStruct(shape, jnp.float32),
        in_specs=[smem()] + [anywhere()] * count + [vmem()] * 4,
        out_specs=vmem(),
        scratch_shapes=[
            pltpu.VMEM((plan.side, plan.side), jnp.float32),
            pltpu.VMEM(shape, jnp.float32),
            pltpu.SemaphoreType.DMA((copies,)),
        ],
        compiler_params=pltpu.CompilerParams(vmem_limit_bytes=VMEM_LIMIT),
        cost_estimate=kernel_cost(plan),
        name="to_spectrum",
    )(me, *blocks, plan.into_even, plan.into_odd, plan.turn, plan.mix)


def from_product(plan, me, left, right, conjugate, shapes, views, copies):
    count = len(shapes)
    return pl.pallas_call(
        functools.partial(inverse_kernel, plan, views, count, conjugate),
        out_shape=[jax.ShapeDtypeStruct(shape, jnp.float32) for shape in shapes],
        in_specs=[smem()] + [vmem()] * 6,
        out_specs=[anywhere()] * count,
        scratch_shapes=[
            pltpu.VMEM((plan.side, plan.side), jnp.float32),
            pltpu.VMEM((2, plan.rows, plan.side), jnp.float32),
            pltpu.SemaphoreType.DMA((copies,)),
        ],
        compiler_params=pltpu.CompilerParams(vmem_limit_bytes=VMEM_LIMIT),
        cost_estimate=kernel_cost(plan),
        name="from_product",
    )(me, left, right, plan.back_even, plan.back_odd, plan.turn, plan.mix)


def swap(block, step, owners):
    if step == 0:
        return block
    return lax.ppermute(block, ("row", "col"), [(i, i ^ step) for i in range(owners)])


def after(first, then):
    return lax.optimization_barrier((first, then))[1]


def gate_kernel(owners, gates, me, *refs):
    blocks = refs[:owners]
    ins = refs[owners : owners + gates]
    outs = refs[owners + gates : owners + 2 * gates]
    got, sems = refs[owners + 2 * gates :]
    here = pl.program_id(0)

    def copy_of(step):
        return pltpu.make_async_copy(blocks[step], got.at[step], sems.at[step])

    @pl.when(here == 0)
    def start():
        for step in range(owners):
            copy_of(step).start()

    for step in range(owners):

        @pl.when(here == step)
        def wait():
            copy_of(step).wait()

    values = got[here]
    for gate, out in zip(ins, outs):
        out[0] = (gate[0].astype(jnp.float32) * values).astype(jnp.bfloat16)


def gated_by(me, blocks, gates):
    owners = len(blocks)
    shape = gates[0].shape
    spec = pl.BlockSpec((1,) + shape[1:], lambda s, me: (me[0] ^ s, 0, 0))
    size = math.prod(shape)
    return pl.pallas_call(
        functools.partial(gate_kernel, owners, len(gates)),
        grid_spec=pltpu.PrefetchScalarGridSpec(
            num_scalar_prefetch=1,
            grid=(owners,),
            in_specs=[anywhere()] * owners + [spec] * len(gates),
            out_specs=[spec] * len(gates),
            scratch_shapes=[
                pltpu.VMEM(shape, jnp.float32),
                pltpu.SemaphoreType.DMA((owners,)),
            ],
        ),
        out_shape=[jax.ShapeDtypeStruct(shape, jnp.bfloat16)] * len(gates),
        compiler_params=pltpu.CompilerParams(vmem_limit_bytes=VMEM_LIMIT),
        cost_estimate=pl.CostEstimate(
            flops=size * len(gates), bytes_accessed=4 * size * (1 + len(gates)), transcendentals=0
        ),
        name="gate_out",
    )(me, *blocks, *gates)


def channel_shards(outer_gate, inner_gate, signal, grad_out, filter_weight):
    side = filter_weight.shape[1]
    block = filter_weight.shape[0]
    plan = Plan(side)
    parts = lax.axis_size("dp")
    rows, cols = lax.axis_size("row"), lax.axis_size("col")
    owners = rows * cols
    place = own_block()
    me = jnp.reshape(place, (1,)).astype(jnp.int32)
    order = sorted(range(owners), key=lambda s: (-(s // cols), s % cols))

    def gated_block(left, right, step):
        at = place ^ step
        return lax.dynamic_index_in_dim(left[0], at, 0, False).astype(
            jnp.float32
        ) * lax.dynamic_index_in_dim(right[0], at, 0, False).astype(jnp.float32)

    width = side // parts
    own_part = lax.dynamic_slice_in_dim(filter_weight, lax.axis_index("dp") * width, width, 1)
    over_row = lax.all_gather(own_part * (1.0 / side), "row")
    over_all = lax.all_gather(over_row, ("dp", "col"))
    by_block = functools.partial(block_views, plan, owners)
    by_tile = functools.partial(tile_views, plan, (parts, rows, cols))
    block_shapes = [(block, side)] * owners
    tile_shapes = [(parts * cols, rows, block, width)]

    def exchange(values_of, earlier=None):
        got = [None] * owners
        for step in order:
            mine = values_of(step)
            if earlier is not None:
                mine = after(earlier[step], mine)
            got[step] = swap(mine, step, owners)
        return got

    gated = exchange(lambda step: gated_block(inner_gate, signal, step))
    filt = to_spectrum(plan, me, [over_all], by_tile, parts * owners)
    grad_conv = exchange(lambda step: gated_block(grad_out, outer_gate, step), gated)
    gated_spec = to_spectrum(plan, me, after(filt, gated), by_block, owners)
    conv_out = from_product(plan, me, filt, gated_spec, False, block_shapes, by_block, owners)
    conv = exchange(lambda step: conv_out[step], grad_conv)
    cot_spec = to_spectrum(plan, me, after(conv_out[0], grad_conv), by_block, owners)
    back_out = from_product(plan, me, filt, cot_spec, True, block_shapes, by_block, owners)
    grad_gated = exchange(lambda step: back_out[step], conv)
    first = [conv[step] for step in order[:3]] + [back_out[0]]
    (term,) = from_product(
        plan, me, gated_spec, after(first, cot_spec), True, tile_shapes, by_tile, parts * owners
    )
    term = lax.psum_scatter(term, ("dp", "col"), scatter_dimension=0, tiled=False)
    term = lax.psum_scatter(term, "row", scatter_dimension=0, tiled=False)
    grad_filter = lax.all_gather(term * (1.0 / side), "dp", axis=1, tiled=True)

    (grad_outer,) = gated_by(me, conv, [grad_out[0]])
    grad_inner, grad_signal = gated_by(me, grad_gated, [signal[0], inner_gate[0]])
    return (grad_outer[None], grad_inner[None], grad_signal[None], grad_filter)


def shards(*arrays):
    owners = lax.axis_size("row") * lax.axis_size("col")
    side = arrays[0].shape[3]
    whole = arrays[0].shape[1] == owners and owners & (owners - 1) == 0
    fits = whole and side % (4 * LANE_PAD) == 0 and side % lax.axis_size("dp") == 0
    return (channel_shards if fits else spread_shards)(*arrays)


def solution(mesh):
    placed = (
        P("dp", None, ("row", "col"), None),
        P("dp", None, ("row", "col"), None),
        P("dp", None, ("row", "col"), None),
        P("dp", None, ("row", "col"), None),
        P(("row", "col"), None),
    )
    return jax.shard_map(
        shards,
        mesh=mesh,
        in_specs=placed,
        out_specs=(
            P("dp", None, ("row", "col"), None),
            P("dp", None, ("row", "col"), None),
            P("dp", None, ("row", "col"), None),
            P(("row", "col"), None),
        ),
        check_vma=False,
    )
```

```python
import functools
import math

import jax
import jax.numpy as jnp
import numpy as np
from jax import lax
from jax.experimental import pallas as pl
from jax.experimental.pallas import tpu as pltpu
from jax.sharding import PartitionSpec as P

TWO_PI = 2.0 * math.pi


def contract(form, left, right):
    return jnp.einsum(
        form, left, right, precision=lax.Precision.HIGHEST, preferred_element_type=jnp.float32
    )


def redistribute(blocks):
    return lax.all_to_all(blocks, ("row", "col"), split_axis=0, concat_axis=0, tiled=True)


def own_block():
    return lax.axis_index("row") * lax.axis_size("col") + lax.axis_index("col")


def turn_angles(first_index, second_index, total):
    product = first_index * second_index % total
    angles = product.astype(jnp.float32) * (TWO_PI / total)
    return (jnp.cos(angles), jnp.sin(angles))


def axis_dft(real, imag, sign):
    length, width = real.shape
    first = 1 << (length.bit_length() - 1) // 2
    second = length // first
    index_a = jnp.arange(first, dtype=jnp.int32)
    index_b = jnp.arange(second, dtype=jnp.int32)
    cos_a, sin_a = turn_angles(index_a[:, None], index_a[None, :], first)
    sin_a = sign * sin_a
    cos_b, sin_b = turn_angles(index_b[:, None], index_b[None, :], second)
    sin_b = sign * sin_b
    twist_cos, twist_sin = turn_angles(index_a[:, None], index_b[None, :], length)
    twist_cos = twist_cos[:, :, None]
    twist_sin = sign * twist_sin[:, :, None]
    real_three = real.reshape(first, second, width)
    step_real = contract("abm,ak->kbm", real_three, cos_a)
    step_imag = contract("abm,ak->kbm", real_three, sin_a)
    if imag is not None:
        imag_three = imag.reshape(first, second, width)
        step_real = step_real - contract("abm,ak->kbm", imag_three, sin_a)
        step_imag = step_imag + contract("abm,ak->kbm", imag_three, cos_a)
    turned_real = step_real * twist_cos - step_imag * twist_sin
    turned_imag = step_real * twist_sin + step_imag * twist_cos
    out_real = contract("kbm,bj->jkm", turned_real, cos_b) - contract(
        "kbm,bj->jkm", turned_imag, sin_b
    )
    out_imag = contract("kbm,bj->jkm", turned_real, sin_b) + contract(
        "kbm,bj->jkm", turned_imag, cos_b
    )
    return (out_real.reshape(length, width), out_imag.reshape(length, width))


def forward(stacked, order):
    count, block, grid_side = stacked.shape
    owners = grid_side // block
    total = grid_side * grid_side
    send = jnp.transpose(stacked.reshape(count, block, owners, block), (2, 1, 0, 3)).reshape(
        owners, block, count * block
    )
    columns = redistribute(send).reshape(grid_side, count * block)
    first_real, first_imag = axis_dft(columns, None, -1.0)
    first_real = first_real.reshape(grid_side, count, block)
    first_imag = first_imag.reshape(grid_side, count, block)
    col_index = own_block() * block + jnp.arange(block, dtype=jnp.int32)
    cos_turn, sin_turn = turn_angles(order[:, None, None], col_index[None, None, :], total)
    turned_real = first_real * cos_turn + first_imag * sin_turn
    turned_imag = first_imag * cos_turn - first_real * sin_turn
    send_two = jnp.concatenate([turned_real, turned_imag], axis=1).reshape(
        owners, block, 2 * count * block
    )
    gotten = redistribute(send_two).reshape(owners, block, 2 * count, block)
    flat_real = jnp.transpose(gotten[:, :, :count, :], (0, 3, 1, 2)).reshape(
        grid_side, block * count
    )
    flat_imag = jnp.transpose(gotten[:, :, count:, :], (0, 3, 1, 2)).reshape(
        grid_side, block * count
    )
    out_real, out_imag = axis_dft(flat_real, flat_imag, -1.0)
    spec_real = jnp.transpose(out_real.reshape(grid_side, block, count), (1, 2, 0))
    spec_imag = jnp.transpose(out_imag.reshape(grid_side, block, count), (1, 2, 0))
    return (spec_real, spec_imag)


def inverse(spec_real, spec_imag, order):
    block, count, grid_side = spec_real.shape
    owners = grid_side // block
    total = grid_side * grid_side
    flat_real = jnp.transpose(spec_real, (2, 0, 1)).reshape(grid_side, block * count)
    flat_imag = jnp.transpose(spec_imag, (2, 0, 1)).reshape(grid_side, block * count)
    out_real, out_imag = axis_dft(flat_real, flat_imag, 1.0)
    back_real = jnp.transpose(out_real.reshape(owners, block, block, count), (0, 2, 3, 1))
    back_imag = jnp.transpose(out_imag.reshape(owners, block, block, count), (0, 2, 3, 1))
    freq_index = lax.dynamic_slice_in_dim(order, own_block() * block, block, 0)
    col_index = (
        jnp.arange(owners, dtype=jnp.int32)[:, None] * block
        + jnp.arange(block, dtype=jnp.int32)[None, :]
    )
    cos_turn, sin_turn = turn_angles(
        freq_index[None, :, None, None], col_index[:, None, None, :], total
    )
    turned_real = back_real * cos_turn - back_imag * sin_turn
    turned_imag = back_real * sin_turn + back_imag * cos_turn
    send = jnp.concatenate([turned_real, turned_imag], axis=2).reshape(
        owners, block, 2 * count * block
    )
    gotten = redistribute(send).reshape(grid_side, 2 * count * block)
    real_part = gotten[:, : count * block]
    imag_part = gotten[:, count * block :]
    full_real, full_imag = axis_dft(real_part, imag_part, 1.0)
    values = full_real * (1.0 / total)
    returned = redistribute(values.reshape(owners, block, count * block)).reshape(
        owners, block, count, block
    )
    return jnp.transpose(returned, (2, 1, 0, 3)).reshape(count, block, grid_side)


def spread_shards(outer_gate, inner_gate, signal, grad_out, filter_weight):
    grid_side = filter_weight.shape[1]
    freq_index = jnp.arange(grid_side, dtype=jnp.int32)
    outer_f = outer_gate[0].astype(jnp.float32)
    inner_f = inner_gate[0].astype(jnp.float32)
    signal_f = signal[0].astype(jnp.float32)
    grad_f = grad_out[0].astype(jnp.float32)
    channels = inner_f.shape[0]
    gated = inner_f * signal_f
    grad_conv = grad_f * outer_f
    taps = (filter_weight * (1.0 / grid_side))[None]
    spec_real, spec_imag = forward(jnp.concatenate([gated, grad_conv], axis=0), freq_index)
    filt_real, filt_imag = forward(taps, freq_index)
    gated_real = spec_real[:, :channels]
    gated_imag = spec_imag[:, :channels]
    cot_real = spec_real[:, channels : 2 * channels]
    cot_imag = spec_imag[:, channels : 2 * channels]
    conv_real = filt_real * gated_real - filt_imag * gated_imag
    conv_imag = filt_real * gated_imag + filt_imag * gated_real
    back_real = filt_real * cot_real + filt_imag * cot_imag
    back_imag = filt_real * cot_imag - filt_imag * cot_real
    term_real = jnp.sum(gated_real * cot_real + gated_imag * cot_imag, axis=1, keepdims=True)
    term_imag = jnp.sum(gated_real * cot_imag - gated_imag * cot_real, axis=1, keepdims=True)
    values = inverse(
        jnp.concatenate([conv_real, back_real, term_real], axis=1),
        jnp.concatenate([conv_imag, back_imag, term_imag], axis=1),
        freq_index,
    )
    grad_filter = lax.psum(values[2 * channels], "dp") * (1.0 / grid_side)
    conv = values[:channels]
    grad_gated = values[channels : 2 * channels]
    grad_outer = (grad_f * conv).astype(jnp.bfloat16)[None]
    grad_inner = (grad_gated * signal_f).astype(jnp.bfloat16)[None]
    grad_signal = (grad_gated * inner_f).astype(jnp.bfloat16)[None]
    return (grad_outer, grad_inner, grad_signal, grad_filter)


VMEM_LIMIT = 18 * 1024 * 1024
UNDER_WAY = 4
ROW_PAD = 16
LANE_PAD = 128


def up_to(value, unit):
    return -(-value // unit) * unit


def high_low(table):
    high = table.astype(jnp.bfloat16)
    low = (table - high.astype(np.float64)).astype(jnp.bfloat16)
    return np.stack([high, low])


class Plan:
    def __init__(self, side):
        half = side // 2
        self.side, self.half, self.quarter = side, half, side // 4
        self.evens = up_to(half // 2 + 1, ROW_PAD)
        self.odds = half // 2
        self.rows = self.evens + self.odds
        self.even_depth = up_to(2 * self.evens, LANE_PAD)
        total = side * side
        even_k = 2 * np.arange(self.evens)
        odd_k = 2 * np.arange(self.odds) + 1
        live = (even_k <= half).astype(np.float64)
        p = np.arange(half)

        def waves(k, scale):
            angle = 2.0 * np.pi * (k[:, None] * p[None, :] % side) / side
            return np.concatenate([np.cos(angle) * scale[:, None], -np.sin(angle) * scale[:, None]])

        ones = np.ones(self.odds)
        self.into_even = high_low(waves(even_k, live))
        self.into_odd = high_low(waves(odd_k, ones))
        weight = np.where((even_k == 0) | (even_k == half), 1.0, 2.0) * live / total
        back_even = np.zeros((half, self.even_depth))
        back_even[:, : 2 * self.evens] = waves(even_k, weight).T
        self.back_even = high_low(back_even)
        self.back_odd = high_low(waves(odd_k, ones * 2.0 / total).T)
        k = np.concatenate([even_k, odd_k])
        turn = 2.0 * np.pi * (k[:, None] * np.arange(side)[None, :] % total) / total
        self.turn = np.stack([np.cos(turn), np.sin(turn)]).astype(np.float32)
        q = np.arange(self.quarter)
        mixes = []
        for r in range(4):
            angle = 2.0 * np.pi * (q[:, None] * (4 * q[None, :] + r) % side) / side
            cos, sin = np.cos(angle), np.sin(angle)
            mixes.append(np.block([[cos, -sin], [sin, cos]]))
        self.mix = high_low(np.stack(mixes))
        self.row_tile = next(t for t in (176, 264, 16, 8) if self.rows % t == 0)


def split_terms(values):
    high = values.astype(jnp.bfloat16)
    return high, (values - high.astype(jnp.float32)).astype(jnp.bfloat16)


def dot_in(table, rows, high, low):
    dot = functools.partial(jnp.dot, preferred_element_type=jnp.float32)
    first, second = table[0, rows], table[1, rows]
    return dot(first, high) + (dot(first, low) + dot(second, high))


def block_views(plan, owners, me, blocks, values):
    size = plan.side // owners
    for step in range(owners):
        at = pl.multiple_of((me[0] ^ step) * size, size)
        yield blocks[step], values.at[pl.ds(at, size)]


def tile_views(plan, parts, owners, me, tiles, values):
    height, width = plan.side // owners, plan.side // parts
    for part in range(parts):
        for owner in range(owners):
            place = values.at[pl.ds(owner * height, height), pl.ds(part * width, width)]
            yield tiles[0].at[part * owners + owner], place


def start_all(pairs, sems):
    copies = [pltpu.make_async_copy(source, to, sems.at[i]) for i, (source, to) in enumerate(pairs)]
    for copy in copies:
        copy.start()
    return copies


def wait_all(copies):
    for copy in copies:
        copy.wait()


def to_spectrum(plan, values, into_even, into_odd, turn, mix, spec, mid):
    side, half, quarter = plan.side, plan.half, plan.quarter

    @pl.loop(0, side // quarter)
    def columns(tile):
        cols = pl.ds(pl.multiple_of(tile * quarter, quarter), quarter)
        top, bottom = values[pl.ds(0, half), cols], values[pl.ds(half, half), cols]
        for first, count, table, part in (
            (0, plan.evens, into_even, top + bottom),
            (plan.evens, plan.odds, into_odd, top - bottom),
        ):
            out = dot_in(table, slice(None), *split_terms(part))
            real, imag = out[:count], out[count:]
            rows = pl.ds(first, count)
            cos, sin = turn[0, rows, cols], turn[1, rows, cols]
            mid[0, rows, cols] = real * cos + imag * sin
            mid[1, rows, cols] = imag * cos - real * sin

    @pl.loop(0, plan.rows // plan.row_tile)
    def rows_loop(tile):
        rows = pl.ds(pl.multiple_of(tile * plan.row_tile, plan.row_tile), plan.row_tile)
        real = [mid[0, rows, pl.ds(j * quarter, quarter)] for j in range(4)]
        imag = [mid[1, rows, pl.ds(j * quarter, quarter)] for j in range(4)]
        sum_r, sum_i = real[0] + real[2], imag[0] + imag[2]
        dif_r, dif_i = real[0] - real[2], imag[0] - imag[2]
        two_r, two_i = real[1] + real[3], imag[1] + imag[3]
        odd_r, odd_i = real[1] - real[3], imag[1] - imag[3]
        turns = (
            (sum_r + two_r, sum_i + two_i),
            (dif_r + odd_i, dif_i - odd_r),
            (sum_r - two_r, sum_i - two_i),
            (dif_r - odd_i, dif_i + odd_r),
        )
        dot = functools.partial(jnp.dot, preferred_element_type=jnp.float32)
        for r, pair in enumerate(turns):
            high, low = split_terms(jnp.concatenate(pair, axis=1))
            out = dot(high, mix[0, r]) + (dot(low, mix[0, r]) + dot(high, mix[1, r]))
            cols = pl.ds(r * quarter, quarter)
            spec[0, rows, cols] = out[:, :quarter]
            spec[1, rows, cols] = out[:, quarter:]


def inverse_rows(plan, conjugate, left, right, turn, mix, mid):
    quarter = plan.quarter

    @pl.loop(0, plan.rows // plan.row_tile)
    def rows_loop(tile):
        rows = pl.ds(pl.multiple_of(tile * plan.row_tile, plan.row_tile), plan.row_tile)
        real, imag = [], []
        for r in range(4):
            cols = pl.ds(r * quarter, quarter)
            left_r, left_i = left[0, rows, cols], left[1, rows, cols]
            right_r, right_i = right[0, rows, cols], right[1, rows, cols]
            if conjugate:
                left_i = -left_i
            pair = (left_r * right_r - left_i * right_i, left_r * right_i + left_i * right_r)
            high, low = split_terms(jnp.concatenate(pair, axis=1))

            def dot(part, table):
                return lax.dot_general(
                    part, table, (((1,), (1,)), ((), ())), preferred_element_type=jnp.float32
                )

            out = dot(high, mix[0, r]) + (dot(low, mix[0, r]) + dot(high, mix[1, r]))
            real.append(out[:, :quarter])
            imag.append(out[:, quarter:])
        sum_r, sum_i = real[0] + real[2], imag[0] + imag[2]
        dif_r, dif_i = real[0] - real[2], imag[0] - imag[2]
        two_r, two_i = real[1] + real[3], imag[1] + imag[3]
        odd_r, odd_i = real[1] - real[3], imag[1] - imag[3]
        turns = (
            (sum_r + two_r, sum_i + two_i),
            (dif_r - odd_i, dif_i + odd_r),
            (sum_r - two_r, sum_i - two_i),
            (dif_r + odd_i, dif_i - odd_r),
        )
        for j, (got_r, got_i) in enumerate(turns):
            cols = pl.ds(j * quarter, quarter)
            cos, sin = turn[0, rows, cols], turn[1, rows, cols]
            mid[0, rows, cols] = got_r * cos - got_i * sin
            mid[1, rows, cols] = got_r * sin + got_i * cos


def inverse_columns(plan, back_even, back_odd, mid, values):
    side, half, quarter = plan.side, plan.half, plan.quarter

    @pl.loop(0, side // quarter)
    def columns(tile):
        cols = pl.ds(pl.multiple_of(tile * quarter, quarter), quarter)
        even = [mid[0, pl.ds(0, plan.evens), cols], mid[1, pl.ds(0, plan.evens), cols]]
        if plan.even_depth > 2 * plan.evens:
            even.append(jnp.zeros((plan.even_depth - 2 * plan.evens, quarter), jnp.float32))
        odd = [mid[0, pl.ds(plan.evens, plan.odds), cols], mid[1, pl.ds(plan.evens, plan.odds), cols]]
        from_even = dot_in(back_even, slice(None), *split_terms(jnp.concatenate(even)))
        from_odd = dot_in(back_odd, slice(None), *split_terms(jnp.concatenate(odd)))
        values[pl.ds(0, half), cols] = from_even + from_odd
        values[pl.ds(half, half), cols] = from_even - from_odd


def filter_kernel(plan, views, me, tiles, into_even, into_odd, turn, mix, spec, values, mid, sems):
    wait_all(start_all(views(me, [tiles], values), sems))
    to_spectrum(plan, values, into_even, into_odd, turn, mix, spec, mid)


def conv_kernel(plan, views, count, me, filt, *refs):
    blocks, tables = refs[:count], refs[count : count + 6]
    into_even, into_odd, back_even, back_odd, turn, mix = tables
    spec, outs = refs[count + 6], refs[count + 7 : 2 * count + 7]
    values, mid, sems = refs[2 * count + 7 :]
    wait_all(start_all(views(me, blocks, values), sems))
    to_spectrum(plan, values, into_even, into_odd, turn, mix, spec, mid)
    inverse_rows(plan, False, filt, spec, turn, mix, mid)
    inverse_columns(plan, back_even, back_odd, mid, values)
    wait_all(start_all(((to, source) for source, to in views(me, outs, values)), sems))


def grads_kernel(plan, views, term_views, count, me, filt, gated, *refs):
    blocks, tables = refs[:count], refs[count : count + 6]
    into_even, into_odd, back_even, back_odd, turn, mix = tables
    outs, term = refs[count + 6 : 2 * count + 6], refs[2 * count + 6]
    values, mid, spec, sems, term_sems = refs[2 * count + 7 :]
    wait_all(start_all(views(me, blocks, values), sems))
    to_spectrum(plan, values, into_even, into_odd, turn, mix, spec, mid)
    inverse_rows(plan, True, filt, spec, turn, mix, mid)
    inverse_columns(plan, back_even, back_odd, mid, values)
    copies = start_all(((to, source) for source, to in views(me, outs, values)), sems)
    inverse_rows(plan, True, gated, spec, turn, mix, mid)
    wait_all(copies)
    inverse_columns(plan, back_even, back_odd, mid, values)
    wait_all(start_all(((to, source) for source, to in term_views(me, [term], values)), term_sems))


def smem():
    return pl.BlockSpec(memory_space=pltpu.SMEM)


def vmem():
    return pl.BlockSpec(memory_space=pltpu.VMEM)


def anywhere():
    return pl.BlockSpec(memory_space=pl.ANY)


def kernel_cost(plan):
    return pl.CostEstimate(flops=plan.side**2, bytes_accessed=plan.side**2, transcendentals=0)


def call_kernel(plan, kernel, name, args, in_specs, out_shape, out_specs, scratch):
    return pl.pallas_call(
        kernel,
        out_shape=out_shape,
        in_specs=in_specs,
        out_specs=out_specs,
        scratch_shapes=scratch,
        compiler_params=pltpu.CompilerParams(vmem_limit_bytes=VMEM_LIMIT),
        cost_estimate=kernel_cost(plan),
        name=name,
    )(*args)


def float_array(shape):
    return jax.ShapeDtypeStruct(shape, jnp.float32)


def filter_spectrum(plan, me, tiles, views, copies):
    shape = (2, plan.rows, plan.side)
    return call_kernel(
        plan,
        functools.partial(filter_kernel, plan, views),
        "filter_spectrum",
        (me, tiles, plan.into_even, plan.into_odd, plan.turn, plan.mix),
        [smem(), anywhere()] + [vmem()] * 4,
        float_array(shape),
        vmem(),
        [
            pltpu.VMEM((plan.side, plan.side), jnp.float32),
            pltpu.VMEM(shape, jnp.float32),
            pltpu.SemaphoreType.DMA((copies,)),
        ],
    )


def tables_of(plan):
    return (plan.into_even, plan.into_odd, plan.back_even, plan.back_odd, plan.turn, plan.mix)


def conv_of(plan, me, filt, blocks, views):
    count = len(blocks)
    shape = (2, plan.rows, plan.side)
    spec, *outs = call_kernel(
        plan,
        functools.partial(conv_kernel, plan, views, count),
        "conv_of",
        (me, filt, *blocks, *tables_of(plan)),
        [smem(), vmem()] + [vmem()] * count + [vmem()] * 6,
        [float_array(shape)] + [float_array(blocks[0].shape)] * count,
        [vmem()] * (count + 1),
        [
            pltpu.VMEM((plan.side, plan.side), jnp.float32),
            pltpu.VMEM(shape, jnp.float32),
            pltpu.SemaphoreType.DMA((count,)),
        ],
    )
    return spec, outs


def grads_of(plan, me, filt, gated, blocks, views, term_shape, term_views):
    count = len(blocks)
    shape = (2, plan.rows, plan.side)
    *outs, term = call_kernel(
        plan,
        functools.partial(grads_kernel, plan, views, term_views, count),
        "grads_of",
        (me, filt, gated, *blocks, *tables_of(plan)),
        [smem(), vmem(), vmem()] + [vmem()] * count + [vmem()] * 6,
        [float_array(blocks[0].shape)] * count + [float_array(term_shape)],
        [vmem()] * count + [anywhere()],
        [
            pltpu.VMEM((plan.side, plan.side), jnp.float32),
            pltpu.VMEM(shape, jnp.float32),
            pltpu.VMEM(shape, jnp.float32),
            pltpu.SemaphoreType.DMA((count,)),
            pltpu.SemaphoreType.DMA((term_shape[0],)),
        ],
    )
    return outs, term


def pairwise(block, axis, step):
    return lax.ppermute(block, axis, [(i, i ^ step) for i in range(lax.axis_size(axis))])


def after(first, then):
    return lax.optimization_barrier((first, then))[1]


def gate_kernel(steps, gates, me, *refs):
    count = len(steps)
    blocks = refs[:count]
    ins = refs[count : count + gates]
    outs, got, sems = refs[-gates - 2 : -2], refs[-2], refs[-1]
    here = pl.program_id(0)

    def copy_of(i):
        return pltpu.make_async_copy(blocks[i], got.at[i], sems.at[i])

    @pl.when(here == 0)
    def start():
        for i in range(count):
            copy_of(i).start()

    for i in range(count):

        @pl.when(here == i)
        def wait():
            copy_of(i).wait()

    values = got[here]
    for gate, out in zip(ins, outs):
        out[0] = (gate[0].astype(jnp.float32) * values).astype(jnp.bfloat16)


def gated_by(me, steps, blocks, gates, done=()):
    count = len(steps)
    shape = gates[0].shape

    def place(i, me):
        step = steps[-1]
        for j in range(count - 1):
            step = jnp.where(i == j, steps[j], step)
        return (me[0] ^ step, 0, 0)

    spec = pl.BlockSpec((1,) + shape[1:], place)
    size = count * shape[1] * shape[2]
    first_done = 1 + count + len(gates)
    return pl.pallas_call(
        functools.partial(gate_kernel, steps, len(gates)),
        grid_spec=pltpu.PrefetchScalarGridSpec(
            num_scalar_prefetch=1,
            grid=(count,),
            in_specs=[anywhere()] * count + [spec] * len(gates) + [anywhere()] * len(done),
            out_specs=[spec] * len(gates),
            scratch_shapes=[
                pltpu.VMEM((count,) + shape[1:], jnp.float32),
                pltpu.SemaphoreType.DMA((count,)),
            ],
        ),
        out_shape=[jax.ShapeDtypeStruct(shape, jnp.bfloat16)] * len(gates),
        input_output_aliases={first_done + i: i for i in range(len(done))},
        compiler_params=pltpu.CompilerParams(vmem_limit_bytes=VMEM_LIMIT),
        cost_estimate=pl.CostEstimate(
            flops=size * len(gates), bytes_accessed=4 * size * (1 + len(gates)), transcendentals=0
        ),
        name="gate_out",
    )(me, *blocks, *gates, *done)


def send_order(owners):
    far = sorted(range(owners // 2, owners), key=lambda s: (s & 1, -s))
    return far + sorted(range(1, owners // 2), reverse=True)


def channel_shards(outer_gate, inner_gate, signal, grad_out, filter_weight):
    block, side = filter_weight.shape
    plan = Plan(side)
    parts, rows, cols = (lax.axis_size(name) for name in ("dp", "row", "col"))
    owners = rows * cols
    place = own_block()
    me = jnp.reshape(place, (1,)).astype(jnp.int32)
    order = send_order(owners)
    far = order[: owners // 2]
    last_order = far[:-1] + order[owners // 2 :] + far[-1:]
    width = side // parts
    by_block = functools.partial(block_views, plan, owners)
    by_tile = functools.partial(tile_views, plan, parts, owners)

    def gated_block(left, right, step):
        at = place ^ step
        return lax.dynamic_index_in_dim(left[0], at, 0, False).astype(
            jnp.float32
        ) * lax.dynamic_index_in_dim(right[0], at, 0, False).astype(jnp.float32)

    sent = []

    def exchange(blocks, what, order=order):
        got = [blocks[0]] + [None] * (owners - 1)
        for step in order:
            mine = blocks[step]
            if len(sent) >= UNDER_WAY:
                mine = after(sent[: len(sent) - UNDER_WAY + 1][-owners:], mine)
            with jax.named_scope(f"{what}_{step}"):
                got[step] = pairwise(mine, ("row", "col"), step)
            sent.append(got[step])
        return got

    first = gated_block(inner_gate, signal, order[0])
    inner_later, signal_later = after(first, [inner_gate, signal])
    gated = exchange(
        [
            first if step == order[0] else gated_block(inner_later, signal_later, step)
            for step in range(owners)
        ],
        "gated",
    )

    own_part = lax.dynamic_slice_in_dim(filter_weight, lax.axis_index("dp") * width, width, 1)
    over_all = lax.all_gather(own_part * (1.0 / side), ("dp", "row", "col"))
    filt = filter_spectrum(plan, me, over_all, by_tile, parts * owners)

    grad_conv = [gated_block(grad_out, outer_gate, step) for step in range(owners)]
    grad_conv = exchange(grad_conv, "grad_conv")
    spec, conv_out = conv_of(plan, me, filt, after(filt, gated), by_block)
    conv = exchange(conv_out, "conv")
    tile_shape = (parts * owners, block, width)
    back_out, term = grads_of(plan, me, filt, spec, grad_conv, by_block, tile_shape, by_tile)
    grad_gated = exchange(back_out, "grad_gated", last_order)

    term = after([conv[step] for step in order[:3]], term)
    term = lax.psum_scatter(term, ("dp", "row", "col"), scatter_dimension=0, tiled=False)
    total = term * (1.0 / side)
    bit = 1
    while bit < parts:
        other = pairwise(total, "dp", bit)
        upper = (lax.axis_index("dp") & bit) != 0
        total = jnp.concatenate([jnp.where(upper, other, total), jnp.where(upper, total, other)], 1)
        bit *= 2
    grad_filter = total

    every = [0] + last_order
    (grad_outer,) = gated_by(me, every, [conv[step] for step in every], [grad_out[0]])
    gates = [signal[0], inner_gate[0]]
    early, late = every[:-1], every[-1:]
    done = gated_by(me, early, [grad_gated[step] for step in early], gates)
    grad_inner, grad_signal = gated_by(me, late, [grad_gated[step] for step in late], gates, done)
    return (grad_outer[None], grad_inner[None], grad_signal[None], grad_filter)


def powers_of_two(*sizes):
    return all(size & (size - 1) == 0 for size in sizes)


def shards(*arrays):
    parts, rows, cols = (lax.axis_size(name) for name in ("dp", "row", "col"))
    side = arrays[0].shape[3]
    whole = arrays[0].shape[1] == rows * cols and rows * cols >= 4
    fits = powers_of_two(parts, rows, cols, side) and side // 4 % LANE_PAD == 0
    fits = fits and side // parts % LANE_PAD == 0
    return (channel_shards if whole and fits else spread_shards)(*arrays)


def solution(mesh):
    placed = (
        P("dp", None, ("row", "col"), None),
        P("dp", None, ("row", "col"), None),
        P("dp", None, ("row", "col"), None),
        P("dp", None, ("row", "col"), None),
        P(("row", "col"), None),
    )
    return jax.shard_map(
        shards,
        mesh=mesh,
        in_specs=placed,
        out_specs=(
            P("dp", None, ("row", "col"), None),
            P("dp", None, ("row", "col"), None),
            P("dp", None, ("row", "col"), None),
            P(("row", "col"), None),
        ),
        check_vma=False,
    )
```

```python
import functools
import math

import jax
import jax.numpy as jnp
import numpy as np
from jax import lax
from jax.experimental import pallas as pl
from jax.experimental.pallas import tpu as pltpu
from jax.sharding import PartitionSpec as P

TWO_PI = 2.0 * math.pi


def contract(form, left, right):
    return jnp.einsum(
        form, left, right, precision=lax.Precision.HIGHEST, preferred_element_type=jnp.float32
    )


def redistribute(blocks):
    return lax.all_to_all(blocks, ("row", "col"), split_axis=0, concat_axis=0, tiled=True)


def own_block():
    return lax.axis_index("row") * lax.axis_size("col") + lax.axis_index("col")


def turn_angles(first_index, second_index, total):
    product = first_index * second_index % total
    angles = product.astype(jnp.float32) * (TWO_PI / total)
    return (jnp.cos(angles), jnp.sin(angles))


def axis_dft(real, imag, sign):
    length, width = real.shape
    first = 1 << (length.bit_length() - 1) // 2
    second = length // first
    index_a = jnp.arange(first, dtype=jnp.int32)
    index_b = jnp.arange(second, dtype=jnp.int32)
    cos_a, sin_a = turn_angles(index_a[:, None], index_a[None, :], first)
    sin_a = sign * sin_a
    cos_b, sin_b = turn_angles(index_b[:, None], index_b[None, :], second)
    sin_b = sign * sin_b
    twist_cos, twist_sin = turn_angles(index_a[:, None], index_b[None, :], length)
    twist_cos = twist_cos[:, :, None]
    twist_sin = sign * twist_sin[:, :, None]
    real_three = real.reshape(first, second, width)
    step_real = contract("abm,ak->kbm", real_three, cos_a)
    step_imag = contract("abm,ak->kbm", real_three, sin_a)
    if imag is not None:
        imag_three = imag.reshape(first, second, width)
        step_real = step_real - contract("abm,ak->kbm", imag_three, sin_a)
        step_imag = step_imag + contract("abm,ak->kbm", imag_three, cos_a)
    turned_real = step_real * twist_cos - step_imag * twist_sin
    turned_imag = step_real * twist_sin + step_imag * twist_cos
    out_real = contract("kbm,bj->jkm", turned_real, cos_b) - contract(
        "kbm,bj->jkm", turned_imag, sin_b
    )
    out_imag = contract("kbm,bj->jkm", turned_real, sin_b) + contract(
        "kbm,bj->jkm", turned_imag, cos_b
    )
    return (out_real.reshape(length, width), out_imag.reshape(length, width))


def forward(stacked, order):
    count, block, grid_side = stacked.shape
    owners = grid_side // block
    total = grid_side * grid_side
    send = jnp.transpose(stacked.reshape(count, block, owners, block), (2, 1, 0, 3)).reshape(
        owners, block, count * block
    )
    columns = redistribute(send).reshape(grid_side, count * block)
    first_real, first_imag = axis_dft(columns, None, -1.0)
    first_real = first_real.reshape(grid_side, count, block)
    first_imag = first_imag.reshape(grid_side, count, block)
    col_index = own_block() * block + jnp.arange(block, dtype=jnp.int32)
    cos_turn, sin_turn = turn_angles(order[:, None, None], col_index[None, None, :], total)
    turned_real = first_real * cos_turn + first_imag * sin_turn
    turned_imag = first_imag * cos_turn - first_real * sin_turn
    send_two = jnp.concatenate([turned_real, turned_imag], axis=1).reshape(
        owners, block, 2 * count * block
    )
    gotten = redistribute(send_two).reshape(owners, block, 2 * count, block)
    flat_real = jnp.transpose(gotten[:, :, :count, :], (0, 3, 1, 2)).reshape(
        grid_side, block * count
    )
    flat_imag = jnp.transpose(gotten[:, :, count:, :], (0, 3, 1, 2)).reshape(
        grid_side, block * count
    )
    out_real, out_imag = axis_dft(flat_real, flat_imag, -1.0)
    spec_real = jnp.transpose(out_real.reshape(grid_side, block, count), (1, 2, 0))
    spec_imag = jnp.transpose(out_imag.reshape(grid_side, block, count), (1, 2, 0))
    return (spec_real, spec_imag)


def inverse(spec_real, spec_imag, order):
    block, count, grid_side = spec_real.shape
    owners = grid_side // block
    total = grid_side * grid_side
    flat_real = jnp.transpose(spec_real, (2, 0, 1)).reshape(grid_side, block * count)
    flat_imag = jnp.transpose(spec_imag, (2, 0, 1)).reshape(grid_side, block * count)
    out_real, out_imag = axis_dft(flat_real, flat_imag, 1.0)
    back_real = jnp.transpose(out_real.reshape(owners, block, block, count), (0, 2, 3, 1))
    back_imag = jnp.transpose(out_imag.reshape(owners, block, block, count), (0, 2, 3, 1))
    freq_index = lax.dynamic_slice_in_dim(order, own_block() * block, block, 0)
    col_index = (
        jnp.arange(owners, dtype=jnp.int32)[:, None] * block
        + jnp.arange(block, dtype=jnp.int32)[None, :]
    )
    cos_turn, sin_turn = turn_angles(
        freq_index[None, :, None, None], col_index[:, None, None, :], total
    )
    turned_real = back_real * cos_turn - back_imag * sin_turn
    turned_imag = back_real * sin_turn + back_imag * cos_turn
    send = jnp.concatenate([turned_real, turned_imag], axis=2).reshape(
        owners, block, 2 * count * block
    )
    gotten = redistribute(send).reshape(grid_side, 2 * count * block)
    real_part = gotten[:, : count * block]
    imag_part = gotten[:, count * block :]
    full_real, full_imag = axis_dft(real_part, imag_part, 1.0)
    values = full_real * (1.0 / total)
    returned = redistribute(values.reshape(owners, block, count * block)).reshape(
        owners, block, count, block
    )
    return jnp.transpose(returned, (2, 1, 0, 3)).reshape(count, block, grid_side)


def spread_shards(outer_gate, inner_gate, signal, grad_out, filter_weight):
    grid_side = filter_weight.shape[1]
    freq_index = jnp.arange(grid_side, dtype=jnp.int32)
    outer_f = outer_gate[0].astype(jnp.float32)
    inner_f = inner_gate[0].astype(jnp.float32)
    signal_f = signal[0].astype(jnp.float32)
    grad_f = grad_out[0].astype(jnp.float32)
    channels = inner_f.shape[0]
    gated = inner_f * signal_f
    grad_conv = grad_f * outer_f
    taps = (filter_weight * (1.0 / grid_side))[None]
    spec_real, spec_imag = forward(jnp.concatenate([gated, grad_conv], axis=0), freq_index)
    filt_real, filt_imag = forward(taps, freq_index)
    gated_real = spec_real[:, :channels]
    gated_imag = spec_imag[:, :channels]
    cot_real = spec_real[:, channels : 2 * channels]
    cot_imag = spec_imag[:, channels : 2 * channels]
    conv_real = filt_real * gated_real - filt_imag * gated_imag
    conv_imag = filt_real * gated_imag + filt_imag * gated_real
    back_real = filt_real * cot_real + filt_imag * cot_imag
    back_imag = filt_real * cot_imag - filt_imag * cot_real
    term_real = jnp.sum(gated_real * cot_real + gated_imag * cot_imag, axis=1, keepdims=True)
    term_imag = jnp.sum(gated_real * cot_imag - gated_imag * cot_real, axis=1, keepdims=True)
    values = inverse(
        jnp.concatenate([conv_real, back_real, term_real], axis=1),
        jnp.concatenate([conv_imag, back_imag, term_imag], axis=1),
        freq_index,
    )
    grad_filter = lax.psum(values[2 * channels], "dp") * (1.0 / grid_side)
    conv = values[:channels]
    grad_gated = values[channels : 2 * channels]
    grad_outer = (grad_f * conv).astype(jnp.bfloat16)[None]
    grad_inner = (grad_gated * signal_f).astype(jnp.bfloat16)[None]
    grad_signal = (grad_gated * inner_f).astype(jnp.bfloat16)[None]
    return (grad_outer, grad_inner, grad_signal, grad_filter)


VMEM_LIMIT = 18 * 1024 * 1024
UNDER_WAY = 4
ROW_PAD = 16
LANE_PAD = 128


def up_to(value, unit):
    return -(-value // unit) * unit


def high_low(table):
    high = table.astype(jnp.bfloat16)
    low = (table - high.astype(np.float64)).astype(jnp.bfloat16)
    return np.stack([high, low])


class Plan:
    def __init__(self, side):
        half = side // 2
        self.side, self.half, self.quarter = side, half, side // 4
        self.evens = up_to(half // 2 + 1, ROW_PAD)
        self.odds = half // 2
        self.rows = self.evens + self.odds
        self.even_depth = up_to(2 * self.evens, LANE_PAD)
        total = side * side
        even_k = 2 * np.arange(self.evens)
        odd_k = 2 * np.arange(self.odds) + 1
        live = (even_k <= half).astype(np.float64)
        p = np.arange(half)

        def waves(k, scale):
            angle = 2.0 * np.pi * (k[:, None] * p[None, :] % side) / side
            return np.concatenate([np.cos(angle) * scale[:, None], -np.sin(angle) * scale[:, None]])

        ones = np.ones(self.odds)
        self.into_even = high_low(waves(even_k, live))
        self.into_odd = high_low(waves(odd_k, ones))
        weight = np.where((even_k == 0) | (even_k == half), 1.0, 2.0) * live / total
        back_even = np.zeros((half, self.even_depth))
        back_even[:, : 2 * self.evens] = waves(even_k, weight).T
        self.back_even = high_low(back_even)
        self.back_odd = high_low(waves(odd_k, ones * 2.0 / total).T)
        k = np.concatenate([even_k, odd_k])
        turn = 2.0 * np.pi * (k[:, None] * np.arange(side)[None, :] % total) / total
        self.turn = np.stack([np.cos(turn), np.sin(turn)]).astype(np.float32)
        q = np.arange(self.quarter)
        mixes = []
        for r in range(4):
            angle = 2.0 * np.pi * (q[:, None] * (4 * q[None, :] + r) % side) / side
            cos, sin = np.cos(angle), np.sin(angle)
            mixes.append(np.block([[cos, -sin], [sin, cos]]))
        self.mix = high_low(np.stack(mixes))
        self.row_tile = next(t for t in (176, 264, 16, 8) if self.rows % t == 0)


def split_terms(values):
    high = values.astype(jnp.bfloat16)
    return high, (values - high.astype(jnp.float32)).astype(jnp.bfloat16)


def dot_in(table, rows, high, low):
    dot = functools.partial(jnp.dot, preferred_element_type=jnp.float32)
    first, second = table[0, rows], table[1, rows]
    return dot(first, high) + (dot(first, low) + dot(second, high))


def block_views(plan, owners, me, blocks, values):
    size = plan.side // owners
    for step in range(owners):
        at = pl.multiple_of((me[0] ^ step) * size, size)
        yield blocks[step].at[pl.ds(0, size)], values.at[pl.ds(at, size)]


def tile_views(plan, grid, me, tiles, values):
    parts, rows, cols = grid
    block = plan.side // (rows * cols)
    height = block // parts
    own_row = me[0] // cols
    for part in range(parts):
        for col in range(cols):
            for i in range(rows):
                at = ((own_row ^ i) * cols + col) * block + part * height
                yield tiles[0].at[part * cols + col, i], values.at[pl.ds(pl.multiple_of(at, height), height)]


def start_all(pairs, sems):
    copies = [pltpu.make_async_copy(source, to, sems.at[i]) for i, (source, to) in enumerate(pairs)]
    for copy in copies:
        copy.start()
    return copies


def wait_all(copies):
    for copy in copies:
        copy.wait()


def to_spectrum(plan, values, into_even, into_odd, turn, mix, spec, mid):
    side, half, quarter = plan.side, plan.half, plan.quarter

    @pl.loop(0, side // quarter)
    def columns(tile):
        cols = pl.ds(pl.multiple_of(tile * quarter, quarter), quarter)
        top, bottom = values[pl.ds(0, half), cols], values[pl.ds(half, half), cols]
        for first, count, table, part in (
            (0, plan.evens, into_even, top + bottom),
            (plan.evens, plan.odds, into_odd, top - bottom),
        ):
            out = dot_in(table, slice(None), *split_terms(part))
            real, imag = out[:count], out[count:]
            rows = pl.ds(first, count)
            cos, sin = turn[0, rows, cols], turn[1, rows, cols]
            mid[0, rows, cols] = real * cos + imag * sin
            mid[1, rows, cols] = imag * cos - real * sin

    @pl.loop(0, plan.rows // plan.row_tile)
    def rows_loop(tile):
        rows = pl.ds(pl.multiple_of(tile * plan.row_tile, plan.row_tile), plan.row_tile)
        real = [mid[0, rows, pl.ds(j * quarter, quarter)] for j in range(4)]
        imag = [mid[1, rows, pl.ds(j * quarter, quarter)] for j in range(4)]
        sum_r, sum_i = real[0] + real[2], imag[0] + imag[2]
        dif_r, dif_i = real[0] - real[2], imag[0] - imag[2]
        two_r, two_i = real[1] + real[3], imag[1] + imag[3]
        odd_r, odd_i = real[1] - real[3], imag[1] - imag[3]
        turns = (
            (sum_r + two_r, sum_i + two_i),
            (dif_r + odd_i, dif_i - odd_r),
            (sum_r - two_r, sum_i - two_i),
            (dif_r - odd_i, dif_i + odd_r),
        )
        dot = functools.partial(jnp.dot, preferred_element_type=jnp.float32)
        for r, pair in enumerate(turns):
            high, low = split_terms(jnp.concatenate(pair, axis=1))
            out = dot(high, mix[0, r]) + (dot(low, mix[0, r]) + dot(high, mix[1, r]))
            cols = pl.ds(r * quarter, quarter)
            spec[0, rows, cols] = out[:, :quarter]
            spec[1, rows, cols] = out[:, quarter:]


def inverse_rows(plan, conjugate, left, right, turn, mix, mid):
    quarter = plan.quarter

    @pl.loop(0, plan.rows // plan.row_tile)
    def rows_loop(tile):
        rows = pl.ds(pl.multiple_of(tile * plan.row_tile, plan.row_tile), plan.row_tile)
        real, imag = [], []
        for r in range(4):
            cols = pl.ds(r * quarter, quarter)
            left_r, left_i = left[0, rows, cols], left[1, rows, cols]
            right_r, right_i = right[0, rows, cols], right[1, rows, cols]
            if conjugate:
                left_i = -left_i
            pair = (left_r * right_r - left_i * right_i, left_r * right_i + left_i * right_r)
            high, low = split_terms(jnp.concatenate(pair, axis=1))

            def dot(part, table):
                return lax.dot_general(
                    part, table, (((1,), (1,)), ((), ())), preferred_element_type=jnp.float32
                )

            out = dot(high, mix[0, r]) + (dot(low, mix[0, r]) + dot(high, mix[1, r]))
            real.append(out[:, :quarter])
            imag.append(out[:, quarter:])
        sum_r, sum_i = real[0] + real[2], imag[0] + imag[2]
        dif_r, dif_i = real[0] - real[2], imag[0] - imag[2]
        two_r, two_i = real[1] + real[3], imag[1] + imag[3]
        odd_r, odd_i = real[1] - real[3], imag[1] - imag[3]
        turns = (
            (sum_r + two_r, sum_i + two_i),
            (dif_r - odd_i, dif_i + odd_r),
            (sum_r - two_r, sum_i - two_i),
            (dif_r + odd_i, dif_i - odd_r),
        )
        for j, (got_r, got_i) in enumerate(turns):
            cols = pl.ds(j * quarter, quarter)
            cos, sin = turn[0, rows, cols], turn[1, rows, cols]
            mid[0, rows, cols] = got_r * cos - got_i * sin
            mid[1, rows, cols] = got_r * sin + got_i * cos


def inverse_columns(plan, back_even, back_odd, mid, values):
    side, half, quarter = plan.side, plan.half, plan.quarter

    @pl.loop(0, side // quarter)
    def columns(tile):
        cols = pl.ds(pl.multiple_of(tile * quarter, quarter), quarter)
        even = [mid[0, pl.ds(0, plan.evens), cols], mid[1, pl.ds(0, plan.evens), cols]]
        if plan.even_depth > 2 * plan.evens:
            even.append(jnp.zeros((plan.even_depth - 2 * plan.evens, quarter), jnp.float32))
        odd = [mid[0, pl.ds(plan.evens, plan.odds), cols], mid[1, pl.ds(plan.evens, plan.odds), cols]]
        from_even = dot_in(back_even, slice(None), *split_terms(jnp.concatenate(even)))
        from_odd = dot_in(back_odd, slice(None), *split_terms(jnp.concatenate(odd)))
        values[pl.ds(0, half), cols] = from_even + from_odd
        values[pl.ds(half, half), cols] = from_even - from_odd


def filter_kernel(plan, views, me, tiles, into_even, into_odd, turn, mix, spec, values, mid, sems):
    wait_all(start_all(views(me, [tiles], values), sems))
    to_spectrum(plan, values, into_even, into_odd, turn, mix, spec, mid)


def conv_kernel(plan, views, count, me, filt, *refs):
    blocks, tables = refs[:count], refs[count : count + 6]
    into_even, into_odd, back_even, back_odd, turn, mix = tables
    spec, outs = refs[count + 6], refs[count + 7 : 2 * count + 7]
    values, mid, sems = refs[2 * count + 7 :]
    wait_all(start_all(views(me, blocks, values), sems))
    to_spectrum(plan, values, into_even, into_odd, turn, mix, spec, mid)
    inverse_rows(plan, False, filt, spec, turn, mix, mid)
    inverse_columns(plan, back_even, back_odd, mid, values)
    wait_all(start_all(((to, source) for source, to in views(me, outs, values)), sems))


def grads_kernel(plan, views, term_views, count, me, filt, gated, *refs):
    blocks, tables = refs[:count], refs[count : count + 6]
    into_even, into_odd, back_even, back_odd, turn, mix = tables
    outs, term = refs[count + 6 : 2 * count + 6], refs[2 * count + 6]
    values, mid, spec, sems, term_sems = refs[2 * count + 7 :]
    wait_all(start_all(views(me, blocks, values), sems))
    to_spectrum(plan, values, into_even, into_odd, turn, mix, spec, mid)
    inverse_rows(plan, True, filt, spec, turn, mix, mid)
    inverse_columns(plan, back_even, back_odd, mid, values)
    copies = start_all(((to, source) for source, to in views(me, outs, values)), sems)
    inverse_rows(plan, True, gated, spec, turn, mix, mid)
    wait_all(copies)
    inverse_columns(plan, back_even, back_odd, mid, values)
    wait_all(start_all(((to, source) for source, to in term_views(me, [term], values)), term_sems))


def smem():
    return pl.BlockSpec(memory_space=pltpu.SMEM)


def vmem():
    return pl.BlockSpec(memory_space=pltpu.VMEM)


def anywhere():
    return pl.BlockSpec(memory_space=pl.ANY)


def kernel_cost(plan):
    return pl.CostEstimate(flops=plan.side**2, bytes_accessed=plan.side**2, transcendentals=0)


def call_kernel(plan, kernel, name, args, in_specs, out_shape, out_specs, scratch):
    return pl.pallas_call(
        kernel,
        out_shape=out_shape,
        in_specs=in_specs,
        out_specs=out_specs,
        scratch_shapes=scratch,
        compiler_params=pltpu.CompilerParams(vmem_limit_bytes=VMEM_LIMIT),
        cost_estimate=kernel_cost(plan),
        name=name,
    )(*args)


def float_array(shape):
    return jax.ShapeDtypeStruct(shape, jnp.float32)


def filter_spectrum(plan, me, tiles, views, copies):
    shape = (2, plan.rows, plan.side)
    return call_kernel(
        plan,
        functools.partial(filter_kernel, plan, views),
        "filter_spectrum",
        (me, tiles, plan.into_even, plan.into_odd, plan.turn, plan.mix),
        [smem(), anywhere()] + [vmem()] * 4,
        float_array(shape),
        vmem(),
        [
            pltpu.VMEM((plan.side, plan.side), jnp.float32),
            pltpu.VMEM(shape, jnp.float32),
            pltpu.SemaphoreType.DMA((copies,)),
        ],
    )


def tables_of(plan):
    return (plan.into_even, plan.into_odd, plan.back_even, plan.back_odd, plan.turn, plan.mix)


def conv_of(plan, me, filt, blocks, views):
    count = len(blocks)
    shape = (2, plan.rows, plan.side)
    spec, *outs = call_kernel(
        plan,
        functools.partial(conv_kernel, plan, views, count),
        "conv_of",
        (me, filt, *blocks, *tables_of(plan)),
        [smem(), vmem()] + [vmem()] * count + [vmem()] * 6,
        [float_array(shape)] + [float_array((plan.side // count, plan.side))] * count,
        [vmem()] * (count + 1),
        [
            pltpu.VMEM((plan.side, plan.side), jnp.float32),
            pltpu.VMEM(shape, jnp.float32),
            pltpu.SemaphoreType.DMA((count,)),
        ],
    )
    return spec, outs


def grads_of(plan, me, filt, gated, blocks, views, term_shape, term_views):
    count = len(blocks)
    shape = (2, plan.rows, plan.side)
    *outs, term = call_kernel(
        plan,
        functools.partial(grads_kernel, plan, views, term_views, count),
        "grads_of",
        (me, filt, gated, *blocks, *tables_of(plan)),
        [smem(), vmem(), vmem()] + [vmem()] * count + [vmem()] * 6,
        [float_array((plan.side // count, plan.side))] * count + [float_array(term_shape)],
        [vmem()] * count + [anywhere()],
        [
            pltpu.VMEM((plan.side, plan.side), jnp.float32),
            pltpu.VMEM(shape, jnp.float32),
            pltpu.VMEM(shape, jnp.float32),
            pltpu.SemaphoreType.DMA((count,)),
            pltpu.SemaphoreType.DMA((math.prod(term_shape[:2]),)),
        ],
    )
    return outs, term


def pairwise(block, axis, step):
    return lax.ppermute(block, axis, [(i, i ^ step) for i in range(lax.axis_size(axis))])


def after(first, then):
    return lax.optimization_barrier((first, then))[1]


def gate_kernel(steps, gates, me, *refs):
    count = len(steps)
    blocks = refs[:count]
    ins = refs[count : count + gates]
    outs, got, sems = refs[-gates - 2 : -2], refs[-2], refs[-1]
    here = pl.program_id(0)

    def copy_of(i):
        return pltpu.make_async_copy(blocks[i], got.at[i], sems.at[i])

    @pl.when(here == 0)
    def start():
        for i in range(count):
            copy_of(i).start()

    for i in range(count):

        @pl.when(here == i)
        def wait():
            copy_of(i).wait()

    values = got[here]
    for gate, out in zip(ins, outs):
        out[0] = (gate[0].astype(jnp.float32) * values).astype(jnp.bfloat16)


def gated_by(me, steps, blocks, gates, done=()):
    count = len(steps)
    shape = gates[0].shape

    def place(i, me):
        step = steps[-1]
        for j in range(count - 1):
            step = jnp.where(i == j, steps[j], step)
        return (me[0] ^ step, 0, 0)

    spec = pl.BlockSpec((1,) + shape[1:], place)
    size = count * shape[1] * shape[2]
    first_done = 1 + count + len(gates)
    return pl.pallas_call(
        functools.partial(gate_kernel, steps, len(gates)),
        grid_spec=pltpu.PrefetchScalarGridSpec(
            num_scalar_prefetch=1,
            grid=(count,),
            in_specs=[anywhere()] * count + [spec] * len(gates) + [anywhere()] * len(done),
            out_specs=[spec] * len(gates),
            scratch_shapes=[
                pltpu.VMEM((count,) + shape[1:], jnp.float32),
                pltpu.SemaphoreType.DMA((count,)),
            ],
        ),
        out_shape=[jax.ShapeDtypeStruct(shape, jnp.bfloat16)] * len(gates),
        input_output_aliases={first_done + i: i for i in range(len(done))},
        compiler_params=pltpu.CompilerParams(vmem_limit_bytes=VMEM_LIMIT),
        cost_estimate=pl.CostEstimate(
            flops=size * len(gates), bytes_accessed=4 * size * (1 + len(gates)), transcendentals=0
        ),
        name="gate_out",
    )(me, *blocks, *gates, *done)


def send_order(owners):
    far = sorted(range(owners // 2, owners), key=lambda s: (s & 1, -s))
    return far + sorted(range(1, owners // 2), reverse=True)


def channel_shards(outer_gate, inner_gate, signal, grad_out, filter_weight):
    block, side = filter_weight.shape
    plan = Plan(side)
    parts, rows, cols = (lax.axis_size(name) for name in ("dp", "row", "col"))
    owners = rows * cols
    place = own_block()
    me = jnp.reshape(place, (1,)).astype(jnp.int32)
    order = send_order(owners)
    far = order[: owners // 2]
    last_order = far[:-1] + order[owners // 2 :] + far[-1:]
    by_block = functools.partial(block_views, plan, owners)
    by_tile = functools.partial(tile_views, plan, (parts, rows, cols))

    def gated_block(left, right, step):
        at = place ^ step
        return lax.dynamic_index_in_dim(left[0], at, 0, False).astype(
            jnp.float32
        ) * lax.dynamic_index_in_dim(right[0], at, 0, False).astype(jnp.float32)

    sent = []

    def exchange(blocks, what, order=order):
        got = [blocks[0]] + [None] * (owners - 1)
        for step in order:
            mine = blocks[step]
            if len(sent) >= UNDER_WAY:
                mine = after(sent[: len(sent) - UNDER_WAY + 1][-owners:], mine)
            with jax.named_scope(f"{what}_{step}"):
                got[step] = pairwise(mine, ("row", "col"), step)
            sent.append(got[step])
        return got

    height = block // parts
    own_part = lax.dynamic_slice_in_dim(filter_weight, lax.axis_index("dp") * height, height, 0)
    own_part = own_part * (1.0 / side)
    inner, values = inner_gate, signal
    gated = [None] * owners
    for step in order + [0]:
        gated[step] = gated_block(inner, values, step)
        if step and step % cols == 0:
            gated[step] = jnp.concatenate([gated[step], own_part])
        if step == order[0]:
            inner, values = after(gated[step], [inner_gate, signal])
    gated = exchange(gated, "gated")
    over_row = jnp.stack([own_part] + [gated[i * cols][block:] for i in range(1, rows)])
    over_row = after([gated[step] for step in order[:5]], over_row)
    over_all = lax.all_gather(over_row, ("dp", "col"))
    filt = filter_spectrum(plan, me, over_all, by_tile, parts * owners)

    grad_conv = [gated_block(grad_out, outer_gate, step) for step in range(owners)]
    grad_conv = exchange(grad_conv, "grad_conv")
    spec, conv_out = conv_of(plan, me, filt, after(filt, gated), by_block)
    conv = exchange(conv_out, "conv")
    tile_shape = (parts * cols, rows, height, side)
    back_out, term = grads_of(plan, me, filt, spec, grad_conv, by_block, tile_shape, by_tile)
    grad_gated = exchange(back_out, "grad_gated", last_order)

    term = after([conv[step] for step in order[:2]], term)
    term = lax.psum_scatter(term, ("dp", "col"), scatter_dimension=0, tiled=False)
    with jax.named_scope("rows_sum"):
        arrived = [pairwise(term[i], "row", i) for i in range(1, rows)]
    total = sum(arrived, term[0]) * (1.0 / side)
    with jax.named_scope("parts_gather"):
        others = [pairwise(total, "dp", i) for i in range(1, parts)]
    pieces = jnp.stack([total] + others)
    bit = 1
    while bit < parts:
        upper = (lax.axis_index("dp") & bit) != 0
        swapped = jnp.flip(pieces.reshape(parts // (2 * bit), 2, bit, height, side), 1)
        pieces = jnp.where(upper, swapped.reshape(pieces.shape), pieces)
        bit *= 2
    grad_filter = pieces.reshape(block, side)

    every = [0] + last_order
    (grad_outer,) = gated_by(me, every, [conv[step] for step in every], [grad_out[0]])
    gates = [signal[0], inner_gate[0]]
    early, late = every[:-1], every[-1:]
    done = gated_by(me, early, [grad_gated[step] for step in early], gates)
    grad_inner, grad_signal = gated_by(me, late, [grad_gated[step] for step in late], gates, done)
    return (grad_outer[None], grad_inner[None], grad_signal[None], grad_filter)


def powers_of_two(*sizes):
    return all(size & (size - 1) == 0 for size in sizes)


def shards(*arrays):
    parts, rows, cols = (lax.axis_size(name) for name in ("dp", "row", "col"))
    side = arrays[0].shape[3]
    whole = arrays[0].shape[1] == rows * cols and rows * cols >= 4
    fits = powers_of_two(parts, rows, cols, side) and side // 4 % LANE_PAD == 0
    fits = fits and arrays[4].shape[0] // parts % ROW_PAD == 0
    return (channel_shards if whole and fits else spread_shards)(*arrays)


def solution(mesh):
    placed = (
        P("dp", None, ("row", "col"), None),
        P("dp", None, ("row", "col"), None),
        P("dp", None, ("row", "col"), None),
        P("dp", None, ("row", "col"), None),
        P(("row", "col"), None),
    )
    return jax.shard_map(
        shards,
        mesh=mesh,
        in_specs=placed,
        out_specs=(
            P("dp", None, ("row", "col"), None),
            P("dp", None, ("row", "col"), None),
            P("dp", None, ("row", "col"), None),
            P(("row", "col"), None),
        ),
        check_vma=False,
    )
```

```python
import functools
import math

import jax
import jax.numpy as jnp
import numpy as np
from jax import lax
from jax.experimental import pallas as pl
from jax.experimental.pallas import tpu as pltpu
from jax.sharding import PartitionSpec as P

TWO_PI = 2.0 * math.pi


def contract(form, left, right):
    return jnp.einsum(
        form, left, right, precision=lax.Precision.HIGHEST, preferred_element_type=jnp.float32
    )


def redistribute(blocks):
    return lax.all_to_all(blocks, ("row", "col"), split_axis=0, concat_axis=0, tiled=True)


def own_block():
    return lax.axis_index("row") * lax.axis_size("col") + lax.axis_index("col")


def turn_angles(first_index, second_index, total):
    product = first_index * second_index % total
    angles = product.astype(jnp.float32) * (TWO_PI / total)
    return (jnp.cos(angles), jnp.sin(angles))


def axis_dft(real, imag, sign):
    length, width = real.shape
    first = 1 << (length.bit_length() - 1) // 2
    second = length // first
    index_a = jnp.arange(first, dtype=jnp.int32)
    index_b = jnp.arange(second, dtype=jnp.int32)
    cos_a, sin_a = turn_angles(index_a[:, None], index_a[None, :], first)
    sin_a = sign * sin_a
    cos_b, sin_b = turn_angles(index_b[:, None], index_b[None, :], second)
    sin_b = sign * sin_b
    twist_cos, twist_sin = turn_angles(index_a[:, None], index_b[None, :], length)
    twist_cos = twist_cos[:, :, None]
    twist_sin = sign * twist_sin[:, :, None]
    real_three = real.reshape(first, second, width)
    step_real = contract("abm,ak->kbm", real_three, cos_a)
    step_imag = contract("abm,ak->kbm", real_three, sin_a)
    if imag is not None:
        imag_three = imag.reshape(first, second, width)
        step_real = step_real - contract("abm,ak->kbm", imag_three, sin_a)
        step_imag = step_imag + contract("abm,ak->kbm", imag_three, cos_a)
    turned_real = step_real * twist_cos - step_imag * twist_sin
    turned_imag = step_real * twist_sin + step_imag * twist_cos
    out_real = contract("kbm,bj->jkm", turned_real, cos_b) - contract(
        "kbm,bj->jkm", turned_imag, sin_b
    )
    out_imag = contract("kbm,bj->jkm", turned_real, sin_b) + contract(
        "kbm,bj->jkm", turned_imag, cos_b
    )
    return (out_real.reshape(length, width), out_imag.reshape(length, width))


def forward(stacked, order):
    count, block, grid_side = stacked.shape
    owners = grid_side // block
    total = grid_side * grid_side
    send = jnp.transpose(stacked.reshape(count, block, owners, block), (2, 1, 0, 3)).reshape(
        owners, block, count * block
    )
    columns = redistribute(send).reshape(grid_side, count * block)
    first_real, first_imag = axis_dft(columns, None, -1.0)
    first_real = first_real.reshape(grid_side, count, block)
    first_imag = first_imag.reshape(grid_side, count, block)
    col_index = own_block() * block + jnp.arange(block, dtype=jnp.int32)
    cos_turn, sin_turn = turn_angles(order[:, None, None], col_index[None, None, :], total)
    turned_real = first_real * cos_turn + first_imag * sin_turn
    turned_imag = first_imag * cos_turn - first_real * sin_turn
    send_two = jnp.concatenate([turned_real, turned_imag], axis=1).reshape(
        owners, block, 2 * count * block
    )
    gotten = redistribute(send_two).reshape(owners, block, 2 * count, block)
    flat_real = jnp.transpose(gotten[:, :, :count, :], (0, 3, 1, 2)).reshape(
        grid_side, block * count
    )
    flat_imag = jnp.transpose(gotten[:, :, count:, :], (0, 3, 1, 2)).reshape(
        grid_side, block * count
    )
    out_real, out_imag = axis_dft(flat_real, flat_imag, -1.0)
    spec_real = jnp.transpose(out_real.reshape(grid_side, block, count), (1, 2, 0))
    spec_imag = jnp.transpose(out_imag.reshape(grid_side, block, count), (1, 2, 0))
    return (spec_real, spec_imag)


def inverse(spec_real, spec_imag, order):
    block, count, grid_side = spec_real.shape
    owners = grid_side // block
    total = grid_side * grid_side
    flat_real = jnp.transpose(spec_real, (2, 0, 1)).reshape(grid_side, block * count)
    flat_imag = jnp.transpose(spec_imag, (2, 0, 1)).reshape(grid_side, block * count)
    out_real, out_imag = axis_dft(flat_real, flat_imag, 1.0)
    back_real = jnp.transpose(out_real.reshape(owners, block, block, count), (0, 2, 3, 1))
    back_imag = jnp.transpose(out_imag.reshape(owners, block, block, count), (0, 2, 3, 1))
    freq_index = lax.dynamic_slice_in_dim(order, own_block() * block, block, 0)
    col_index = (
        jnp.arange(owners, dtype=jnp.int32)[:, None] * block
        + jnp.arange(block, dtype=jnp.int32)[None, :]
    )
    cos_turn, sin_turn = turn_angles(
        freq_index[None, :, None, None], col_index[:, None, None, :], total
    )
    turned_real = back_real * cos_turn - back_imag * sin_turn
    turned_imag = back_real * sin_turn + back_imag * cos_turn
    send = jnp.concatenate([turned_real, turned_imag], axis=2).reshape(
        owners, block, 2 * count * block
    )
    gotten = redistribute(send).reshape(grid_side, 2 * count * block)
    real_part = gotten[:, : count * block]
    imag_part = gotten[:, count * block :]
    full_real, full_imag = axis_dft(real_part, imag_part, 1.0)
    values = full_real * (1.0 / total)
    returned = redistribute(values.reshape(owners, block, count * block)).reshape(
        owners, block, count, block
    )
    return jnp.transpose(returned, (2, 1, 0, 3)).reshape(count, block, grid_side)


def spread_shards(outer_gate, inner_gate, signal, grad_out, filter_weight):
    grid_side = filter_weight.shape[1]
    freq_index = jnp.arange(grid_side, dtype=jnp.int32)
    outer_f = outer_gate[0].astype(jnp.float32)
    inner_f = inner_gate[0].astype(jnp.float32)
    signal_f = signal[0].astype(jnp.float32)
    grad_f = grad_out[0].astype(jnp.float32)
    channels = inner_f.shape[0]
    gated = inner_f * signal_f
    grad_conv = grad_f * outer_f
    taps = (filter_weight * (1.0 / grid_side))[None]
    spec_real, spec_imag = forward(jnp.concatenate([gated, grad_conv], axis=0), freq_index)
    filt_real, filt_imag = forward(taps, freq_index)
    gated_real = spec_real[:, :channels]
    gated_imag = spec_imag[:, :channels]
    cot_real = spec_real[:, channels : 2 * channels]
    cot_imag = spec_imag[:, channels : 2 * channels]
    conv_real = filt_real * gated_real - filt_imag * gated_imag
    conv_imag = filt_real * gated_imag + filt_imag * gated_real
    back_real = filt_real * cot_real + filt_imag * cot_imag
    back_imag = filt_real * cot_imag - filt_imag * cot_real
    term_real = jnp.sum(gated_real * cot_real + gated_imag * cot_imag, axis=1, keepdims=True)
    term_imag = jnp.sum(gated_real * cot_imag - gated_imag * cot_real, axis=1, keepdims=True)
    values = inverse(
        jnp.concatenate([conv_real, back_real, term_real], axis=1),
        jnp.concatenate([conv_imag, back_imag, term_imag], axis=1),
        freq_index,
    )
    grad_filter = lax.psum(values[2 * channels], "dp") * (1.0 / grid_side)
    conv = values[:channels]
    grad_gated = values[channels : 2 * channels]
    grad_outer = (grad_f * conv).astype(jnp.bfloat16)[None]
    grad_inner = (grad_gated * signal_f).astype(jnp.bfloat16)[None]
    grad_signal = (grad_gated * inner_f).astype(jnp.bfloat16)[None]
    return (grad_outer, grad_inner, grad_signal, grad_filter)


VMEM_LIMIT = 18 * 1024 * 1024
UNDER_WAY = 4
ROW_PAD = 16
LANE_PAD = 128


def up_to(value, unit):
    return -(-value // unit) * unit


def high_low(table):
    high = table.astype(jnp.bfloat16)
    low = (table - high.astype(np.float64)).astype(jnp.bfloat16)
    return np.stack([high, low])


class Plan:
    def __init__(self, side):
        half = side // 2
        self.side, self.half, self.quarter = side, half, side // 4
        self.evens = up_to(half // 2 + 1, ROW_PAD)
        self.odds = half // 2
        self.rows = self.evens + self.odds
        self.even_depth = up_to(2 * self.evens, LANE_PAD)
        total = side * side
        even_k = 2 * np.arange(self.evens)
        odd_k = 2 * np.arange(self.odds) + 1
        live = (even_k <= half).astype(np.float64)
        p = np.arange(half)

        def waves(k, scale):
            angle = 2.0 * np.pi * (k[:, None] * p[None, :] % side) / side
            return np.concatenate([np.cos(angle) * scale[:, None], -np.sin(angle) * scale[:, None]])

        ones = np.ones(self.odds)
        self.into_even = high_low(waves(even_k, live))
        self.into_odd = high_low(waves(odd_k, ones))
        weight = np.where((even_k == 0) | (even_k == half), 1.0, 2.0) * live / total
        back_even = np.zeros((half, self.even_depth))
        back_even[:, : 2 * self.evens] = waves(even_k, weight).T
        self.back_even = high_low(back_even)
        self.back_odd = high_low(waves(odd_k, ones * 2.0 / total).T)
        k = np.concatenate([even_k, odd_k])
        turn = 2.0 * np.pi * (k[:, None] * np.arange(side)[None, :] % total) / total
        self.turn = np.stack([np.cos(turn), np.sin(turn)]).astype(np.float32)
        q = np.arange(self.quarter)
        mixes = []
        for r in range(4):
            angle = 2.0 * np.pi * (q[:, None] * (4 * q[None, :] + r) % side) / side
            cos, sin = np.cos(angle), np.sin(angle)
            mixes.append(np.block([[cos, -sin], [sin, cos]]))
        self.mix = high_low(np.stack(mixes))
        self.row_tile = next(t for t in (176, 264, 16, 8) if self.rows % t == 0)


def split_terms(values):
    high = values.astype(jnp.bfloat16)
    return high, (values - high.astype(jnp.float32)).astype(jnp.bfloat16)


def dot_in(table, rows, high, low):
    dot = functools.partial(jnp.dot, preferred_element_type=jnp.float32)
    first, second = table[0, rows], table[1, rows]
    return dot(first, high) + (dot(first, low) + dot(second, high))


def block_views(plan, owners, me, blocks, values):
    size = plan.side // owners
    for step in range(owners):
        at = pl.multiple_of((me[0] ^ step) * size, size)
        yield blocks[step].at[pl.ds(0, size)], values.at[pl.ds(at, size)]


def tile_views(plan, grid, me, tiles, values):
    parts, rows, cols = grid
    block = plan.side // (rows * cols)
    height = block // parts
    own_row = me[0] // cols
    for part in range(parts):
        for col in range(cols):
            for i in range(rows):
                at = ((own_row ^ i) * cols + col) * block + part * height
                yield tiles[0].at[part * cols + col, i], values.at[pl.ds(pl.multiple_of(at, height), height)]


def start_all(pairs, sems):
    copies = [pltpu.make_async_copy(source, to, sems.at[i]) for i, (source, to) in enumerate(pairs)]
    for copy in copies:
        copy.start()
    return copies


def wait_all(copies):
    for copy in copies:
        copy.wait()


def to_spectrum(plan, values, into_even, into_odd, turn, mix, spec, mid):
    side, half, quarter = plan.side, plan.half, plan.quarter

    @pl.loop(0, side // quarter)
    def columns(tile):
        cols = pl.ds(pl.multiple_of(tile * quarter, quarter), quarter)
        top, bottom = values[pl.ds(0, half), cols], values[pl.ds(half, half), cols]
        for first, count, table, part in (
            (0, plan.evens, into_even, top + bottom),
            (plan.evens, plan.odds, into_odd, top - bottom),
        ):
            out = dot_in(table, slice(None), *split_terms(part))
            real, imag = out[:count], out[count:]
            rows = pl.ds(first, count)
            cos, sin = turn[0, rows, cols], turn[1, rows, cols]
            mid[0, rows, cols] = real * cos + imag * sin
            mid[1, rows, cols] = imag * cos - real * sin

    @pl.loop(0, plan.rows // plan.row_tile)
    def rows_loop(tile):
        rows = pl.ds(pl.multiple_of(tile * plan.row_tile, plan.row_tile), plan.row_tile)
        real = [mid[0, rows, pl.ds(j * quarter, quarter)] for j in range(4)]
        imag = [mid[1, rows, pl.ds(j * quarter, quarter)] for j in range(4)]
        sum_r, sum_i = real[0] + real[2], imag[0] + imag[2]
        dif_r, dif_i = real[0] - real[2], imag[0] - imag[2]
        two_r, two_i = real[1] + real[3], imag[1] + imag[3]
        odd_r, odd_i = real[1] - real[3], imag[1] - imag[3]
        turns = (
            (sum_r + two_r, sum_i + two_i),
            (dif_r + odd_i, dif_i - odd_r),
            (sum_r - two_r, sum_i - two_i),
            (dif_r - odd_i, dif_i + odd_r),
        )
        dot = functools.partial(jnp.dot, preferred_element_type=jnp.float32)
        for r, pair in enumerate(turns):
            high, low = split_terms(jnp.concatenate(pair, axis=1))
            out = dot(high, mix[0, r]) + (dot(low, mix[0, r]) + dot(high, mix[1, r]))
            cols = pl.ds(r * quarter, quarter)
            spec[0, rows, cols] = out[:, :quarter]
            spec[1, rows, cols] = out[:, quarter:]


def inverse_rows(plan, conjugate, left, right, turn, mix, mid):
    quarter = plan.quarter

    @pl.loop(0, plan.rows // plan.row_tile)
    def rows_loop(tile):
        rows = pl.ds(pl.multiple_of(tile * plan.row_tile, plan.row_tile), plan.row_tile)
        real, imag = [], []
        for r in range(4):
            cols = pl.ds(r * quarter, quarter)
            left_r, left_i = left[0, rows, cols], left[1, rows, cols]
            right_r, right_i = right[0, rows, cols], right[1, rows, cols]
            if conjugate:
                left_i = -left_i
            pair = (left_r * right_r - left_i * right_i, left_r * right_i + left_i * right_r)
            high, low = split_terms(jnp.concatenate(pair, axis=1))

            def dot(part, table):
                return lax.dot_general(
                    part, table, (((1,), (1,)), ((), ())), preferred_element_type=jnp.float32
                )

            out = dot(high, mix[0, r]) + (dot(low, mix[0, r]) + dot(high, mix[1, r]))
            real.append(out[:, :quarter])
            imag.append(out[:, quarter:])
        sum_r, sum_i = real[0] + real[2], imag[0] + imag[2]
        dif_r, dif_i = real[0] - real[2], imag[0] - imag[2]
        two_r, two_i = real[1] + real[3], imag[1] + imag[3]
        odd_r, odd_i = real[1] - real[3], imag[1] - imag[3]
        turns = (
            (sum_r + two_r, sum_i + two_i),
            (dif_r - odd_i, dif_i + odd_r),
            (sum_r - two_r, sum_i - two_i),
            (dif_r + odd_i, dif_i - odd_r),
        )
        for j, (got_r, got_i) in enumerate(turns):
            cols = pl.ds(j * quarter, quarter)
            cos, sin = turn[0, rows, cols], turn[1, rows, cols]
            mid[0, rows, cols] = got_r * cos - got_i * sin
            mid[1, rows, cols] = got_r * sin + got_i * cos


def inverse_columns(plan, back_even, back_odd, mid, values):
    side, half, quarter = plan.side, plan.half, plan.quarter

    @pl.loop(0, side // quarter)
    def columns(tile):
        cols = pl.ds(pl.multiple_of(tile * quarter, quarter), quarter)
        even = [mid[0, pl.ds(0, plan.evens), cols], mid[1, pl.ds(0, plan.evens), cols]]
        if plan.even_depth > 2 * plan.evens:
            even.append(jnp.zeros((plan.even_depth - 2 * plan.evens, quarter), jnp.float32))
        odd = [mid[0, pl.ds(plan.evens, plan.odds), cols], mid[1, pl.ds(plan.evens, plan.odds), cols]]
        from_even = dot_in(back_even, slice(None), *split_terms(jnp.concatenate(even)))
        from_odd = dot_in(back_odd, slice(None), *split_terms(jnp.concatenate(odd)))
        values[pl.ds(0, half), cols] = from_even + from_odd
        values[pl.ds(half, half), cols] = from_even - from_odd


def filter_kernel(plan, views, count, me, *refs):
    tiles = refs[:count]
    into_even, into_odd, turn, mix, spec, values, mid, sems = refs[count:]
    wait_all(start_all(views(me, tiles, values), sems))
    to_spectrum(plan, values, into_even, into_odd, turn, mix, spec, mid)


def conv_kernel(plan, views, count, me, filt, *refs):
    blocks, tables = refs[:count], refs[count : count + 6]
    into_even, into_odd, back_even, back_odd, turn, mix = tables
    spec, outs = refs[count + 6], refs[count + 7 : 2 * count + 7]
    values, mid, sems = refs[2 * count + 7 :]
    wait_all(start_all(views(me, blocks, values), sems))
    to_spectrum(plan, values, into_even, into_odd, turn, mix, spec, mid)
    inverse_rows(plan, False, filt, spec, turn, mix, mid)
    inverse_columns(plan, back_even, back_odd, mid, values)
    wait_all(start_all(((to, source) for source, to in views(me, outs, values)), sems))


def grads_kernel(plan, views, term_views, count, me, filt, gated, *refs):
    blocks, tables = refs[:count], refs[count : count + 6]
    into_even, into_odd, back_even, back_odd, turn, mix = tables
    outs, term = refs[count + 6 : 2 * count + 6], refs[2 * count + 6]
    values, mid, spec, sems, term_sems = refs[2 * count + 7 :]
    wait_all(start_all(views(me, blocks, values), sems))
    to_spectrum(plan, values, into_even, into_odd, turn, mix, spec, mid)
    inverse_rows(plan, True, filt, spec, turn, mix, mid)
    inverse_columns(plan, back_even, back_odd, mid, values)
    copies = start_all(((to, source) for source, to in views(me, outs, values)), sems)
    inverse_rows(plan, True, gated, spec, turn, mix, mid)
    wait_all(copies)
    inverse_columns(plan, back_even, back_odd, mid, values)
    wait_all(start_all(((to, source) for source, to in term_views(me, [term], values)), term_sems))


def smem():
    return pl.BlockSpec(memory_space=pltpu.SMEM)


def vmem():
    return pl.BlockSpec(memory_space=pltpu.VMEM)


def anywhere():
    return pl.BlockSpec(memory_space=pl.ANY)


def kernel_cost(plan):
    return pl.CostEstimate(flops=plan.side**2, bytes_accessed=plan.side**2, transcendentals=0)


def call_kernel(plan, kernel, name, args, in_specs, out_shape, out_specs, scratch):
    return pl.pallas_call(
        kernel,
        out_shape=out_shape,
        in_specs=in_specs,
        out_specs=out_specs,
        scratch_shapes=scratch,
        compiler_params=pltpu.CompilerParams(vmem_limit_bytes=VMEM_LIMIT),
        cost_estimate=kernel_cost(plan),
        name=name,
    )(*args)


def float_array(shape):
    return jax.ShapeDtypeStruct(shape, jnp.float32)


def filter_spectrum(plan, me, tiles, views, copies):
    shape = (2, plan.rows, plan.side)
    return call_kernel(
        plan,
        functools.partial(filter_kernel, plan, views, len(tiles)),
        "filter_spectrum",
        (me, *tiles, plan.into_even, plan.into_odd, plan.turn, plan.mix),
        [smem()] + [anywhere()] * len(tiles) + [vmem()] * 4,
        float_array(shape),
        vmem(),
        [
            pltpu.VMEM((plan.side, plan.side), jnp.float32),
            pltpu.VMEM(shape, jnp.float32),
            pltpu.SemaphoreType.DMA((copies,)),
        ],
    )


def tables_of(plan):
    return (plan.into_even, plan.into_odd, plan.back_even, plan.back_odd, plan.turn, plan.mix)


def conv_of(plan, me, filt, blocks, views):
    count = len(blocks)
    shape = (2, plan.rows, plan.side)
    spec, *outs = call_kernel(
        plan,
        functools.partial(conv_kernel, plan, views, count),
        "conv_of",
        (me, filt, *blocks, *tables_of(plan)),
        [smem(), vmem()] + [vmem()] * count + [vmem()] * 6,
        [float_array(shape)] + [float_array((plan.side // count, plan.side))] * count,
        [vmem()] * (count + 1),
        [
            pltpu.VMEM((plan.side, plan.side), jnp.float32),
            pltpu.VMEM(shape, jnp.float32),
            pltpu.SemaphoreType.DMA((count,)),
        ],
    )
    return spec, outs


def grads_of(plan, me, filt, gated, blocks, views, term_shape, term_views):
    count = len(blocks)
    shape = (2, plan.rows, plan.side)
    *outs, term = call_kernel(
        plan,
        functools.partial(grads_kernel, plan, views, term_views, count),
        "grads_of",
        (me, filt, gated, *blocks, *tables_of(plan)),
        [smem(), vmem(), vmem()] + [vmem()] * count + [vmem()] * 6,
        [float_array((plan.side // count, plan.side))] * count + [float_array(term_shape)],
        [vmem()] * count + [anywhere()],
        [
            pltpu.VMEM((plan.side, plan.side), jnp.float32),
            pltpu.VMEM(shape, jnp.float32),
            pltpu.VMEM(shape, jnp.float32),
            pltpu.SemaphoreType.DMA((count,)),
            pltpu.SemaphoreType.DMA((math.prod(term_shape[:2]),)),
        ],
    )
    return outs, term


def pairwise(block, axis, step):
    return lax.ppermute(block, axis, [(i, i ^ step) for i in range(lax.axis_size(axis))])


def after(first, then):
    return lax.optimization_barrier((first, then))[1]


def gate_kernel(steps, gates, me, *refs):
    count = len(steps)
    blocks = refs[:count]
    ins = refs[count : count + gates]
    outs, got, sems = refs[-gates - 2 : -2], refs[-2], refs[-1]
    here = pl.program_id(0)

    def copy_of(i):
        return pltpu.make_async_copy(blocks[i], got.at[i], sems.at[i])

    @pl.when(here == 0)
    def start():
        for i in range(count):
            copy_of(i).start()

    for i in range(count):

        @pl.when(here == i)
        def wait():
            copy_of(i).wait()

    values = got[here]
    for gate, out in zip(ins, outs):
        out[0] = (gate[0].astype(jnp.float32) * values).astype(jnp.bfloat16)


def gated_by(me, steps, blocks, gates, done=()):
    count = len(steps)
    shape = gates[0].shape

    def place(i, me):
        step = steps[-1]
        for j in range(count - 1):
            step = jnp.where(i == j, steps[j], step)
        return (me[0] ^ step, 0, 0)

    spec = pl.BlockSpec((1,) + shape[1:], place)
    size = count * shape[1] * shape[2]
    first_done = 1 + count + len(gates)
    return pl.pallas_call(
        functools.partial(gate_kernel, steps, len(gates)),
        grid_spec=pltpu.PrefetchScalarGridSpec(
            num_scalar_prefetch=1,
            grid=(count,),
            in_specs=[anywhere()] * count + [spec] * len(gates) + [anywhere()] * len(done),
            out_specs=[spec] * len(gates),
            scratch_shapes=[
                pltpu.VMEM((count,) + shape[1:], jnp.float32),
                pltpu.SemaphoreType.DMA((count,)),
            ],
        ),
        out_shape=[jax.ShapeDtypeStruct(shape, jnp.bfloat16)] * len(gates),
        input_output_aliases={first_done + i: i for i in range(len(done))},
        compiler_params=pltpu.CompilerParams(vmem_limit_bytes=VMEM_LIMIT),
        cost_estimate=pl.CostEstimate(
            flops=size * len(gates), bytes_accessed=4 * size * (1 + len(gates)), transcendentals=0
        ),
        name="gate_out",
    )(me, *blocks, *gates, *done)


def send_order(owners):
    far = sorted(range(owners // 2, owners), key=lambda s: (s & 1, -s))
    return far + sorted(range(1, owners // 2), reverse=True)


def channel_shards(outer_gate, inner_gate, signal, grad_out, filter_weight):
    block, side = filter_weight.shape
    plan = Plan(side)
    parts, rows, cols = (lax.axis_size(name) for name in ("dp", "row", "col"))
    owners = rows * cols
    place = own_block()
    me = jnp.reshape(place, (1,)).astype(jnp.int32)
    order = send_order(owners)
    far, near = order[: owners // 2], order[owners // 2 :]
    mixed_order = far[:1] + [step for pair in zip(far[1:], sorted(near, key=lambda s: s % cols)) for step in pair]
    last_order = far[:-1] + near + far[-1:]
    by_block = functools.partial(block_views, plan, owners)
    by_tile = functools.partial(tile_views, plan, (parts, rows, cols))

    def gated_block(left, right, step):
        at = place ^ step
        return lax.dynamic_index_in_dim(left[0], at, 0, False).astype(
            jnp.float32
        ) * lax.dynamic_index_in_dim(right[0], at, 0, False).astype(jnp.float32)

    sent = []

    def exchange(blocks, what, order=order):
        got = [blocks[0]] + [None] * (owners - 1)
        for step in order:
            mine = blocks[step]
            if len(sent) >= UNDER_WAY:
                mine = after(sent[: len(sent) - UNDER_WAY + 1][-owners:], mine)
            with jax.named_scope(f"{what}_{step}"):
                got[step] = pairwise(mine, ("row", "col"), step)
            sent.append(got[step])
        return got

    height = block // parts
    own_part = lax.dynamic_slice_in_dim(filter_weight, lax.axis_index("dp") * height, height, 0)
    own_part = own_part * (1.0 / side)
    inner, values = inner_gate, signal
    gated = [None] * owners
    for step in order + [0]:
        gated[step] = gated_block(inner, values, step)
        if step and step % cols == 0:
            gated[step] = jnp.concatenate([gated[step], own_part])
        if step == order[0]:
            inner, values = after(gated[step], [inner_gate, signal])
    gated = exchange(gated, "gated", mixed_order)
    over_row = jnp.stack([own_part] + [gated[i * cols][block:] for i in range(1, rows)])
    over_row = after([gated[step] for step in far], over_row)
    over_all = [lax.all_gather(over_row, ("dp", "col"))]
    filt = filter_spectrum(plan, me, over_all, by_tile, parts * owners)

    grad_conv = [gated_block(grad_out, outer_gate, step) for step in range(owners)]
    spec, conv_out = conv_of(plan, me, filt, after(filt, gated), by_block)
    for step in near:
        grad_conv[step] = after(conv_out[0], grad_conv[step])
    grad_conv = exchange(grad_conv, "grad_conv")
    conv = exchange(conv_out, "conv")
    tile_shape = (parts * cols, rows, height, side)
    back_out, term = grads_of(plan, me, filt, spec, grad_conv, by_block, tile_shape, by_tile)
    grad_gated = exchange(back_out, "grad_gated", last_order)

    term = after([conv[step] for step in far], term)
    term = lax.psum_scatter(term, ("dp", "col"), scatter_dimension=0, tiled=False)
    with jax.named_scope("rows_sum"):
        arrived = [pairwise(term[i], "row", i) for i in range(1, rows)]
    total = sum(arrived, term[0]) * (1.0 / side)
    with jax.named_scope("parts_gather"):
        others = [pairwise(total, "dp", i) for i in range(1, parts)]
    pieces = jnp.stack([total] + others)
    bit = 1
    while bit < parts:
        upper = (lax.axis_index("dp") & bit) != 0
        swapped = jnp.flip(pieces.reshape(parts // (2 * bit), 2, bit, height, side), 1)
        pieces = jnp.where(upper, swapped.reshape(pieces.shape), pieces)
        bit *= 2
    grad_filter = pieces.reshape(block, side)

    every = [0] + last_order
    (grad_outer,) = gated_by(me, every, [conv[step] for step in every], [grad_out[0]])
    gates = [signal[0], inner_gate[0]]
    early, late = every[:-1], every[-1:]
    done = gated_by(me, early, [grad_gated[step] for step in early], gates)
    grad_inner, grad_signal = gated_by(me, late, [grad_gated[step] for step in late], gates, done)
    return (grad_outer[None], grad_inner[None], grad_signal[None], grad_filter)


def powers_of_two(*sizes):
    return all(size & (size - 1) == 0 for size in sizes)


def shards(*arrays):
    parts, rows, cols = (lax.axis_size(name) for name in ("dp", "row", "col"))
    side = arrays[0].shape[3]
    whole = arrays[0].shape[1] == rows * cols and rows >= 2 and cols == 2
    fits = powers_of_two(parts, rows, cols, side) and side // 4 % LANE_PAD == 0
    fits = fits and arrays[4].shape[0] // parts % ROW_PAD == 0
    return (channel_shards if whole and fits else spread_shards)(*arrays)


def solution(mesh):
    placed = (
        P("dp", None, ("row", "col"), None),
        P("dp", None, ("row", "col"), None),
        P("dp", None, ("row", "col"), None),
        P("dp", None, ("row", "col"), None),
        P(("row", "col"), None),
    )
    return jax.shard_map(
        shards,
        mesh=mesh,
        in_specs=placed,
        out_specs=(
            P("dp", None, ("row", "col"), None),
            P("dp", None, ("row", "col"), None),
            P("dp", None, ("row", "col"), None),
            P(("row", "col"), None),
        ),
        check_vma=False,
    )
```

```python
import functools
import math

import jax
import jax.numpy as jnp
import numpy as np
from jax import lax
from jax.experimental import pallas as pl
from jax.experimental.pallas import tpu as pltpu
from jax.sharding import PartitionSpec as P

TWO_PI = 2.0 * math.pi


def contract(form, left, right):
    return jnp.einsum(
        form, left, right, precision=lax.Precision.HIGHEST, preferred_element_type=jnp.float32
    )


def redistribute(blocks):
    return lax.all_to_all(blocks, ("row", "col"), split_axis=0, concat_axis=0, tiled=True)


def own_block():
    return lax.axis_index("row") * lax.axis_size("col") + lax.axis_index("col")


def turn_angles(first_index, second_index, total):
    product = first_index * second_index % total
    angles = product.astype(jnp.float32) * (TWO_PI / total)
    return (jnp.cos(angles), jnp.sin(angles))


def axis_dft(real, imag, sign):
    length, width = real.shape
    first = 1 << (length.bit_length() - 1) // 2
    second = length // first
    index_a = jnp.arange(first, dtype=jnp.int32)
    index_b = jnp.arange(second, dtype=jnp.int32)
    cos_a, sin_a = turn_angles(index_a[:, None], index_a[None, :], first)
    sin_a = sign * sin_a
    cos_b, sin_b = turn_angles(index_b[:, None], index_b[None, :], second)
    sin_b = sign * sin_b
    twist_cos, twist_sin = turn_angles(index_a[:, None], index_b[None, :], length)
    twist_cos = twist_cos[:, :, None]
    twist_sin = sign * twist_sin[:, :, None]
    real_three = real.reshape(first, second, width)
    step_real = contract("abm,ak->kbm", real_three, cos_a)
    step_imag = contract("abm,ak->kbm", real_three, sin_a)
    if imag is not None:
        imag_three = imag.reshape(first, second, width)
        step_real = step_real - contract("abm,ak->kbm", imag_three, sin_a)
        step_imag = step_imag + contract("abm,ak->kbm", imag_three, cos_a)
    turned_real = step_real * twist_cos - step_imag * twist_sin
    turned_imag = step_real * twist_sin + step_imag * twist_cos
    out_real = contract("kbm,bj->jkm", turned_real, cos_b) - contract(
        "kbm,bj->jkm", turned_imag, sin_b
    )
    out_imag = contract("kbm,bj->jkm", turned_real, sin_b) + contract(
        "kbm,bj->jkm", turned_imag, cos_b
    )
    return (out_real.reshape(length, width), out_imag.reshape(length, width))


def forward(stacked, order):
    count, block, grid_side = stacked.shape
    owners = grid_side // block
    total = grid_side * grid_side
    send = jnp.transpose(stacked.reshape(count, block, owners, block), (2, 1, 0, 3)).reshape(
        owners, block, count * block
    )
    columns = redistribute(send).reshape(grid_side, count * block)
    first_real, first_imag = axis_dft(columns, None, -1.0)
    first_real = first_real.reshape(grid_side, count, block)
    first_imag = first_imag.reshape(grid_side, count, block)
    col_index = own_block() * block + jnp.arange(block, dtype=jnp.int32)
    cos_turn, sin_turn = turn_angles(order[:, None, None], col_index[None, None, :], total)
    turned_real = first_real * cos_turn + first_imag * sin_turn
    turned_imag = first_imag * cos_turn - first_real * sin_turn
    send_two = jnp.concatenate([turned_real, turned_imag], axis=1).reshape(
        owners, block, 2 * count * block
    )
    gotten = redistribute(send_two).reshape(owners, block, 2 * count, block)
    flat_real = jnp.transpose(gotten[:, :, :count, :], (0, 3, 1, 2)).reshape(
        grid_side, block * count
    )
    flat_imag = jnp.transpose(gotten[:, :, count:, :], (0, 3, 1, 2)).reshape(
        grid_side, block * count
    )
    out_real, out_imag = axis_dft(flat_real, flat_imag, -1.0)
    spec_real = jnp.transpose(out_real.reshape(grid_side, block, count), (1, 2, 0))
    spec_imag = jnp.transpose(out_imag.reshape(grid_side, block, count), (1, 2, 0))
    return (spec_real, spec_imag)


def inverse(spec_real, spec_imag, order):
    block, count, grid_side = spec_real.shape
    owners = grid_side // block
    total = grid_side * grid_side
    flat_real = jnp.transpose(spec_real, (2, 0, 1)).reshape(grid_side, block * count)
    flat_imag = jnp.transpose(spec_imag, (2, 0, 1)).reshape(grid_side, block * count)
    out_real, out_imag = axis_dft(flat_real, flat_imag, 1.0)
    back_real = jnp.transpose(out_real.reshape(owners, block, block, count), (0, 2, 3, 1))
    back_imag = jnp.transpose(out_imag.reshape(owners, block, block, count), (0, 2, 3, 1))
    freq_index = lax.dynamic_slice_in_dim(order, own_block() * block, block, 0)
    col_index = (
        jnp.arange(owners, dtype=jnp.int32)[:, None] * block
        + jnp.arange(block, dtype=jnp.int32)[None, :]
    )
    cos_turn, sin_turn = turn_angles(
        freq_index[None, :, None, None], col_index[:, None, None, :], total
    )
    turned_real = back_real * cos_turn - back_imag * sin_turn
    turned_imag = back_real * sin_turn + back_imag * cos_turn
    send = jnp.concatenate([turned_real, turned_imag], axis=2).reshape(
        owners, block, 2 * count * block
    )
    gotten = redistribute(send).reshape(grid_side, 2 * count * block)
    real_part = gotten[:, : count * block]
    imag_part = gotten[:, count * block :]
    full_real, full_imag = axis_dft(real_part, imag_part, 1.0)
    values = full_real * (1.0 / total)
    returned = redistribute(values.reshape(owners, block, count * block)).reshape(
        owners, block, count, block
    )
    return jnp.transpose(returned, (2, 1, 0, 3)).reshape(count, block, grid_side)


def spread_shards(outer_gate, inner_gate, signal, grad_out, filter_weight):
    grid_side = filter_weight.shape[1]
    freq_index = jnp.arange(grid_side, dtype=jnp.int32)
    outer_f = outer_gate[0].astype(jnp.float32)
    inner_f = inner_gate[0].astype(jnp.float32)
    signal_f = signal[0].astype(jnp.float32)
    grad_f = grad_out[0].astype(jnp.float32)
    channels = inner_f.shape[0]
    gated = inner_f * signal_f
    grad_conv = grad_f * outer_f
    taps = (filter_weight * (1.0 / grid_side))[None]
    spec_real, spec_imag = forward(jnp.concatenate([gated, grad_conv], axis=0), freq_index)
    filt_real, filt_imag = forward(taps, freq_index)
    gated_real = spec_real[:, :channels]
    gated_imag = spec_imag[:, :channels]
    cot_real = spec_real[:, channels : 2 * channels]
    cot_imag = spec_imag[:, channels : 2 * channels]
    conv_real = filt_real * gated_real - filt_imag * gated_imag
    conv_imag = filt_real * gated_imag + filt_imag * gated_real
    back_real = filt_real * cot_real + filt_imag * cot_imag
    back_imag = filt_real * cot_imag - filt_imag * cot_real
    term_real = jnp.sum(gated_real * cot_real + gated_imag * cot_imag, axis=1, keepdims=True)
    term_imag = jnp.sum(gated_real * cot_imag - gated_imag * cot_real, axis=1, keepdims=True)
    values = inverse(
        jnp.concatenate([conv_real, back_real, term_real], axis=1),
        jnp.concatenate([conv_imag, back_imag, term_imag], axis=1),
        freq_index,
    )
    grad_filter = lax.psum(values[2 * channels], "dp") * (1.0 / grid_side)
    conv = values[:channels]
    grad_gated = values[channels : 2 * channels]
    grad_outer = (grad_f * conv).astype(jnp.bfloat16)[None]
    grad_inner = (grad_gated * signal_f).astype(jnp.bfloat16)[None]
    grad_signal = (grad_gated * inner_f).astype(jnp.bfloat16)[None]
    return (grad_outer, grad_inner, grad_signal, grad_filter)


VMEM_LIMIT = 18 * 1024 * 1024
UNDER_WAY = 3
ROW_PAD = 16
LANE_PAD = 128


def up_to(value, unit):
    return -(-value // unit) * unit


def high_low(table):
    high = table.astype(jnp.bfloat16)
    low = (table - high.astype(np.float64)).astype(jnp.bfloat16)
    return np.stack([high, low])


class Plan:
    def __init__(self, side):
        half = side // 2
        self.side, self.half, self.quarter = side, half, side // 4
        self.evens = up_to(half // 2 + 1, ROW_PAD)
        self.odds = half // 2
        self.rows = self.evens + self.odds
        self.even_depth = up_to(2 * self.evens, LANE_PAD)
        total = side * side
        even_k = 2 * np.arange(self.evens)
        odd_k = 2 * np.arange(self.odds) + 1
        live = (even_k <= half).astype(np.float64)
        p = np.arange(half)

        def waves(k, scale):
            angle = 2.0 * np.pi * (k[:, None] * p[None, :] % side) / side
            return np.concatenate([np.cos(angle) * scale[:, None], -np.sin(angle) * scale[:, None]])

        ones = np.ones(self.odds)
        self.into_even = high_low(waves(even_k, live))
        self.into_odd = high_low(waves(odd_k, ones))
        weight = np.where((even_k == 0) | (even_k == half), 1.0, 2.0) * live / total
        back_even = np.zeros((half, self.even_depth))
        back_even[:, : 2 * self.evens] = waves(even_k, weight).T
        self.back_even = high_low(back_even)
        self.back_odd = high_low(waves(odd_k, ones * 2.0 / total).T)
        k = np.concatenate([even_k, odd_k])
        turn = 2.0 * np.pi * (k[:, None] * np.arange(side)[None, :] % total) / total
        self.turn = np.stack([np.cos(turn), np.sin(turn)]).astype(np.float32)
        q = np.arange(self.quarter)
        mixes = []
        for r in range(4):
            angle = 2.0 * np.pi * (q[:, None] * (4 * q[None, :] + r) % side) / side
            cos, sin = np.cos(angle), np.sin(angle)
            mixes.append(np.block([[cos, -sin], [sin, cos]]))
        self.mix = high_low(np.stack(mixes))
        self.row_tile = next(t for t in (176, 264, 16, 8) if self.rows % t == 0)


def split_terms(values):
    high = values.astype(jnp.bfloat16)
    return high, (values - high.astype(jnp.float32)).astype(jnp.bfloat16)


def dot_in(table, rows, high, low):
    dot = functools.partial(jnp.dot, preferred_element_type=jnp.float32)
    first, second = table[0, rows], table[1, rows]
    return dot(first, high) + (dot(first, low) + dot(second, high))


def block_views(plan, owners, me, blocks, values):
    size = plan.side // owners
    for step in range(owners):
        at = pl.multiple_of((me[0] ^ step) * size, size)
        yield blocks[step].at[pl.ds(0, size)], values.at[pl.ds(at, size)]


def tile_views(plan, grid, me, tiles, values):
    parts, rows, cols = grid
    block = plan.side // (rows * cols)
    height = block // parts
    own_row = me[0] // cols
    for part in range(parts):
        for col in range(cols):
            for i in range(rows):
                at = ((own_row ^ i) * cols + col) * block + part * height
                yield tiles[0].at[part * cols + col, i], values.at[pl.ds(pl.multiple_of(at, height), height)]


def start_all(pairs, sems):
    copies = [pltpu.make_async_copy(source, to, sems.at[i]) for i, (source, to) in enumerate(pairs)]
    for copy in copies:
        copy.start()
    return copies


def wait_all(copies):
    for copy in copies:
        copy.wait()


def to_spectrum(plan, values, into_even, into_odd, turn, mix, spec, mid):
    side, half, quarter = plan.side, plan.half, plan.quarter

    @pl.loop(0, side // quarter)
    def columns(tile):
        cols = pl.ds(pl.multiple_of(tile * quarter, quarter), quarter)
        top, bottom = values[pl.ds(0, half), cols], values[pl.ds(half, half), cols]
        for first, count, table, part in (
            (0, plan.evens, into_even, top + bottom),
            (plan.evens, plan.odds, into_odd, top - bottom),
        ):
            out = dot_in(table, slice(None), *split_terms(part))
            real, imag = out[:count], out[count:]
            rows = pl.ds(first, count)
            cos, sin = turn[0, rows, cols], turn[1, rows, cols]
            mid[0, rows, cols] = real * cos + imag * sin
            mid[1, rows, cols] = imag * cos - real * sin

    @pl.loop(0, plan.rows // plan.row_tile)
    def rows_loop(tile):
        rows = pl.ds(pl.multiple_of(tile * plan.row_tile, plan.row_tile), plan.row_tile)
        real = [mid[0, rows, pl.ds(j * quarter, quarter)] for j in range(4)]
        imag = [mid[1, rows, pl.ds(j * quarter, quarter)] for j in range(4)]
        sum_r, sum_i = real[0] + real[2], imag[0] + imag[2]
        dif_r, dif_i = real[0] - real[2], imag[0] - imag[2]
        two_r, two_i = real[1] + real[3], imag[1] + imag[3]
        odd_r, odd_i = real[1] - real[3], imag[1] - imag[3]
        turns = (
            (sum_r + two_r, sum_i + two_i),
            (dif_r + odd_i, dif_i - odd_r),
            (sum_r - two_r, sum_i - two_i),
            (dif_r - odd_i, dif_i + odd_r),
        )
        dot = functools.partial(jnp.dot, preferred_element_type=jnp.float32)
        for r, pair in enumerate(turns):
            high, low = split_terms(jnp.concatenate(pair, axis=1))
            out = dot(high, mix[0, r]) + (dot(low, mix[0, r]) + dot(high, mix[1, r]))
            cols = pl.ds(r * quarter, quarter)
            spec[0, rows, cols] = out[:, :quarter]
            spec[1, rows, cols] = out[:, quarter:]


def inverse_rows(plan, conjugate, left, right, turn, mix, mid):
    quarter = plan.quarter

    @pl.loop(0, plan.rows // plan.row_tile)
    def rows_loop(tile):
        rows = pl.ds(pl.multiple_of(tile * plan.row_tile, plan.row_tile), plan.row_tile)
        real, imag = [], []
        for r in range(4):
            cols = pl.ds(r * quarter, quarter)
            left_r, left_i = left[0, rows, cols], left[1, rows, cols]
            right_r, right_i = right[0, rows, cols], right[1, rows, cols]
            if conjugate:
                left_i = -left_i
            pair = (left_r * right_r - left_i * right_i, left_r * right_i + left_i * right_r)
            high, low = split_terms(jnp.concatenate(pair, axis=1))

            def dot(part, table):
                return lax.dot_general(
                    part, table, (((1,), (1,)), ((), ())), preferred_element_type=jnp.float32
                )

            out = dot(high, mix[0, r]) + (dot(low, mix[0, r]) + dot(high, mix[1, r]))
            real.append(out[:, :quarter])
            imag.append(out[:, quarter:])
        sum_r, sum_i = real[0] + real[2], imag[0] + imag[2]
        dif_r, dif_i = real[0] - real[2], imag[0] - imag[2]
        two_r, two_i = real[1] + real[3], imag[1] + imag[3]
        odd_r, odd_i = real[1] - real[3], imag[1] - imag[3]
        turns = (
            (sum_r + two_r, sum_i + two_i),
            (dif_r - odd_i, dif_i + odd_r),
            (sum_r - two_r, sum_i - two_i),
            (dif_r + odd_i, dif_i - odd_r),
        )
        for j, (got_r, got_i) in enumerate(turns):
            cols = pl.ds(j * quarter, quarter)
            cos, sin = turn[0, rows, cols], turn[1, rows, cols]
            mid[0, rows, cols] = got_r * cos - got_i * sin
            mid[1, rows, cols] = got_r * sin + got_i * cos


def inverse_columns(plan, back_even, back_odd, mid, values):
    side, half, quarter = plan.side, plan.half, plan.quarter

    @pl.loop(0, side // quarter)
    def columns(tile):
        cols = pl.ds(pl.multiple_of(tile * quarter, quarter), quarter)
        even = [mid[0, pl.ds(0, plan.evens), cols], mid[1, pl.ds(0, plan.evens), cols]]
        if plan.even_depth > 2 * plan.evens:
            even.append(jnp.zeros((plan.even_depth - 2 * plan.evens, quarter), jnp.float32))
        odd = [mid[0, pl.ds(plan.evens, plan.odds), cols], mid[1, pl.ds(plan.evens, plan.odds), cols]]
        from_even = dot_in(back_even, slice(None), *split_terms(jnp.concatenate(even)))
        from_odd = dot_in(back_odd, slice(None), *split_terms(jnp.concatenate(odd)))
        values[pl.ds(0, half), cols] = from_even + from_odd
        values[pl.ds(half, half), cols] = from_even - from_odd


def filter_kernel(plan, views, count, me, *refs):
    tiles = refs[:count]
    into_even, into_odd, turn, mix, spec, values, mid, sems = refs[count:]
    wait_all(start_all(views(me, tiles, values), sems))
    to_spectrum(plan, values, into_even, into_odd, turn, mix, spec, mid)


def conv_kernel(plan, views, count, me, filt, *refs):
    blocks, tables = refs[:count], refs[count : count + 6]
    into_even, into_odd, back_even, back_odd, turn, mix = tables
    spec, outs = refs[count + 6], refs[count + 7 : 2 * count + 7]
    values, mid, sems = refs[2 * count + 7 :]
    wait_all(start_all(views(me, blocks, values), sems))
    to_spectrum(plan, values, into_even, into_odd, turn, mix, spec, mid)
    inverse_rows(plan, False, filt, spec, turn, mix, mid)
    inverse_columns(plan, back_even, back_odd, mid, values)
    wait_all(start_all(((to, source) for source, to in views(me, outs, values)), sems))


def term_kernel(plan, views, term_views, count, me, gated, *refs):
    blocks, tables = refs[:count], refs[count : count + 6]
    into_even, into_odd, back_even, back_odd, turn, mix = tables
    spec, term, values, mid, sems, term_sems = refs[count + 6 :]
    wait_all(start_all(views(me, blocks, values), sems))
    to_spectrum(plan, values, into_even, into_odd, turn, mix, spec, mid)
    inverse_rows(plan, True, gated, spec, turn, mix, mid)
    inverse_columns(plan, back_even, back_odd, mid, values)
    wait_all(start_all(((to, source) for source, to in term_views(me, [term], values)), term_sems))


def grad_kernel(plan, views, count, me, filt, spec, back_even, back_odd, turn, mix, *refs):
    outs = refs[:count]
    values, mid, sems = refs[count:]
    inverse_rows(plan, True, filt, spec, turn, mix, mid)
    inverse_columns(plan, back_even, back_odd, mid, values)
    wait_all(start_all(((to, source) for source, to in views(me, outs, values)), sems))


def smem():
    return pl.BlockSpec(memory_space=pltpu.SMEM)


def vmem():
    return pl.BlockSpec(memory_space=pltpu.VMEM)


def anywhere():
    return pl.BlockSpec(memory_space=pl.ANY)


def kernel_cost(plan):
    return pl.CostEstimate(flops=plan.side**2, bytes_accessed=plan.side**2, transcendentals=0)


def call_kernel(plan, kernel, name, args, in_specs, out_shape, out_specs, scratch):
    return pl.pallas_call(
        kernel,
        out_shape=out_shape,
        in_specs=in_specs,
        out_specs=out_specs,
        scratch_shapes=scratch,
        compiler_params=pltpu.CompilerParams(vmem_limit_bytes=VMEM_LIMIT),
        cost_estimate=kernel_cost(plan),
        name=name,
    )(*args)


def float_array(shape):
    return jax.ShapeDtypeStruct(shape, jnp.float32)


def filter_spectrum(plan, me, tiles, views, copies):
    shape = (2, plan.rows, plan.side)
    return call_kernel(
        plan,
        functools.partial(filter_kernel, plan, views, len(tiles)),
        "filter_spectrum",
        (me, *tiles, plan.into_even, plan.into_odd, plan.turn, plan.mix),
        [smem()] + [anywhere()] * len(tiles) + [vmem()] * 4,
        float_array(shape),
        vmem(),
        [
            pltpu.VMEM((plan.side, plan.side), jnp.float32),
            pltpu.VMEM(shape, jnp.float32),
            pltpu.SemaphoreType.DMA((copies,)),
        ],
    )


def tables_of(plan):
    return (plan.into_even, plan.into_odd, plan.back_even, plan.back_odd, plan.turn, plan.mix)


def conv_of(plan, me, filt, blocks, views):
    count = len(blocks)
    shape = (2, plan.rows, plan.side)
    spec, *outs = call_kernel(
        plan,
        functools.partial(conv_kernel, plan, views, count),
        "conv_of",
        (me, filt, *blocks, *tables_of(plan)),
        [smem(), vmem()] + [vmem()] * count + [vmem()] * 6,
        [float_array(shape)] + [float_array((plan.side // count, plan.side))] * count,
        [vmem()] * (count + 1),
        [
            pltpu.VMEM((plan.side, plan.side), jnp.float32),
            pltpu.VMEM(shape, jnp.float32),
            pltpu.SemaphoreType.DMA((count,)),
        ],
    )
    return spec, outs


def term_of(plan, me, gated, blocks, views, term_shape, term_views):
    count = len(blocks)
    shape = (2, plan.rows, plan.side)
    return call_kernel(
        plan,
        functools.partial(term_kernel, plan, views, term_views, count),
        "term_of",
        (me, gated, *blocks, *tables_of(plan)),
        [smem(), vmem()] + [vmem()] * count + [vmem()] * 6,
        [float_array(shape), float_array(term_shape)],
        [vmem(), anywhere()],
        [
            pltpu.VMEM((plan.side, plan.side), jnp.float32),
            pltpu.VMEM(shape, jnp.float32),
            pltpu.SemaphoreType.DMA((count,)),
            pltpu.SemaphoreType.DMA((math.prod(term_shape[:2]),)),
        ],
    )


def grad_of(plan, me, filt, spec, count, views):
    return call_kernel(
        plan,
        functools.partial(grad_kernel, plan, views, count),
        "grad_of",
        (me, filt, spec, *tables_of(plan)[2:]),
        [smem()] + [vmem()] * 6,
        [float_array((plan.side // count, plan.side))] * count,
        [vmem()] * count,
        [
            pltpu.VMEM((plan.side, plan.side), jnp.float32),
            pltpu.VMEM((2, plan.rows, plan.side), jnp.float32),
            pltpu.SemaphoreType.DMA((count,)),
        ],
    )


def pairwise(block, axis, step):
    return lax.ppermute(block, axis, [(i, i ^ step) for i in range(lax.axis_size(axis))])


def after(first, then):
    return lax.optimization_barrier((first, then))[1]


def gate_kernel(steps, gates, me, *refs):
    count = len(steps)
    blocks = refs[:count]
    ins = refs[count : count + gates]
    outs, got, sems = refs[-gates - 2 : -2], refs[-2], refs[-1]
    here = pl.program_id(0)

    def copy_of(i):
        return pltpu.make_async_copy(blocks[i], got.at[i], sems.at[i])

    @pl.when(here == 0)
    def start():
        for i in range(count):
            copy_of(i).start()

    for i in range(count):

        @pl.when(here == i)
        def wait():
            copy_of(i).wait()

    values = got[here]
    for gate, out in zip(ins, outs):
        out[0] = (gate[0].astype(jnp.float32) * values).astype(jnp.bfloat16)


def gated_by(me, steps, blocks, gates, done=()):
    count = len(steps)
    shape = gates[0].shape

    def place(i, me):
        step = steps[-1]
        for j in range(count - 1):
            step = jnp.where(i == j, steps[j], step)
        return (me[0] ^ step, 0, 0)

    spec = pl.BlockSpec((1,) + shape[1:], place)
    size = count * shape[1] * shape[2]
    first_done = 1 + count + len(gates)
    return pl.pallas_call(
        functools.partial(gate_kernel, steps, len(gates)),
        grid_spec=pltpu.PrefetchScalarGridSpec(
            num_scalar_prefetch=1,
            grid=(count,),
            in_specs=[anywhere()] * count + [spec] * len(gates) + [anywhere()] * len(done),
            out_specs=[spec] * len(gates),
            scratch_shapes=[
                pltpu.VMEM((count,) + shape[1:], jnp.float32),
                pltpu.SemaphoreType.DMA((count,)),
            ],
        ),
        out_shape=[jax.ShapeDtypeStruct(shape, jnp.bfloat16)] * len(gates),
        input_output_aliases={first_done + i: i for i in range(len(done))},
        compiler_params=pltpu.CompilerParams(vmem_limit_bytes=VMEM_LIMIT),
        cost_estimate=pl.CostEstimate(
            flops=size * len(gates), bytes_accessed=4 * size * (1 + len(gates)), transcendentals=0
        ),
        name="gate_out",
    )(me, *blocks, *gates, *done)


def send_order(owners, cols):
    far = sorted(range(owners // 2, owners), key=lambda s: (-s // cols, -s))
    near = sorted(range(1, owners // 2), key=lambda s: (s % cols, -s))
    return far, near


def channel_shards(outer_gate, inner_gate, signal, grad_out, filter_weight):
    block, side = filter_weight.shape
    plan = Plan(side)
    parts, rows, cols = (lax.axis_size(name) for name in ("dp", "row", "col"))
    owners = rows * cols
    place = own_block()
    me = jnp.reshape(place, (1,)).astype(jnp.int32)
    far, near = send_order(owners, cols)
    order = far[:2]
    for i in range(2, len(far)):
        order = order + near[i - 2 : i - 1] + far[i : i + 1]
    order = order[:-1] + near[len(far) - 2 :] + order[-1:]
    by_block = functools.partial(block_views, plan, owners)
    by_tile = functools.partial(tile_views, plan, (parts, rows, cols))

    def gated_block(left, right, step):
        at = place ^ step
        return lax.dynamic_index_in_dim(left[0], at, 0, False).astype(
            jnp.float32
        ) * lax.dynamic_index_in_dim(right[0], at, 0, False).astype(jnp.float32)

    crossed, neared = [], []

    def exchange(blocks, what, order, extra=None):
        got = [blocks[0]] + [None] * (owners - 1)
        before, near_before = len(crossed), list(neared)
        neared.clear()
        for step in order:
            mine, waits = blocks[step], []
            if step in far:
                waits = crossed[max(0, len(crossed) - UNDER_WAY - 1) : max(0, len(crossed) - UNDER_WAY + 1)]
                if len(crossed) - before >= len(far) // 2:
                    waits = waits + near_before
            elif before:
                waits = crossed[before - 1 : before]
            if waits:
                mine = after(waits, mine)
            with jax.named_scope(f"{what}_{step}"):
                got[step] = pairwise(mine, ("row", "col"), step)
            (crossed if step in far else neared).append(got[step])
        return got

    height = block // parts
    own_part = lax.dynamic_slice_in_dim(filter_weight, lax.axis_index("dp") * height, height, 0)
    own_part = own_part * (1.0 / side)
    inner, values = inner_gate, signal
    gated = [None] * owners
    for step in order + [0]:
        gated[step] = gated_block(inner, values, step)
        if step and step % cols == 0:
            gated[step] = jnp.concatenate([gated[step], own_part])
        if step == order[0]:
            inner, values = after(gated[step], [inner_gate, signal])
    gated = exchange(gated, "gated", order)
    over_row = jnp.stack([own_part] + [gated[i * cols][block:] for i in range(1, rows)])
    grad_conv = [gated_block(grad_out, outer_gate, step) for step in range(owners)]
    over_row = after([gated[step] for step in far] + grad_conv, over_row)
    over_all = [lax.all_gather(over_row, ("dp", "col"))]
    filt = filter_spectrum(plan, me, over_all, by_tile, parts * owners)

    spec, conv_out = conv_of(plan, me, filt, after(filt, gated), by_block)
    grad_conv[near[-1]] = after(conv_out[0], grad_conv[near[-1]])
    grad_conv = exchange(grad_conv, "grad_conv", order)
    conv = exchange(conv_out, "conv", order)
    tile_shape = (parts * cols, rows, height, side)
    cot, term = term_of(plan, me, spec, grad_conv, by_block, tile_shape, by_tile)
    back_out = grad_of(plan, me, filt, cot, owners, by_block)
    grad_gated = exchange(back_out, "grad_gated", order)

    term = after([conv[step] for step in far[:2]], term)
    term = lax.psum_scatter(term, ("dp", "col"), scatter_dimension=0, tiled=False)
    with jax.named_scope("rows_sum"):
        arrived = [pairwise(term[i], "row", i) for i in range(1, rows)]
    total = sum(arrived, term[0]) * (1.0 / side)
    every = [0] + order
    (grad_outer,) = gated_by(me, every, [conv[step] for step in every], [grad_out[0]])
    total = after(grad_outer, total)
    with jax.named_scope("parts_gather"):
        others = [pairwise(total, "dp", i) for i in range(1, parts)]
    pieces = jnp.stack([total] + others)
    bit = 1
    while bit < parts:
        upper = (lax.axis_index("dp") & bit) != 0
        swapped = jnp.flip(pieces.reshape(parts // (2 * bit), 2, bit, height, side), 1)
        pieces = jnp.where(upper, swapped.reshape(pieces.shape), pieces)
        bit *= 2
    grad_filter = pieces.reshape(block, side)

    gates = [signal[0], inner_gate[0]]
    early, late = every[:-1], every[-1:]
    done = gated_by(me, early, [grad_gated[step] for step in early], gates)
    grad_inner, grad_signal = gated_by(me, late, [grad_gated[step] for step in late], gates, done)
    return (grad_outer[None], grad_inner[None], grad_signal[None], grad_filter)


def powers_of_two(*sizes):
    return all(size & (size - 1) == 0 for size in sizes)


def shards(*arrays):
    parts, rows, cols = (lax.axis_size(name) for name in ("dp", "row", "col"))
    side = arrays[0].shape[3]
    whole = arrays[0].shape[1] == rows * cols and rows >= 2 and cols == 2
    fits = powers_of_two(parts, rows, cols, side) and side // 4 % LANE_PAD == 0
    fits = fits and arrays[4].shape[0] // parts % ROW_PAD == 0
    return (channel_shards if whole and fits else spread_shards)(*arrays)


def solution(mesh):
    placed = (
        P("dp", None, ("row", "col"), None),
        P("dp", None, ("row", "col"), None),
        P("dp", None, ("row", "col"), None),
        P("dp", None, ("row", "col"), None),
        P(("row", "col"), None),
    )
    return jax.shard_map(
        shards,
        mesh=mesh,
        in_specs=placed,
        out_specs=(
            P("dp", None, ("row", "col"), None),
            P("dp", None, ("row", "col"), None),
            P("dp", None, ("row", "col"), None),
            P(("row", "col"), None),
        ),
        check_vma=False,
    )
```

```python
import functools
import math

import jax
import jax.numpy as jnp
import numpy as np
from jax import lax
from jax.experimental import pallas as pl
from jax.experimental.pallas import tpu as pltpu
from jax.sharding import PartitionSpec as P

TWO_PI = 2.0 * math.pi


def contract(form, left, right):
    return jnp.einsum(
        form, left, right, precision=lax.Precision.HIGHEST, preferred_element_type=jnp.float32
    )


def redistribute(blocks):
    return lax.all_to_all(blocks, ("row", "col"), split_axis=0, concat_axis=0, tiled=True)


def own_block():
    return lax.axis_index("row") * lax.axis_size("col") + lax.axis_index("col")


def turn_angles(first_index, second_index, total):
    product = first_index * second_index % total
    angles = product.astype(jnp.float32) * (TWO_PI / total)
    return (jnp.cos(angles), jnp.sin(angles))


def axis_dft(real, imag, sign):
    length, width = real.shape
    first = 1 << (length.bit_length() - 1) // 2
    second = length // first
    index_a = jnp.arange(first, dtype=jnp.int32)
    index_b = jnp.arange(second, dtype=jnp.int32)
    cos_a, sin_a = turn_angles(index_a[:, None], index_a[None, :], first)
    sin_a = sign * sin_a
    cos_b, sin_b = turn_angles(index_b[:, None], index_b[None, :], second)
    sin_b = sign * sin_b
    twist_cos, twist_sin = turn_angles(index_a[:, None], index_b[None, :], length)
    twist_cos = twist_cos[:, :, None]
    twist_sin = sign * twist_sin[:, :, None]
    real_three = real.reshape(first, second, width)
    step_real = contract("abm,ak->kbm", real_three, cos_a)
    step_imag = contract("abm,ak->kbm", real_three, sin_a)
    if imag is not None:
        imag_three = imag.reshape(first, second, width)
        step_real = step_real - contract("abm,ak->kbm", imag_three, sin_a)
        step_imag = step_imag + contract("abm,ak->kbm", imag_three, cos_a)
    turned_real = step_real * twist_cos - step_imag * twist_sin
    turned_imag = step_real * twist_sin + step_imag * twist_cos
    out_real = contract("kbm,bj->jkm", turned_real, cos_b) - contract(
        "kbm,bj->jkm", turned_imag, sin_b
    )
    out_imag = contract("kbm,bj->jkm", turned_real, sin_b) + contract(
        "kbm,bj->jkm", turned_imag, cos_b
    )
    return (out_real.reshape(length, width), out_imag.reshape(length, width))


def forward(stacked, order):
    count, block, grid_side = stacked.shape
    owners = grid_side // block
    total = grid_side * grid_side
    send = jnp.transpose(stacked.reshape(count, block, owners, block), (2, 1, 0, 3)).reshape(
        owners, block, count * block
    )
    columns = redistribute(send).reshape(grid_side, count * block)
    first_real, first_imag = axis_dft(columns, None, -1.0)
    first_real = first_real.reshape(grid_side, count, block)
    first_imag = first_imag.reshape(grid_side, count, block)
    col_index = own_block() * block + jnp.arange(block, dtype=jnp.int32)
    cos_turn, sin_turn = turn_angles(order[:, None, None], col_index[None, None, :], total)
    turned_real = first_real * cos_turn + first_imag * sin_turn
    turned_imag = first_imag * cos_turn - first_real * sin_turn
    send_two = jnp.concatenate([turned_real, turned_imag], axis=1).reshape(
        owners, block, 2 * count * block
    )
    gotten = redistribute(send_two).reshape(owners, block, 2 * count, block)
    flat_real = jnp.transpose(gotten[:, :, :count, :], (0, 3, 1, 2)).reshape(
        grid_side, block * count
    )
    flat_imag = jnp.transpose(gotten[:, :, count:, :], (0, 3, 1, 2)).reshape(
        grid_side, block * count
    )
    out_real, out_imag = axis_dft(flat_real, flat_imag, -1.0)
    spec_real = jnp.transpose(out_real.reshape(grid_side, block, count), (1, 2, 0))
    spec_imag = jnp.transpose(out_imag.reshape(grid_side, block, count), (1, 2, 0))
    return (spec_real, spec_imag)


def inverse(spec_real, spec_imag, order):
    block, count, grid_side = spec_real.shape
    owners = grid_side // block
    total = grid_side * grid_side
    flat_real = jnp.transpose(spec_real, (2, 0, 1)).reshape(grid_side, block * count)
    flat_imag = jnp.transpose(spec_imag, (2, 0, 1)).reshape(grid_side, block * count)
    out_real, out_imag = axis_dft(flat_real, flat_imag, 1.0)
    back_real = jnp.transpose(out_real.reshape(owners, block, block, count), (0, 2, 3, 1))
    back_imag = jnp.transpose(out_imag.reshape(owners, block, block, count), (0, 2, 3, 1))
    freq_index = lax.dynamic_slice_in_dim(order, own_block() * block, block, 0)
    col_index = (
        jnp.arange(owners, dtype=jnp.int32)[:, None] * block
        + jnp.arange(block, dtype=jnp.int32)[None, :]
    )
    cos_turn, sin_turn = turn_angles(
        freq_index[None, :, None, None], col_index[:, None, None, :], total
    )
    turned_real = back_real * cos_turn - back_imag * sin_turn
    turned_imag = back_real * sin_turn + back_imag * cos_turn
    send = jnp.concatenate([turned_real, turned_imag], axis=2).reshape(
        owners, block, 2 * count * block
    )
    gotten = redistribute(send).reshape(grid_side, 2 * count * block)
    real_part = gotten[:, : count * block]
    imag_part = gotten[:, count * block :]
    full_real, full_imag = axis_dft(real_part, imag_part, 1.0)
    values = full_real * (1.0 / total)
    returned = redistribute(values.reshape(owners, block, count * block)).reshape(
        owners, block, count, block
    )
    return jnp.transpose(returned, (2, 1, 0, 3)).reshape(count, block, grid_side)


def spread_shards(outer_gate, inner_gate, signal, grad_out, filter_weight):
    grid_side = filter_weight.shape[1]
    freq_index = jnp.arange(grid_side, dtype=jnp.int32)
    outer_f = outer_gate[0].astype(jnp.float32)
    inner_f = inner_gate[0].astype(jnp.float32)
    signal_f = signal[0].astype(jnp.float32)
    grad_f = grad_out[0].astype(jnp.float32)
    channels = inner_f.shape[0]
    gated = inner_f * signal_f
    grad_conv = grad_f * outer_f
    taps = (filter_weight * (1.0 / grid_side))[None]
    spec_real, spec_imag = forward(jnp.concatenate([gated, grad_conv], axis=0), freq_index)
    filt_real, filt_imag = forward(taps, freq_index)
    gated_real = spec_real[:, :channels]
    gated_imag = spec_imag[:, :channels]
    cot_real = spec_real[:, channels : 2 * channels]
    cot_imag = spec_imag[:, channels : 2 * channels]
    conv_real = filt_real * gated_real - filt_imag * gated_imag
    conv_imag = filt_real * gated_imag + filt_imag * gated_real
    back_real = filt_real * cot_real + filt_imag * cot_imag
    back_imag = filt_real * cot_imag - filt_imag * cot_real
    term_real = jnp.sum(gated_real * cot_real + gated_imag * cot_imag, axis=1, keepdims=True)
    term_imag = jnp.sum(gated_real * cot_imag - gated_imag * cot_real, axis=1, keepdims=True)
    values = inverse(
        jnp.concatenate([conv_real, back_real, term_real], axis=1),
        jnp.concatenate([conv_imag, back_imag, term_imag], axis=1),
        freq_index,
    )
    grad_filter = lax.psum(values[2 * channels], "dp") * (1.0 / grid_side)
    conv = values[:channels]
    grad_gated = values[channels : 2 * channels]
    grad_outer = (grad_f * conv).astype(jnp.bfloat16)[None]
    grad_inner = (grad_gated * signal_f).astype(jnp.bfloat16)[None]
    grad_signal = (grad_gated * inner_f).astype(jnp.bfloat16)[None]
    return (grad_outer, grad_inner, grad_signal, grad_filter)


VMEM_LIMIT = 18 * 1024 * 1024
ROW_PAD = 16
LANE_PAD = 128


def up_to(value, unit):
    return -(-value // unit) * unit


def high_low(table):
    high = table.astype(jnp.bfloat16)
    low = (table - high.astype(np.float64)).astype(jnp.bfloat16)
    return np.stack([high, low])


class Plan:
    def __init__(self, side):
        half = side // 2
        self.side, self.half, self.quarter = side, half, side // 4
        self.evens = up_to(half // 2 + 1, ROW_PAD)
        self.odds = half // 2
        self.rows = self.evens + self.odds
        self.even_depth = up_to(2 * self.evens, LANE_PAD)
        total = side * side
        even_k = 2 * np.arange(self.evens)
        odd_k = 2 * np.arange(self.odds) + 1
        live = (even_k <= half).astype(np.float64)
        p = np.arange(half)

        def waves(k, scale):
            angle = 2.0 * np.pi * (k[:, None] * p[None, :] % side) / side
            return np.concatenate([np.cos(angle) * scale[:, None], -np.sin(angle) * scale[:, None]])

        ones = np.ones(self.odds)
        self.into_even = high_low(waves(even_k, live))
        self.into_odd = high_low(waves(odd_k, ones))
        weight = np.where((even_k == 0) | (even_k == half), 1.0, 2.0) * live / total
        back_even = np.zeros((half, self.even_depth))
        back_even[:, : 2 * self.evens] = waves(even_k, weight).T
        self.back_even = high_low(back_even)
        self.back_odd = high_low(waves(odd_k, ones * 2.0 / total).T)
        k = np.concatenate([even_k, odd_k])
        turn = 2.0 * np.pi * (k[:, None] * np.arange(side)[None, :] % total) / total
        self.turn = np.stack([np.cos(turn), np.sin(turn)]).astype(np.float32)
        q = np.arange(self.quarter)
        mixes = []
        for r in range(4):
            angle = 2.0 * np.pi * (q[:, None] * (4 * q[None, :] + r) % side) / side
            cos, sin = np.cos(angle), np.sin(angle)
            mixes.append(np.block([[cos, -sin], [sin, cos]]))
        self.mix = high_low(np.stack(mixes))
        self.row_tile = next(t for t in (176, 264, 16, 8) if self.rows % t == 0)


def split_terms(values):
    high = values.astype(jnp.bfloat16)
    return high, (values - high.astype(jnp.float32)).astype(jnp.bfloat16)


def dot_in(table, rows, high, low):
    dot = functools.partial(jnp.dot, preferred_element_type=jnp.float32)
    first, second = table[0, rows], table[1, rows]
    return dot(first, high) + (dot(first, low) + dot(second, high))


def block_views(plan, owners, me, blocks, values):
    size = plan.side // owners
    for step in range(owners):
        at = pl.multiple_of((me[0] ^ step) * size, size)
        yield blocks[step].at[pl.ds(0, size)], values.at[pl.ds(at, size)]


def tile_views(plan, grid, me, tiles, values):
    parts, rows, cols = grid
    block = plan.side // (rows * cols)
    height = block // parts
    own_row = me[0] // cols
    for part in range(parts):
        for col in range(cols):
            for i in range(rows):
                at = ((own_row ^ i) * cols + col) * block + part * height
                yield tiles[0].at[part * cols + col, i], values.at[pl.ds(pl.multiple_of(at, height), height)]


def start_all(pairs, sems):
    copies = [pltpu.make_async_copy(source, to, sems.at[i]) for i, (source, to) in enumerate(pairs)]
    for copy in copies:
        copy.start()
    return copies


def wait_all(copies):
    for copy in copies:
        copy.wait()


def to_spectrum(plan, values, into_even, into_odd, turn, mix, spec, mid):
    side, half, quarter = plan.side, plan.half, plan.quarter

    @pl.loop(0, side // quarter)
    def columns(tile):
        cols = pl.ds(pl.multiple_of(tile * quarter, quarter), quarter)
        top, bottom = values[pl.ds(0, half), cols], values[pl.ds(half, half), cols]
        for first, count, table, part in (
            (0, plan.evens, into_even, top + bottom),
            (plan.evens, plan.odds, into_odd, top - bottom),
        ):
            out = dot_in(table, slice(None), *split_terms(part))
            real, imag = out[:count], out[count:]
            rows = pl.ds(first, count)
            cos, sin = turn[0, rows, cols], turn[1, rows, cols]
            mid[0, rows, cols] = real * cos + imag * sin
            mid[1, rows, cols] = imag * cos - real * sin

    @pl.loop(0, plan.rows // plan.row_tile)
    def rows_loop(tile):
        rows = pl.ds(pl.multiple_of(tile * plan.row_tile, plan.row_tile), plan.row_tile)
        real = [mid[0, rows, pl.ds(j * quarter, quarter)] for j in range(4)]
        imag = [mid[1, rows, pl.ds(j * quarter, quarter)] for j in range(4)]
        sum_r, sum_i = real[0] + real[2], imag[0] + imag[2]
        dif_r, dif_i = real[0] - real[2], imag[0] - imag[2]
        two_r, two_i = real[1] + real[3], imag[1] + imag[3]
        odd_r, odd_i = real[1] - real[3], imag[1] - imag[3]
        turns = (
            (sum_r + two_r, sum_i + two_i),
            (dif_r + odd_i, dif_i - odd_r),
            (sum_r - two_r, sum_i - two_i),
            (dif_r - odd_i, dif_i + odd_r),
        )
        dot = functools.partial(jnp.dot, preferred_element_type=jnp.float32)
        for r, pair in enumerate(turns):
            high, low = split_terms(jnp.concatenate(pair, axis=1))
            out = dot(high, mix[0, r]) + (dot(low, mix[0, r]) + dot(high, mix[1, r]))
            cols = pl.ds(r * quarter, quarter)
            spec[0, rows, cols] = out[:, :quarter]
            spec[1, rows, cols] = out[:, quarter:]


def inverse_rows(plan, conjugate, left, right, turn, mix, mid):
    quarter = plan.quarter

    @pl.loop(0, plan.rows // plan.row_tile)
    def rows_loop(tile):
        rows = pl.ds(pl.multiple_of(tile * plan.row_tile, plan.row_tile), plan.row_tile)
        real, imag = [], []
        for r in range(4):
            cols = pl.ds(r * quarter, quarter)
            left_r, left_i = left[0, rows, cols], left[1, rows, cols]
            right_r, right_i = right[0, rows, cols], right[1, rows, cols]
            if conjugate:
                left_i = -left_i
            pair = (left_r * right_r - left_i * right_i, left_r * right_i + left_i * right_r)
            high, low = split_terms(jnp.concatenate(pair, axis=1))

            def dot(part, table):
                return lax.dot_general(
                    part, table, (((1,), (1,)), ((), ())), preferred_element_type=jnp.float32
                )

            out = dot(high, mix[0, r]) + (dot(low, mix[0, r]) + dot(high, mix[1, r]))
            real.append(out[:, :quarter])
            imag.append(out[:, quarter:])
        sum_r, sum_i = real[0] + real[2], imag[0] + imag[2]
        dif_r, dif_i = real[0] - real[2], imag[0] - imag[2]
        two_r, two_i = real[1] + real[3], imag[1] + imag[3]
        odd_r, odd_i = real[1] - real[3], imag[1] - imag[3]
        turns = (
            (sum_r + two_r, sum_i + two_i),
            (dif_r - odd_i, dif_i + odd_r),
            (sum_r - two_r, sum_i - two_i),
            (dif_r + odd_i, dif_i - odd_r),
        )
        for j, (got_r, got_i) in enumerate(turns):
            cols = pl.ds(j * quarter, quarter)
            cos, sin = turn[0, rows, cols], turn[1, rows, cols]
            mid[0, rows, cols] = got_r * cos - got_i * sin
            mid[1, rows, cols] = got_r * sin + got_i * cos


def inverse_columns(plan, back_even, back_odd, mid, values):
    side, half, quarter = plan.side, plan.half, plan.quarter

    @pl.loop(0, side // quarter)
    def columns(tile):
        cols = pl.ds(pl.multiple_of(tile * quarter, quarter), quarter)
        even = [mid[0, pl.ds(0, plan.evens), cols], mid[1, pl.ds(0, plan.evens), cols]]
        if plan.even_depth > 2 * plan.evens:
            even.append(jnp.zeros((plan.even_depth - 2 * plan.evens, quarter), jnp.float32))
        odd = [mid[0, pl.ds(plan.evens, plan.odds), cols], mid[1, pl.ds(plan.evens, plan.odds), cols]]
        from_even = dot_in(back_even, slice(None), *split_terms(jnp.concatenate(even)))
        from_odd = dot_in(back_odd, slice(None), *split_terms(jnp.concatenate(odd)))
        values[pl.ds(0, half), cols] = from_even + from_odd
        values[pl.ds(half, half), cols] = from_even - from_odd


def filter_kernel(plan, views, count, me, *refs):
    tiles = refs[:count]
    into_even, into_odd, turn, mix, spec, values, mid, sems = refs[count:]
    wait_all(start_all(views(me, tiles, values), sems))
    to_spectrum(plan, values, into_even, into_odd, turn, mix, spec, mid)


def conv_kernel(plan, views, count, me, filt, *refs):
    blocks, tables = refs[:count], refs[count : count + 6]
    into_even, into_odd, back_even, back_odd, turn, mix = tables
    spec, outs = refs[count + 6], refs[count + 7 : 2 * count + 7]
    values, mid, sems = refs[2 * count + 7 :]
    wait_all(start_all(views(me, blocks, values), sems))
    to_spectrum(plan, values, into_even, into_odd, turn, mix, spec, mid)
    inverse_rows(plan, False, filt, spec, turn, mix, mid)
    inverse_columns(plan, back_even, back_odd, mid, values)
    wait_all(start_all(((to, source) for source, to in views(me, outs, values)), sems))


def term_kernel(plan, views, term_views, count, me, gated, *refs):
    blocks, tables = refs[:count], refs[count : count + 6]
    into_even, into_odd, back_even, back_odd, turn, mix = tables
    spec, term, values, mid, sems, term_sems = refs[count + 6 :]
    wait_all(start_all(views(me, blocks, values), sems))
    to_spectrum(plan, values, into_even, into_odd, turn, mix, spec, mid)
    inverse_rows(plan, True, gated, spec, turn, mix, mid)
    inverse_columns(plan, back_even, back_odd, mid, values)
    wait_all(start_all(((to, source) for source, to in term_views(me, [term], values)), term_sems))


def grad_kernel(plan, views, count, me, filt, spec, back_even, back_odd, turn, mix, *refs):
    outs = refs[:count]
    values, mid, sems = refs[count:]
    inverse_rows(plan, True, filt, spec, turn, mix, mid)
    inverse_columns(plan, back_even, back_odd, mid, values)
    wait_all(start_all(((to, source) for source, to in views(me, outs, values)), sems))


def smem():
    return pl.BlockSpec(memory_space=pltpu.SMEM)


def vmem():
    return pl.BlockSpec(memory_space=pltpu.VMEM)


def anywhere():
    return pl.BlockSpec(memory_space=pl.ANY)


def kernel_cost(plan):
    return pl.CostEstimate(flops=plan.side**2, bytes_accessed=plan.side**2, transcendentals=0)


def call_kernel(plan, kernel, name, args, in_specs, out_shape, out_specs, scratch):
    return pl.pallas_call(
        kernel,
        out_shape=out_shape,
        in_specs=in_specs,
        out_specs=out_specs,
        scratch_shapes=scratch,
        compiler_params=pltpu.CompilerParams(vmem_limit_bytes=VMEM_LIMIT),
        cost_estimate=kernel_cost(plan),
        name=name,
    )(*args)


def float_array(shape):
    return jax.ShapeDtypeStruct(shape, jnp.float32)


def filter_spectrum(plan, me, tiles, views, copies):
    shape = (2, plan.rows, plan.side)
    return call_kernel(
        plan,
        functools.partial(filter_kernel, plan, views, len(tiles)),
        "filter_spectrum",
        (me, *tiles, plan.into_even, plan.into_odd, plan.turn, plan.mix),
        [smem()] + [anywhere()] * len(tiles) + [vmem()] * 4,
        float_array(shape),
        vmem(),
        [
            pltpu.VMEM((plan.side, plan.side), jnp.float32),
            pltpu.VMEM(shape, jnp.float32),
            pltpu.SemaphoreType.DMA((copies,)),
        ],
    )


def tables_of(plan):
    return (plan.into_even, plan.into_odd, plan.back_even, plan.back_odd, plan.turn, plan.mix)


def conv_of(plan, me, filt, blocks, views):
    count = len(blocks)
    shape = (2, plan.rows, plan.side)
    spec, *outs = call_kernel(
        plan,
        functools.partial(conv_kernel, plan, views, count),
        "conv_of",
        (me, filt, *blocks, *tables_of(plan)),
        [smem(), vmem()] + [vmem()] * count + [vmem()] * 6,
        [float_array(shape)] + [float_array((plan.side // count, plan.side))] * count,
        [vmem()] * (count + 1),
        [
            pltpu.VMEM((plan.side, plan.side), jnp.float32),
            pltpu.VMEM(shape, jnp.float32),
            pltpu.SemaphoreType.DMA((count,)),
        ],
    )
    return spec, outs


def term_of(plan, me, gated, blocks, views, term_shape, term_views):
    count = len(blocks)
    shape = (2, plan.rows, plan.side)
    return call_kernel(
        plan,
        functools.partial(term_kernel, plan, views, term_views, count),
        "term_of",
        (me, gated, *blocks, *tables_of(plan)),
        [smem(), vmem()] + [vmem()] * count + [vmem()] * 6,
        [float_array(shape), float_array(term_shape)],
        [vmem(), anywhere()],
        [
            pltpu.VMEM((plan.side, plan.side), jnp.float32),
            pltpu.VMEM(shape, jnp.float32),
            pltpu.SemaphoreType.DMA((count,)),
            pltpu.SemaphoreType.DMA((math.prod(term_shape[:2]),)),
        ],
    )


def grad_of(plan, me, filt, spec, count, views):
    return call_kernel(
        plan,
        functools.partial(grad_kernel, plan, views, count),
        "grad_of",
        (me, filt, spec, *tables_of(plan)[2:]),
        [smem()] + [vmem()] * 6,
        [float_array((plan.side // count, plan.side))] * count,
        [vmem()] * count,
        [
            pltpu.VMEM((plan.side, plan.side), jnp.float32),
            pltpu.VMEM((2, plan.rows, plan.side), jnp.float32),
            pltpu.SemaphoreType.DMA((count,)),
        ],
    )


def pairwise(block, axis, step):
    return lax.ppermute(block, axis, [(i, i ^ step) for i in range(lax.axis_size(axis))])


def after(first, then):
    return lax.optimization_barrier((first, then))[1]


def gate_kernel(steps, gates, me, *refs):
    count = len(steps)
    blocks = refs[:count]
    ins = refs[count : count + gates]
    outs, got, sems = refs[-gates - 2 : -2], refs[-2], refs[-1]
    here = pl.program_id(0)

    def copy_of(i):
        return pltpu.make_async_copy(blocks[i], got.at[i], sems.at[i])

    @pl.when(here == 0)
    def start():
        for i in range(count):
            copy_of(i).start()

    for i in range(count):

        @pl.when(here == i)
        def wait():
            copy_of(i).wait()

    values = got[here]
    for gate, out in zip(ins, outs):
        out[0] = (gate[0].astype(jnp.float32) * values).astype(jnp.bfloat16)


def gated_by(me, steps, blocks, gates, done=()):
    count = len(steps)
    shape = gates[0].shape

    def place(i, me):
        step = steps[-1]
        for j in range(count - 1):
            step = jnp.where(i == j, steps[j], step)
        return (me[0] ^ step, 0, 0)

    spec = pl.BlockSpec((1,) + shape[1:], place)
    size = count * shape[1] * shape[2]
    first_done = 1 + count + len(gates)
    return pl.pallas_call(
        functools.partial(gate_kernel, steps, len(gates)),
        grid_spec=pltpu.PrefetchScalarGridSpec(
            num_scalar_prefetch=1,
            grid=(count,),
            in_specs=[anywhere()] * count + [spec] * len(gates) + [anywhere()] * len(done),
            out_specs=[spec] * len(gates),
            scratch_shapes=[
                pltpu.VMEM((count,) + shape[1:], jnp.float32),
                pltpu.SemaphoreType.DMA((count,)),
            ],
        ),
        out_shape=[jax.ShapeDtypeStruct(shape, jnp.bfloat16)] * len(gates),
        input_output_aliases={first_done + i: i for i in range(len(done))},
        compiler_params=pltpu.CompilerParams(vmem_limit_bytes=VMEM_LIMIT),
        cost_estimate=pl.CostEstimate(
            flops=size * len(gates), bytes_accessed=4 * size * (1 + len(gates)), transcendentals=0
        ),
        name="gate_out",
    )(me, *blocks, *gates, *done)


def send_order(owners, cols):
    far = sorted(range(owners // 2, owners), key=lambda s: (-s // cols, -s))
    near = sorted(range(1, owners // 2), key=lambda s: (s % cols, -s))
    return far, near


def channel_shards(outer_gate, inner_gate, signal, grad_out, filter_weight):
    block, side = filter_weight.shape
    plan = Plan(side)
    parts, rows, cols = (lax.axis_size(name) for name in ("dp", "row", "col"))
    owners = rows * cols
    place = own_block()
    me = jnp.reshape(place, (1,)).astype(jnp.int32)
    far, near = send_order(owners, cols)
    order = far[:2]
    for i in range(2, len(far)):
        order = order + near[i - 2 : i - 1] + far[i : i + 1]
    order = order[:-1] + near[len(far) - 2 :] + order[-1:]
    by_block = functools.partial(block_views, plan, owners)
    by_tile = functools.partial(tile_views, plan, (parts, rows, cols))

    def gated_block(left, right, step):
        at = place ^ step
        return lax.dynamic_index_in_dim(left[0], at, 0, False).astype(
            jnp.float32
        ) * lax.dynamic_index_in_dim(right[0], at, 0, False).astype(jnp.float32)

    crossed, neared = [], []

    def exchange(blocks, what, order, deep=3, near_wait=0):
        got = [blocks[0]] + [None] * (owners - 1)
        before, near_before = len(crossed), list(neared)
        neared.clear()
        for step in order:
            mine, waits = blocks[step], []
            if step in far:
                waits = crossed[max(0, len(crossed) - deep - 1) : max(0, len(crossed) - deep + 1)]
                if len(crossed) - before >= len(far) // 2:
                    waits = waits + near_before
            elif before:
                waits = crossed[before - 1 + near_wait : before + near_wait]
            if waits:
                mine = after(waits, mine)
            with jax.named_scope(f"{what}_{step}"):
                got[step] = pairwise(mine, ("row", "col"), step)
            (crossed if step in far else neared).append(got[step])
        return got

    height = block // parts
    own_part = lax.dynamic_slice_in_dim(filter_weight, lax.axis_index("dp") * height, height, 0)
    own_part = own_part * (1.0 / side)
    inner, values = inner_gate, signal
    gated = [None] * owners
    for step in order + [0]:
        gated[step] = gated_block(inner, values, step)
        if step and step % cols == 0:
            gated[step] = jnp.concatenate([gated[step], own_part])
        if step == order[0]:
            inner, values = after(gated[step], [inner_gate, signal])
    gated = exchange(gated, "gated", order)
    over_row = jnp.stack([own_part] + [gated[i * cols][block:] for i in range(1, rows)])
    grad_conv = [gated_block(grad_out, outer_gate, step) for step in range(owners)]
    over_row = after(gated + grad_conv, over_row)
    over_all = [lax.all_gather(over_row, ("dp", "col"))]
    filt = filter_spectrum(plan, me, over_all, by_tile, parts * owners)

    spec, conv_out = conv_of(plan, me, filt, after(filt, gated), by_block)
    for step in near[1:]:
        grad_conv[step] = after(conv_out[0], grad_conv[step])
    grad_conv = exchange(grad_conv, "grad_conv", order, 4)
    conv = exchange(conv_out, "conv", order, 4)
    tile_shape = (parts * cols, rows, height, side)
    cot, term = term_of(plan, me, spec, grad_conv, by_block, tile_shape, by_tile)
    back_out = grad_of(plan, me, filt, cot, owners, by_block)
    grad_gated = exchange(back_out, "grad_gated", order, 3, 2)

    term = after([conv[step] for step in far[:2]], term)
    term = lax.psum_scatter(term, ("dp", "col"), scatter_dimension=0, tiled=False)
    with jax.named_scope("rows_sum"):
        arrived = [pairwise(term[i], "row", i) for i in range(1, rows)]
    total = sum(arrived, term[0]) * (1.0 / side)
    every = [0] + order
    (grad_outer,) = gated_by(me, every, [conv[step] for step in every], [grad_out[0]])
    total = after(grad_outer, total)
    with jax.named_scope("parts_gather"):
        others = [pairwise(total, "dp", i) for i in range(1, parts)]
    pieces = jnp.stack([total] + others)
    bit = 1
    while bit < parts:
        upper = (lax.axis_index("dp") & bit) != 0
        swapped = jnp.flip(pieces.reshape(parts // (2 * bit), 2, bit, height, side), 1)
        pieces = jnp.where(upper, swapped.reshape(pieces.shape), pieces)
        bit *= 2
    grad_filter = pieces.reshape(block, side)

    gates = [signal[0], inner_gate[0]]
    early, late = every[:-1], every[-1:]
    done = gated_by(me, early, [grad_gated[step] for step in early], gates)
    grad_inner, grad_signal = gated_by(me, late, [grad_gated[step] for step in late], gates, done)
    return (grad_outer[None], grad_inner[None], grad_signal[None], grad_filter)


def powers_of_two(*sizes):
    return all(size & (size - 1) == 0 for size in sizes)


def shards(*arrays):
    parts, rows, cols = (lax.axis_size(name) for name in ("dp", "row", "col"))
    side = arrays[0].shape[3]
    whole = arrays[0].shape[1] == rows * cols and rows >= 2 and cols == 2
    fits = powers_of_two(parts, rows, cols, side) and side // 4 % LANE_PAD == 0
    fits = fits and arrays[4].shape[0] // parts % ROW_PAD == 0
    return (channel_shards if whole and fits else spread_shards)(*arrays)


def solution(mesh):
    placed = (
        P("dp", None, ("row", "col"), None),
        P("dp", None, ("row", "col"), None),
        P("dp", None, ("row", "col"), None),
        P("dp", None, ("row", "col"), None),
        P(("row", "col"), None),
    )
    return jax.shard_map(
        shards,
        mesh=mesh,
        in_specs=placed,
        out_specs=(
            P("dp", None, ("row", "col"), None),
            P("dp", None, ("row", "col"), None),
            P("dp", None, ("row", "col"), None),
            P(("row", "col"), None),
        ),
        check_vma=False,
    )
```

```python
import functools
import math

import jax
import jax.numpy as jnp
import numpy as np
from jax import lax
from jax.experimental import pallas as pl
from jax.experimental.pallas import tpu as pltpu
from jax.sharding import PartitionSpec as P

TWO_PI = 2.0 * math.pi


def contract(form, left, right):
    return jnp.einsum(
        form, left, right, precision=lax.Precision.HIGHEST, preferred_element_type=jnp.float32
    )


def redistribute(blocks):
    return lax.all_to_all(blocks, ("row", "col"), split_axis=0, concat_axis=0, tiled=True)


def own_block():
    return lax.axis_index("row") * lax.axis_size("col") + lax.axis_index("col")


def turn_angles(first_index, second_index, total):
    product = first_index * second_index % total
    angles = product.astype(jnp.float32) * (TWO_PI / total)
    return (jnp.cos(angles), jnp.sin(angles))


def axis_dft(real, imag, sign):
    length, width = real.shape
    first = 1 << (length.bit_length() - 1) // 2
    second = length // first
    index_a = jnp.arange(first, dtype=jnp.int32)
    index_b = jnp.arange(second, dtype=jnp.int32)
    cos_a, sin_a = turn_angles(index_a[:, None], index_a[None, :], first)
    sin_a = sign * sin_a
    cos_b, sin_b = turn_angles(index_b[:, None], index_b[None, :], second)
    sin_b = sign * sin_b
    twist_cos, twist_sin = turn_angles(index_a[:, None], index_b[None, :], length)
    twist_cos = twist_cos[:, :, None]
    twist_sin = sign * twist_sin[:, :, None]
    real_three = real.reshape(first, second, width)
    step_real = contract("abm,ak->kbm", real_three, cos_a)
    step_imag = contract("abm,ak->kbm", real_three, sin_a)
    if imag is not None:
        imag_three = imag.reshape(first, second, width)
        step_real = step_real - contract("abm,ak->kbm", imag_three, sin_a)
        step_imag = step_imag + contract("abm,ak->kbm", imag_three, cos_a)
    turned_real = step_real * twist_cos - step_imag * twist_sin
    turned_imag = step_real * twist_sin + step_imag * twist_cos
    out_real = contract("kbm,bj->jkm", turned_real, cos_b) - contract(
        "kbm,bj->jkm", turned_imag, sin_b
    )
    out_imag = contract("kbm,bj->jkm", turned_real, sin_b) + contract(
        "kbm,bj->jkm", turned_imag, cos_b
    )
    return (out_real.reshape(length, width), out_imag.reshape(length, width))


def forward(stacked, order):
    count, block, grid_side = stacked.shape
    owners = grid_side // block
    total = grid_side * grid_side
    send = jnp.transpose(stacked.reshape(count, block, owners, block), (2, 1, 0, 3)).reshape(
        owners, block, count * block
    )
    columns = redistribute(send).reshape(grid_side, count * block)
    first_real, first_imag = axis_dft(columns, None, -1.0)
    first_real = first_real.reshape(grid_side, count, block)
    first_imag = first_imag.reshape(grid_side, count, block)
    col_index = own_block() * block + jnp.arange(block, dtype=jnp.int32)
    cos_turn, sin_turn = turn_angles(order[:, None, None], col_index[None, None, :], total)
    turned_real = first_real * cos_turn + first_imag * sin_turn
    turned_imag = first_imag * cos_turn - first_real * sin_turn
    send_two = jnp.concatenate([turned_real, turned_imag], axis=1).reshape(
        owners, block, 2 * count * block
    )
    gotten = redistribute(send_two).reshape(owners, block, 2 * count, block)
    flat_real = jnp.transpose(gotten[:, :, :count, :], (0, 3, 1, 2)).reshape(
        grid_side, block * count
    )
    flat_imag = jnp.transpose(gotten[:, :, count:, :], (0, 3, 1, 2)).reshape(
        grid_side, block * count
    )
    out_real, out_imag = axis_dft(flat_real, flat_imag, -1.0)
    spec_real = jnp.transpose(out_real.reshape(grid_side, block, count), (1, 2, 0))
    spec_imag = jnp.transpose(out_imag.reshape(grid_side, block, count), (1, 2, 0))
    return (spec_real, spec_imag)


def inverse(spec_real, spec_imag, order):
    block, count, grid_side = spec_real.shape
    owners = grid_side // block
    total = grid_side * grid_side
    flat_real = jnp.transpose(spec_real, (2, 0, 1)).reshape(grid_side, block * count)
    flat_imag = jnp.transpose(spec_imag, (2, 0, 1)).reshape(grid_side, block * count)
    out_real, out_imag = axis_dft(flat_real, flat_imag, 1.0)
    back_real = jnp.transpose(out_real.reshape(owners, block, block, count), (0, 2, 3, 1))
    back_imag = jnp.transpose(out_imag.reshape(owners, block, block, count), (0, 2, 3, 1))
    freq_index = lax.dynamic_slice_in_dim(order, own_block() * block, block, 0)
    col_index = (
        jnp.arange(owners, dtype=jnp.int32)[:, None] * block
        + jnp.arange(block, dtype=jnp.int32)[None, :]
    )
    cos_turn, sin_turn = turn_angles(
        freq_index[None, :, None, None], col_index[:, None, None, :], total
    )
    turned_real = back_real * cos_turn - back_imag * sin_turn
    turned_imag = back_real * sin_turn + back_imag * cos_turn
    send = jnp.concatenate([turned_real, turned_imag], axis=2).reshape(
        owners, block, 2 * count * block
    )
    gotten = redistribute(send).reshape(grid_side, 2 * count * block)
    real_part = gotten[:, : count * block]
    imag_part = gotten[:, count * block :]
    full_real, full_imag = axis_dft(real_part, imag_part, 1.0)
    values = full_real * (1.0 / total)
    returned = redistribute(values.reshape(owners, block, count * block)).reshape(
        owners, block, count, block
    )
    return jnp.transpose(returned, (2, 1, 0, 3)).reshape(count, block, grid_side)


def spread_shards(outer_gate, inner_gate, signal, grad_out, filter_weight):
    grid_side = filter_weight.shape[1]
    freq_index = jnp.arange(grid_side, dtype=jnp.int32)
    outer_f = outer_gate[0].astype(jnp.float32)
    inner_f = inner_gate[0].astype(jnp.float32)
    signal_f = signal[0].astype(jnp.float32)
    grad_f = grad_out[0].astype(jnp.float32)
    channels = inner_f.shape[0]
    gated = inner_f * signal_f
    grad_conv = grad_f * outer_f
    taps = (filter_weight * (1.0 / grid_side))[None]
    spec_real, spec_imag = forward(jnp.concatenate([gated, grad_conv], axis=0), freq_index)
    filt_real, filt_imag = forward(taps, freq_index)
    gated_real = spec_real[:, :channels]
    gated_imag = spec_imag[:, :channels]
    cot_real = spec_real[:, channels : 2 * channels]
    cot_imag = spec_imag[:, channels : 2 * channels]
    conv_real = filt_real * gated_real - filt_imag * gated_imag
    conv_imag = filt_real * gated_imag + filt_imag * gated_real
    back_real = filt_real * cot_real + filt_imag * cot_imag
    back_imag = filt_real * cot_imag - filt_imag * cot_real
    term_real = jnp.sum(gated_real * cot_real + gated_imag * cot_imag, axis=1, keepdims=True)
    term_imag = jnp.sum(gated_real * cot_imag - gated_imag * cot_real, axis=1, keepdims=True)
    values = inverse(
        jnp.concatenate([conv_real, back_real, term_real], axis=1),
        jnp.concatenate([conv_imag, back_imag, term_imag], axis=1),
        freq_index,
    )
    grad_filter = lax.psum(values[2 * channels], "dp") * (1.0 / grid_side)
    conv = values[:channels]
    grad_gated = values[channels : 2 * channels]
    grad_outer = (grad_f * conv).astype(jnp.bfloat16)[None]
    grad_inner = (grad_gated * signal_f).astype(jnp.bfloat16)[None]
    grad_signal = (grad_gated * inner_f).astype(jnp.bfloat16)[None]
    return (grad_outer, grad_inner, grad_signal, grad_filter)


VMEM_LIMIT = 18 * 1024 * 1024
ROW_PAD = 16
LANE_PAD = 128


def up_to(value, unit):
    return -(-value // unit) * unit


def high_low(table):
    high = table.astype(jnp.bfloat16)
    low = (table - high.astype(np.float64)).astype(jnp.bfloat16)
    return np.stack([high, low])


class Plan:
    def __init__(self, side):
        half = side // 2
        self.side, self.half, self.quarter = side, half, side // 4
        self.evens = up_to(half // 2 + 1, ROW_PAD)
        self.odds = half // 2
        self.rows = self.evens + self.odds
        self.even_depth = up_to(2 * self.evens, LANE_PAD)
        total = side * side
        even_k = 2 * np.arange(self.evens)
        odd_k = 2 * np.arange(self.odds) + 1
        live = (even_k <= half).astype(np.float64)
        p = np.arange(half)

        def waves(k, scale):
            angle = 2.0 * np.pi * (k[:, None] * p[None, :] % side) / side
            return np.concatenate([np.cos(angle) * scale[:, None], -np.sin(angle) * scale[:, None]])

        ones = np.ones(self.odds)
        self.into_even = high_low(waves(even_k, live))
        self.into_odd = high_low(waves(odd_k, ones))
        weight = np.where((even_k == 0) | (even_k == half), 1.0, 2.0) * live / total
        back_even = np.zeros((half, self.even_depth))
        back_even[:, : 2 * self.evens] = waves(even_k, weight).T
        self.back_even = high_low(back_even)
        self.back_odd = high_low(waves(odd_k, ones * 2.0 / total).T)
        k = np.concatenate([even_k, odd_k])
        turn = 2.0 * np.pi * (k[:, None] * np.arange(side)[None, :] % total) / total
        self.turn = np.stack([np.cos(turn), np.sin(turn)]).astype(np.float32)
        q = np.arange(self.quarter)
        mixes = []
        for r in range(4):
            angle = 2.0 * np.pi * (q[:, None] * (4 * q[None, :] + r) % side) / side
            cos, sin = np.cos(angle), np.sin(angle)
            mixes.append(np.block([[cos, -sin], [sin, cos]]))
        self.mix = high_low(np.stack(mixes))
        self.row_tile = next(t for t in (176, 264, 16, 8) if self.rows % t == 0)


def split_terms(values):
    high = values.astype(jnp.bfloat16)
    return high, (values - high.astype(jnp.float32)).astype(jnp.bfloat16)


def dot_in(table, rows, high, low):
    dot = functools.partial(jnp.dot, preferred_element_type=jnp.float32)
    first, second = table[0, rows], table[1, rows]
    return dot(first, high) + (dot(first, low) + dot(second, high))


def block_views(plan, owners, me, blocks, values):
    size = plan.side // owners
    for step in range(owners):
        at = pl.multiple_of((me[0] ^ step) * size, size)
        yield blocks[step].at[pl.ds(0, size)], values.at[pl.ds(at, size)]


def tile_views(plan, grid, natural, me, tiles, values):
    parts, rows, cols = grid
    block = plan.side // (rows * cols)
    height = block // parts
    own_row = me[0] // cols
    for part in range(parts):
        for col in range(cols):
            for i in range(rows):
                row = i if natural else own_row ^ i
                at = (row * cols + col) * block + part * height
                at = at if natural else pl.multiple_of(at, height)
                yield tiles[0].at[part * cols + col, i], values.at[pl.ds(at, height)]


def start_all(pairs, sems):
    copies = [pltpu.make_async_copy(source, to, sems.at[i]) for i, (source, to) in enumerate(pairs)]
    for copy in copies:
        copy.start()
    return copies


def wait_all(copies):
    for copy in copies:
        copy.wait()


def to_spectrum(plan, values, into_even, into_odd, turn, mix, spec, mid):
    side, half, quarter = plan.side, plan.half, plan.quarter

    @pl.loop(0, side // quarter)
    def columns(tile):
        cols = pl.ds(pl.multiple_of(tile * quarter, quarter), quarter)
        top, bottom = values[pl.ds(0, half), cols], values[pl.ds(half, half), cols]
        for first, count, table, part in (
            (0, plan.evens, into_even, top + bottom),
            (plan.evens, plan.odds, into_odd, top - bottom),
        ):
            out = dot_in(table, slice(None), *split_terms(part))
            real, imag = out[:count], out[count:]
            rows = pl.ds(first, count)
            cos, sin = turn[0, rows, cols], turn[1, rows, cols]
            mid[0, rows, cols] = real * cos + imag * sin
            mid[1, rows, cols] = imag * cos - real * sin

    @pl.loop(0, plan.rows // plan.row_tile)
    def rows_loop(tile):
        rows = pl.ds(pl.multiple_of(tile * plan.row_tile, plan.row_tile), plan.row_tile)
        real = [mid[0, rows, pl.ds(j * quarter, quarter)] for j in range(4)]
        imag = [mid[1, rows, pl.ds(j * quarter, quarter)] for j in range(4)]
        sum_r, sum_i = real[0] + real[2], imag[0] + imag[2]
        dif_r, dif_i = real[0] - real[2], imag[0] - imag[2]
        two_r, two_i = real[1] + real[3], imag[1] + imag[3]
        odd_r, odd_i = real[1] - real[3], imag[1] - imag[3]
        turns = (
            (sum_r + two_r, sum_i + two_i),
            (dif_r + odd_i, dif_i - odd_r),
            (sum_r - two_r, sum_i - two_i),
            (dif_r - odd_i, dif_i + odd_r),
        )
        dot = functools.partial(jnp.dot, preferred_element_type=jnp.float32)
        for r, pair in enumerate(turns):
            high, low = split_terms(jnp.concatenate(pair, axis=1))
            out = dot(high, mix[0, r]) + (dot(low, mix[0, r]) + dot(high, mix[1, r]))
            cols = pl.ds(r * quarter, quarter)
            spec[0, rows, cols] = out[:, :quarter]
            spec[1, rows, cols] = out[:, quarter:]


def inverse_rows(plan, conjugate, left, right, turn, mix, mid):
    quarter = plan.quarter

    @pl.loop(0, plan.rows // plan.row_tile)
    def rows_loop(tile):
        rows = pl.ds(pl.multiple_of(tile * plan.row_tile, plan.row_tile), plan.row_tile)
        real, imag = [], []
        for r in range(4):
            cols = pl.ds(r * quarter, quarter)
            left_r, left_i = left[0, rows, cols], left[1, rows, cols]
            right_r, right_i = right[0, rows, cols], right[1, rows, cols]
            if conjugate:
                left_i = -left_i
            pair = (left_r * right_r - left_i * right_i, left_r * right_i + left_i * right_r)
            high, low = split_terms(jnp.concatenate(pair, axis=1))

            def dot(part, table):
                return lax.dot_general(
                    part, table, (((1,), (1,)), ((), ())), preferred_element_type=jnp.float32
                )

            out = dot(high, mix[0, r]) + (dot(low, mix[0, r]) + dot(high, mix[1, r]))
            real.append(out[:, :quarter])
            imag.append(out[:, quarter:])
        sum_r, sum_i = real[0] + real[2], imag[0] + imag[2]
        dif_r, dif_i = real[0] - real[2], imag[0] - imag[2]
        two_r, two_i = real[1] + real[3], imag[1] + imag[3]
        odd_r, odd_i = real[1] - real[3], imag[1] - imag[3]
        turns = (
            (sum_r + two_r, sum_i + two_i),
            (dif_r - odd_i, dif_i + odd_r),
            (sum_r - two_r, sum_i - two_i),
            (dif_r + odd_i, dif_i - odd_r),
        )
        for j, (got_r, got_i) in enumerate(turns):
            cols = pl.ds(j * quarter, quarter)
            cos, sin = turn[0, rows, cols], turn[1, rows, cols]
            mid[0, rows, cols] = got_r * cos - got_i * sin
            mid[1, rows, cols] = got_r * sin + got_i * cos


def inverse_columns(plan, back_even, back_odd, mid, values):
    side, half, quarter = plan.side, plan.half, plan.quarter

    @pl.loop(0, side // quarter)
    def columns(tile):
        cols = pl.ds(pl.multiple_of(tile * quarter, quarter), quarter)
        even = [mid[0, pl.ds(0, plan.evens), cols], mid[1, pl.ds(0, plan.evens), cols]]
        if plan.even_depth > 2 * plan.evens:
            even.append(jnp.zeros((plan.even_depth - 2 * plan.evens, quarter), jnp.float32))
        odd = [mid[0, pl.ds(plan.evens, plan.odds), cols], mid[1, pl.ds(plan.evens, plan.odds), cols]]
        from_even = dot_in(back_even, slice(None), *split_terms(jnp.concatenate(even)))
        from_odd = dot_in(back_odd, slice(None), *split_terms(jnp.concatenate(odd)))
        values[pl.ds(0, half), cols] = from_even + from_odd
        values[pl.ds(half, half), cols] = from_even - from_odd


def filter_kernel(plan, views, count, me, *refs):
    tiles = refs[:count]
    into_even, into_odd, turn, mix, spec, values, mid, sems = refs[count:]
    wait_all(start_all(views(me, tiles, values), sems))
    to_spectrum(plan, values, into_even, into_odd, turn, mix, spec, mid)


def conv_kernel(plan, views, count, me, filt, *refs):
    blocks, tables = refs[:count], refs[count : count + 6]
    into_even, into_odd, back_even, back_odd, turn, mix = tables
    spec, outs = refs[count + 6], refs[count + 7 : 2 * count + 7]
    values, mid, sems = refs[2 * count + 7 :]
    wait_all(start_all(views(me, blocks, values), sems))
    to_spectrum(plan, values, into_even, into_odd, turn, mix, spec, mid)
    inverse_rows(plan, False, filt, spec, turn, mix, mid)
    inverse_columns(plan, back_even, back_odd, mid, values)
    wait_all(start_all(((to, source) for source, to in views(me, outs, values)), sems))


def term_kernel(plan, views, term_views, count, me, gated, *refs):
    blocks, tables = refs[:count], refs[count : count + 6]
    into_even, into_odd, back_even, back_odd, turn, mix = tables
    spec, term, values, mid, sems, term_sems = refs[count + 6 :]
    wait_all(start_all(views(me, blocks, values), sems))
    to_spectrum(plan, values, into_even, into_odd, turn, mix, spec, mid)
    inverse_rows(plan, True, gated, spec, turn, mix, mid)
    inverse_columns(plan, back_even, back_odd, mid, values)
    wait_all(start_all(((to, source) for source, to in term_views(me, [term], values)), term_sems))


def grad_kernel(plan, views, count, me, filt, spec, back_even, back_odd, turn, mix, *refs):
    outs = refs[:count]
    values, mid, sems = refs[count:]
    inverse_rows(plan, True, filt, spec, turn, mix, mid)
    inverse_columns(plan, back_even, back_odd, mid, values)
    wait_all(start_all(((to, source) for source, to in views(me, outs, values)), sems))


def smem():
    return pl.BlockSpec(memory_space=pltpu.SMEM)


def vmem():
    return pl.BlockSpec(memory_space=pltpu.VMEM)


def anywhere():
    return pl.BlockSpec(memory_space=pl.ANY)


def kernel_cost(plan):
    return pl.CostEstimate(flops=plan.side**2, bytes_accessed=plan.side**2, transcendentals=0)


def call_kernel(plan, kernel, name, args, in_specs, out_shape, out_specs, scratch):
    return pl.pallas_call(
        kernel,
        out_shape=out_shape,
        in_specs=in_specs,
        out_specs=out_specs,
        scratch_shapes=scratch,
        compiler_params=pltpu.CompilerParams(vmem_limit_bytes=VMEM_LIMIT),
        cost_estimate=kernel_cost(plan),
        name=name,
    )(*args)


def float_array(shape):
    return jax.ShapeDtypeStruct(shape, jnp.float32)


def filter_spectrum(plan, me, tiles, views, copies):
    shape = (2, plan.rows, plan.side)
    return call_kernel(
        plan,
        functools.partial(filter_kernel, plan, views, len(tiles)),
        "filter_spectrum",
        (me, *tiles, plan.into_even, plan.into_odd, plan.turn, plan.mix),
        [smem()] + [anywhere()] * len(tiles) + [vmem()] * 4,
        float_array(shape),
        vmem(),
        [
            pltpu.VMEM((plan.side, plan.side), jnp.float32),
            pltpu.VMEM(shape, jnp.float32),
            pltpu.SemaphoreType.DMA((copies,)),
        ],
    )


def tables_of(plan):
    return (plan.into_even, plan.into_odd, plan.back_even, plan.back_odd, plan.turn, plan.mix)


def conv_of(plan, me, filt, blocks, views):
    count = len(blocks)
    shape = (2, plan.rows, plan.side)
    spec, *outs = call_kernel(
        plan,
        functools.partial(conv_kernel, plan, views, count),
        "conv_of",
        (me, filt, *blocks, *tables_of(plan)),
        [smem(), vmem()] + [vmem()] * count + [vmem()] * 6,
        [float_array(shape)] + [float_array((plan.side // count, plan.side))] * count,
        [vmem()] * (count + 1),
        [
            pltpu.VMEM((plan.side, plan.side), jnp.float32),
            pltpu.VMEM(shape, jnp.float32),
            pltpu.SemaphoreType.DMA((count,)),
        ],
    )
    return spec, outs


def term_of(plan, me, gated, blocks, views, term_shape, term_views):
    count = len(blocks)
    shape = (2, plan.rows, plan.side)
    return call_kernel(
        plan,
        functools.partial(term_kernel, plan, views, term_views, count),
        "term_of",
        (me, gated, *blocks, *tables_of(plan)),
        [smem(), vmem()] + [vmem()] * count + [vmem()] * 6,
        [float_array(shape), float_array(term_shape)],
        [vmem(), anywhere()],
        [
            pltpu.VMEM((plan.side, plan.side), jnp.float32),
            pltpu.VMEM(shape, jnp.float32),
            pltpu.SemaphoreType.DMA((count,)),
            pltpu.SemaphoreType.DMA((math.prod(term_shape[:2]),)),
        ],
    )


def grad_of(plan, me, filt, spec, count, views):
    return call_kernel(
        plan,
        functools.partial(grad_kernel, plan, views, count),
        "grad_of",
        (me, filt, spec, *tables_of(plan)[2:]),
        [smem()] + [vmem()] * 6,
        [float_array((plan.side // count, plan.side))] * count,
        [vmem()] * count,
        [
            pltpu.VMEM((plan.side, plan.side), jnp.float32),
            pltpu.VMEM((2, plan.rows, plan.side), jnp.float32),
            pltpu.SemaphoreType.DMA((count,)),
        ],
    )


def pairwise(block, axis, step):
    return lax.ppermute(block, axis, [(i, i ^ step) for i in range(lax.axis_size(axis))])


def after(first, then):
    return lax.optimization_barrier((first, then))[1]


def gate_kernel(steps, gates, me, *refs):
    count = len(steps)
    blocks = refs[:count]
    ins = refs[count : count + gates]
    outs, got, sems = refs[-gates - 2 : -2], refs[-2], refs[-1]
    here = pl.program_id(0)

    def copy_of(i):
        return pltpu.make_async_copy(blocks[i], got.at[i], sems.at[i])

    @pl.when(here == 0)
    def start():
        for i in range(count):
            copy_of(i).start()

    for i in range(count):

        @pl.when(here == i)
        def wait():
            copy_of(i).wait()

    values = got[here]
    for gate, out in zip(ins, outs):
        out[0] = (gate[0].astype(jnp.float32) * values).astype(jnp.bfloat16)


def gated_by(me, steps, blocks, gates, done=()):
    count = len(steps)
    shape = gates[0].shape

    def place(i, me):
        step = steps[-1]
        for j in range(count - 1):
            step = jnp.where(i == j, steps[j], step)
        return (me[0] ^ step, 0, 0)

    spec = pl.BlockSpec((1,) + shape[1:], place)
    size = count * shape[1] * shape[2]
    first_done = 1 + count + len(gates)
    return pl.pallas_call(
        functools.partial(gate_kernel, steps, len(gates)),
        grid_spec=pltpu.PrefetchScalarGridSpec(
            num_scalar_prefetch=1,
            grid=(count,),
            in_specs=[anywhere()] * count + [spec] * len(gates) + [anywhere()] * len(done),
            out_specs=[spec] * len(gates),
            scratch_shapes=[
                pltpu.VMEM((count,) + shape[1:], jnp.float32),
                pltpu.SemaphoreType.DMA((count,)),
            ],
        ),
        out_shape=[jax.ShapeDtypeStruct(shape, jnp.bfloat16)] * len(gates),
        input_output_aliases={first_done + i: i for i in range(len(done))},
        compiler_params=pltpu.CompilerParams(vmem_limit_bytes=VMEM_LIMIT),
        cost_estimate=pl.CostEstimate(
            flops=size * len(gates), bytes_accessed=4 * size * (1 + len(gates)), transcendentals=0
        ),
        name="gate_out",
    )(me, *blocks, *gates, *done)


def send_order(owners, cols):
    far = sorted(range(owners // 2, owners), key=lambda s: (-s // cols, -s))
    near = sorted(range(1, owners // 2), key=lambda s: (s % cols, -s))
    return far, near


def channel_shards(outer_gate, inner_gate, signal, grad_out, filter_weight):
    block, side = filter_weight.shape
    plan = Plan(side)
    parts, rows, cols = (lax.axis_size(name) for name in ("dp", "row", "col"))
    owners = rows * cols
    place = own_block()
    me = jnp.reshape(place, (1,)).astype(jnp.int32)
    far, near = send_order(owners, cols)
    order = far[:2]
    for i in range(2, len(far)):
        order = order + near[i - 2 : i - 1] + far[i : i + 1]
    order = order[:-1] + near[len(far) - 2 :] + order[-1:]
    last_order = far + near[:1] + near[2:] + near[1:2]
    by_block = functools.partial(block_views, plan, owners)
    by_tile = functools.partial(tile_views, plan, (parts, rows, cols), False)
    by_row = functools.partial(tile_views, plan, (parts, rows, cols), True)

    def gated_block(left, right, step):
        at = place ^ step
        return lax.dynamic_index_in_dim(left[0], at, 0, False).astype(
            jnp.float32
        ) * lax.dynamic_index_in_dim(right[0], at, 0, False).astype(jnp.float32)

    crossed, neared = [], []

    def exchange(blocks, what, order, deep=3, near_wait=0):
        got = [blocks[0]] + [None] * (owners - 1)
        before, near_before = len(crossed), list(neared)
        neared.clear()
        for step in order:
            mine, waits = blocks[step], []
            if step in far:
                waits = crossed[max(0, len(crossed) - deep - 1) : max(0, len(crossed) - deep + 1)]
                if len(crossed) - before >= len(far) // 2:
                    waits = waits + near_before
            elif before:
                waits = crossed[before - 1 + near_wait : before + near_wait]
            if waits:
                mine = after(waits, mine)
            with jax.named_scope(f"{what}_{step}"):
                got[step] = pairwise(mine, ("row", "col"), step)
            (crossed if step in far else neared).append(got[step])
        return got

    height = block // parts
    own_part = lax.dynamic_slice_in_dim(filter_weight, lax.axis_index("dp") * height, height, 0)
    own_part = own_part * (1.0 / side)
    inner, values = inner_gate, signal
    gated = [None] * owners
    for step in order + [0]:
        gated[step] = gated_block(inner, values, step)
        if step and step % cols == 0:
            gated[step] = jnp.concatenate([gated[step], own_part])
        if step == order[0]:
            inner, values = after(gated[step], [inner_gate, signal])
    gated = exchange(gated, "gated", order)
    over_row = jnp.stack([own_part] + [gated[i * cols][block:] for i in range(1, rows)])
    grad_conv = [gated_block(grad_out, outer_gate, step) for step in range(owners)]
    over_row = after(gated + grad_conv, over_row)
    over_all = [lax.all_gather(over_row, ("dp", "col"))]
    filt = filter_spectrum(plan, me, over_all, by_tile, parts * owners)

    got = exchange(grad_conv, "grad_conv", [step for step in order if step != near[-1]], 4)
    spec, conv_out = conv_of(plan, me, filt, after([filt] + [got[step] for step in far[:1]], gated), by_block)
    with jax.named_scope(f"grad_conv_{near[-1]}"):
        got[near[-1]] = pairwise(after(conv_out[0], grad_conv[near[-1]]), ("row", "col"), near[-1])
    grad_conv = got
    conv = exchange(conv_out, "conv", order, 4)
    tile_shape = (parts * cols, rows, height, side)
    cot, term = term_of(plan, me, spec, grad_conv, by_block, tile_shape, by_row)
    back_out = grad_of(plan, me, filt, cot, owners, by_block)
    grad_gated = exchange(back_out, "grad_gated", last_order, 2, 3)

    term = after([conv[step] for step in far[:2]], term)
    term = lax.psum_scatter(term, ("dp", "col"), scatter_dimension=0, tiled=False)
    total = lax.psum_scatter(term, "row", scatter_dimension=0, tiled=False) * (1.0 / side)
    every = [0] + last_order
    (grad_outer,) = gated_by(me, every, [conv[step] for step in every], [grad_out[0]])
    total = after(grad_outer, total)
    with jax.named_scope("parts_gather"):
        others = [pairwise(total, "dp", i) for i in range(1, parts)]
    pieces = jnp.stack([total] + others)
    bit = 1
    while bit < parts:
        upper = (lax.axis_index("dp") & bit) != 0
        swapped = jnp.flip(pieces.reshape(parts // (2 * bit), 2, bit, height, side), 1)
        pieces = jnp.where(upper, swapped.reshape(pieces.shape), pieces)
        bit *= 2
    grad_filter = pieces.reshape(block, side)

    gates = [signal[0], inner_gate[0]]
    early, late = every[:-1], every[-1:]
    done = gated_by(me, early, [grad_gated[step] for step in early], gates)
    grad_inner, grad_signal = gated_by(me, late, [grad_gated[step] for step in late], gates, done)
    return (grad_outer[None], grad_inner[None], grad_signal[None], grad_filter)


def powers_of_two(*sizes):
    return all(size & (size - 1) == 0 for size in sizes)


def shards(*arrays):
    parts, rows, cols = (lax.axis_size(name) for name in ("dp", "row", "col"))
    side = arrays[0].shape[3]
    whole = arrays[0].shape[1] == rows * cols and rows >= 2 and cols == 2
    fits = powers_of_two(parts, rows, cols, side) and side // 4 % LANE_PAD == 0
    fits = fits and arrays[4].shape[0] // parts % ROW_PAD == 0
    return (channel_shards if whole and fits else spread_shards)(*arrays)


def solution(mesh):
    placed = (
        P("dp", None, ("row", "col"), None),
        P("dp", None, ("row", "col"), None),
        P("dp", None, ("row", "col"), None),
        P("dp", None, ("row", "col"), None),
        P(("row", "col"), None),
    )
    return jax.shard_map(
        shards,
        mesh=mesh,
        in_specs=placed,
        out_specs=(
            P("dp", None, ("row", "col"), None),
            P("dp", None, ("row", "col"), None),
            P("dp", None, ("row", "col"), None),
            P(("row", "col"), None),
        ),
        check_vma=False,
    )
```

```python
import functools
import math

import jax
import jax.numpy as jnp
import numpy as np
from jax import lax
from jax.experimental import pallas as pl
from jax.experimental.pallas import tpu as pltpu
from jax.sharding import PartitionSpec as P

TWO_PI = 2.0 * math.pi


def contract(form, left, right):
    return jnp.einsum(
        form, left, right, precision=lax.Precision.HIGHEST, preferred_element_type=jnp.float32
    )


def redistribute(blocks):
    return lax.all_to_all(blocks, ("row", "col"), split_axis=0, concat_axis=0, tiled=True)


def own_block():
    return lax.axis_index("row") * lax.axis_size("col") + lax.axis_index("col")


def turn_angles(first_index, second_index, total):
    product = first_index * second_index % total
    angles = product.astype(jnp.float32) * (TWO_PI / total)
    return (jnp.cos(angles), jnp.sin(angles))


def axis_dft(real, imag, sign):
    length, width = real.shape
    first = 1 << (length.bit_length() - 1) // 2
    second = length // first
    index_a = jnp.arange(first, dtype=jnp.int32)
    index_b = jnp.arange(second, dtype=jnp.int32)
    cos_a, sin_a = turn_angles(index_a[:, None], index_a[None, :], first)
    sin_a = sign * sin_a
    cos_b, sin_b = turn_angles(index_b[:, None], index_b[None, :], second)
    sin_b = sign * sin_b
    twist_cos, twist_sin = turn_angles(index_a[:, None], index_b[None, :], length)
    twist_cos = twist_cos[:, :, None]
    twist_sin = sign * twist_sin[:, :, None]
    real_three = real.reshape(first, second, width)
    step_real = contract("abm,ak->kbm", real_three, cos_a)
    step_imag = contract("abm,ak->kbm", real_three, sin_a)
    if imag is not None:
        imag_three = imag.reshape(first, second, width)
        step_real = step_real - contract("abm,ak->kbm", imag_three, sin_a)
        step_imag = step_imag + contract("abm,ak->kbm", imag_three, cos_a)
    turned_real = step_real * twist_cos - step_imag * twist_sin
    turned_imag = step_real * twist_sin + step_imag * twist_cos
    out_real = contract("kbm,bj->jkm", turned_real, cos_b) - contract(
        "kbm,bj->jkm", turned_imag, sin_b
    )
    out_imag = contract("kbm,bj->jkm", turned_real, sin_b) + contract(
        "kbm,bj->jkm", turned_imag, cos_b
    )
    return (out_real.reshape(length, width), out_imag.reshape(length, width))


def forward(stacked, order):
    count, block, grid_side = stacked.shape
    owners = grid_side // block
    total = grid_side * grid_side
    send = jnp.transpose(stacked.reshape(count, block, owners, block), (2, 1, 0, 3)).reshape(
        owners, block, count * block
    )
    columns = redistribute(send).reshape(grid_side, count * block)
    first_real, first_imag = axis_dft(columns, None, -1.0)
    first_real = first_real.reshape(grid_side, count, block)
    first_imag = first_imag.reshape(grid_side, count, block)
    col_index = own_block() * block + jnp.arange(block, dtype=jnp.int32)
    cos_turn, sin_turn = turn_angles(order[:, None, None], col_index[None, None, :], total)
    turned_real = first_real * cos_turn + first_imag * sin_turn
    turned_imag = first_imag * cos_turn - first_real * sin_turn
    send_two = jnp.concatenate([turned_real, turned_imag], axis=1).reshape(
        owners, block, 2 * count * block
    )
    gotten = redistribute(send_two).reshape(owners, block, 2 * count, block)
    flat_real = jnp.transpose(gotten[:, :, :count, :], (0, 3, 1, 2)).reshape(
        grid_side, block * count
    )
    flat_imag = jnp.transpose(gotten[:, :, count:, :], (0, 3, 1, 2)).reshape(
        grid_side, block * count
    )
    out_real, out_imag = axis_dft(flat_real, flat_imag, -1.0)
    spec_real = jnp.transpose(out_real.reshape(grid_side, block, count), (1, 2, 0))
    spec_imag = jnp.transpose(out_imag.reshape(grid_side, block, count), (1, 2, 0))
    return (spec_real, spec_imag)


def inverse(spec_real, spec_imag, order):
    block, count, grid_side = spec_real.shape
    owners = grid_side // block
    total = grid_side * grid_side
    flat_real = jnp.transpose(spec_real, (2, 0, 1)).reshape(grid_side, block * count)
    flat_imag = jnp.transpose(spec_imag, (2, 0, 1)).reshape(grid_side, block * count)
    out_real, out_imag = axis_dft(flat_real, flat_imag, 1.0)
    back_real = jnp.transpose(out_real.reshape(owners, block, block, count), (0, 2, 3, 1))
    back_imag = jnp.transpose(out_imag.reshape(owners, block, block, count), (0, 2, 3, 1))
    freq_index = lax.dynamic_slice_in_dim(order, own_block() * block, block, 0)
    col_index = (
        jnp.arange(owners, dtype=jnp.int32)[:, None] * block
        + jnp.arange(block, dtype=jnp.int32)[None, :]
    )
    cos_turn, sin_turn = turn_angles(
        freq_index[None, :, None, None], col_index[:, None, None, :], total
    )
    turned_real = back_real * cos_turn - back_imag * sin_turn
    turned_imag = back_real * sin_turn + back_imag * cos_turn
    send = jnp.concatenate([turned_real, turned_imag], axis=2).reshape(
        owners, block, 2 * count * block
    )
    gotten = redistribute(send).reshape(grid_side, 2 * count * block)
    real_part = gotten[:, : count * block]
    imag_part = gotten[:, count * block :]
    full_real, full_imag = axis_dft(real_part, imag_part, 1.0)
    values = full_real * (1.0 / total)
    returned = redistribute(values.reshape(owners, block, count * block)).reshape(
        owners, block, count, block
    )
    return jnp.transpose(returned, (2, 1, 0, 3)).reshape(count, block, grid_side)


def spread_shards(outer_gate, inner_gate, signal, grad_out, filter_weight):
    grid_side = filter_weight.shape[1]
    freq_index = jnp.arange(grid_side, dtype=jnp.int32)
    outer_f = outer_gate[0].astype(jnp.float32)
    inner_f = inner_gate[0].astype(jnp.float32)
    signal_f = signal[0].astype(jnp.float32)
    grad_f = grad_out[0].astype(jnp.float32)
    channels = inner_f.shape[0]
    gated = inner_f * signal_f
    grad_conv = grad_f * outer_f
    taps = (filter_weight * (1.0 / grid_side))[None]
    spec_real, spec_imag = forward(jnp.concatenate([gated, grad_conv], axis=0), freq_index)
    filt_real, filt_imag = forward(taps, freq_index)
    gated_real = spec_real[:, :channels]
    gated_imag = spec_imag[:, :channels]
    cot_real = spec_real[:, channels : 2 * channels]
    cot_imag = spec_imag[:, channels : 2 * channels]
    conv_real = filt_real * gated_real - filt_imag * gated_imag
    conv_imag = filt_real * gated_imag + filt_imag * gated_real
    back_real = filt_real * cot_real + filt_imag * cot_imag
    back_imag = filt_real * cot_imag - filt_imag * cot_real
    term_real = jnp.sum(gated_real * cot_real + gated_imag * cot_imag, axis=1, keepdims=True)
    term_imag = jnp.sum(gated_real * cot_imag - gated_imag * cot_real, axis=1, keepdims=True)
    values = inverse(
        jnp.concatenate([conv_real, back_real, term_real], axis=1),
        jnp.concatenate([conv_imag, back_imag, term_imag], axis=1),
        freq_index,
    )
    grad_filter = lax.psum(values[2 * channels], "dp") * (1.0 / grid_side)
    conv = values[:channels]
    grad_gated = values[channels : 2 * channels]
    grad_outer = (grad_f * conv).astype(jnp.bfloat16)[None]
    grad_inner = (grad_gated * signal_f).astype(jnp.bfloat16)[None]
    grad_signal = (grad_gated * inner_f).astype(jnp.bfloat16)[None]
    return (grad_outer, grad_inner, grad_signal, grad_filter)


VMEM_LIMIT = 18 * 1024 * 1024
ROW_PAD = 16
LANE_PAD = 128


def up_to(value, unit):
    return -(-value // unit) * unit


def high_low(table):
    high = table.astype(jnp.bfloat16)
    low = (table - high.astype(np.float64)).astype(jnp.bfloat16)
    return np.stack([high, low])


class Plan:
    def __init__(self, side):
        half = side // 2
        self.side, self.half, self.quarter = side, half, side // 4
        self.evens = up_to(half // 2 + 1, ROW_PAD)
        self.odds = half // 2
        self.rows = self.evens + self.odds
        self.even_depth = up_to(2 * self.evens, LANE_PAD)
        total = side * side
        even_k = 2 * np.arange(self.evens)
        odd_k = 2 * np.arange(self.odds) + 1
        live = (even_k <= half).astype(np.float64)
        p = np.arange(half)

        def waves(k, scale):
            angle = 2.0 * np.pi * (k[:, None] * p[None, :] % side) / side
            return np.concatenate([np.cos(angle) * scale[:, None], -np.sin(angle) * scale[:, None]])

        ones = np.ones(self.odds)
        self.into_even = high_low(waves(even_k, live))
        self.into_odd = high_low(waves(odd_k, ones))
        weight = np.where((even_k == 0) | (even_k == half), 1.0, 2.0) * live / total
        back_even = np.zeros((half, self.even_depth))
        back_even[:, : 2 * self.evens] = waves(even_k, weight).T
        self.back_even = high_low(back_even)
        self.back_odd = high_low(waves(odd_k, ones * 2.0 / total).T)
        k = np.concatenate([even_k, odd_k])
        turn = 2.0 * np.pi * (k[:, None] * np.arange(side)[None, :] % total) / total
        self.turn = np.stack([np.cos(turn), np.sin(turn)]).astype(np.float32)
        q = np.arange(self.quarter)
        mixes = []
        for r in range(4):
            angle = 2.0 * np.pi * (q[:, None] * (4 * q[None, :] + r) % side) / side
            cos, sin = np.cos(angle), np.sin(angle)
            mixes.append(np.block([[cos, -sin], [sin, cos]]))
        self.mix = high_low(np.stack(mixes))
        self.row_tile = next(t for t in (176, 264, 16, 8) if self.rows % t == 0)


def split_terms(values):
    high = values.astype(jnp.bfloat16)
    return high, (values - high.astype(jnp.float32)).astype(jnp.bfloat16)


def dot_in(table, rows, high, low):
    dot = functools.partial(jnp.dot, preferred_element_type=jnp.float32)
    first, second = table[0, rows], table[1, rows]
    return dot(first, high) + (dot(first, low) + dot(second, high))


def block_views(plan, owners, me, blocks, values):
    size = plan.side // owners
    for step in range(owners):
        at = pl.multiple_of((me[0] ^ step) * size, size)
        yield blocks[step].at[pl.ds(0, size)], values.at[pl.ds(at, size)]


def tile_views(plan, grid, natural, me, tiles, values):
    parts, rows, cols = grid
    block = plan.side // (rows * cols)
    height = block // parts
    own_row = me[0] // cols
    for part in range(parts):
        for col in range(cols):
            for i in range(rows):
                row = i if natural else own_row ^ i
                at = (row * cols + col) * block + part * height
                at = at if natural else pl.multiple_of(at, height)
                yield tiles[0].at[part * cols + col, i], values.at[pl.ds(at, height)]


def start_all(pairs, sems):
    copies = [pltpu.make_async_copy(source, to, sems.at[i]) for i, (source, to) in enumerate(pairs)]
    for copy in copies:
        copy.start()
    return copies


def wait_all(copies):
    for copy in copies:
        copy.wait()


def to_spectrum(plan, values, into_even, into_odd, turn, mix, spec, mid):
    side, half, quarter = plan.side, plan.half, plan.quarter

    @pl.loop(0, side // quarter)
    def columns(tile):
        cols = pl.ds(pl.multiple_of(tile * quarter, quarter), quarter)
        top, bottom = values[pl.ds(0, half), cols], values[pl.ds(half, half), cols]
        for first, count, table, part in (
            (0, plan.evens, into_even, top + bottom),
            (plan.evens, plan.odds, into_odd, top - bottom),
        ):
            out = dot_in(table, slice(None), *split_terms(part))
            real, imag = out[:count], out[count:]
            rows = pl.ds(first, count)
            cos, sin = turn[0, rows, cols], turn[1, rows, cols]
            mid[0, rows, cols] = real * cos + imag * sin
            mid[1, rows, cols] = imag * cos - real * sin

    @pl.loop(0, plan.rows // plan.row_tile)
    def rows_loop(tile):
        rows = pl.ds(pl.multiple_of(tile * plan.row_tile, plan.row_tile), plan.row_tile)
        real = [mid[0, rows, pl.ds(j * quarter, quarter)] for j in range(4)]
        imag = [mid[1, rows, pl.ds(j * quarter, quarter)] for j in range(4)]
        sum_r, sum_i = real[0] + real[2], imag[0] + imag[2]
        dif_r, dif_i = real[0] - real[2], imag[0] - imag[2]
        two_r, two_i = real[1] + real[3], imag[1] + imag[3]
        odd_r, odd_i = real[1] - real[3], imag[1] - imag[3]
        turns = (
            (sum_r + two_r, sum_i + two_i),
            (dif_r + odd_i, dif_i - odd_r),
            (sum_r - two_r, sum_i - two_i),
            (dif_r - odd_i, dif_i + odd_r),
        )
        dot = functools.partial(jnp.dot, preferred_element_type=jnp.float32)
        for r, pair in enumerate(turns):
            high, low = split_terms(jnp.concatenate(pair, axis=1))
            out = dot(high, mix[0, r]) + (dot(low, mix[0, r]) + dot(high, mix[1, r]))
            cols = pl.ds(r * quarter, quarter)
            spec[0, rows, cols] = out[:, :quarter]
            spec[1, rows, cols] = out[:, quarter:]


def inverse_rows(plan, conjugate, left, right, turn, mix, mid):
    quarter = plan.quarter

    @pl.loop(0, plan.rows // plan.row_tile)
    def rows_loop(tile):
        rows = pl.ds(pl.multiple_of(tile * plan.row_tile, plan.row_tile), plan.row_tile)
        real, imag = [], []
        for r in range(4):
            cols = pl.ds(r * quarter, quarter)
            left_r, left_i = left[0, rows, cols], left[1, rows, cols]
            right_r, right_i = right[0, rows, cols], right[1, rows, cols]
            if conjugate:
                left_i = -left_i
            pair = (left_r * right_r - left_i * right_i, left_r * right_i + left_i * right_r)
            high, low = split_terms(jnp.concatenate(pair, axis=1))

            def dot(part, table):
                return lax.dot_general(
                    part, table, (((1,), (1,)), ((), ())), preferred_element_type=jnp.float32
                )

            out = dot(high, mix[0, r]) + (dot(low, mix[0, r]) + dot(high, mix[1, r]))
            real.append(out[:, :quarter])
            imag.append(out[:, quarter:])
        sum_r, sum_i = real[0] + real[2], imag[0] + imag[2]
        dif_r, dif_i = real[0] - real[2], imag[0] - imag[2]
        two_r, two_i = real[1] + real[3], imag[1] + imag[3]
        odd_r, odd_i = real[1] - real[3], imag[1] - imag[3]
        turns = (
            (sum_r + two_r, sum_i + two_i),
            (dif_r - odd_i, dif_i + odd_r),
            (sum_r - two_r, sum_i - two_i),
            (dif_r + odd_i, dif_i - odd_r),
        )
        for j, (got_r, got_i) in enumerate(turns):
            cols = pl.ds(j * quarter, quarter)
            cos, sin = turn[0, rows, cols], turn[1, rows, cols]
            mid[0, rows, cols] = got_r * cos - got_i * sin
            mid[1, rows, cols] = got_r * sin + got_i * cos


def inverse_columns(plan, back_even, back_odd, mid, values):
    side, half, quarter = plan.side, plan.half, plan.quarter

    @pl.loop(0, side // quarter)
    def columns(tile):
        cols = pl.ds(pl.multiple_of(tile * quarter, quarter), quarter)
        even = [mid[0, pl.ds(0, plan.evens), cols], mid[1, pl.ds(0, plan.evens), cols]]
        if plan.even_depth > 2 * plan.evens:
            even.append(jnp.zeros((plan.even_depth - 2 * plan.evens, quarter), jnp.float32))
        odd = [mid[0, pl.ds(plan.evens, plan.odds), cols], mid[1, pl.ds(plan.evens, plan.odds), cols]]
        from_even = dot_in(back_even, slice(None), *split_terms(jnp.concatenate(even)))
        from_odd = dot_in(back_odd, slice(None), *split_terms(jnp.concatenate(odd)))
        values[pl.ds(0, half), cols] = from_even + from_odd
        values[pl.ds(half, half), cols] = from_even - from_odd


def filter_kernel(plan, views, count, me, *refs):
    tiles = refs[:count]
    into_even, into_odd, turn, mix, spec, values, mid, sems = refs[count:]
    wait_all(start_all(views(me, tiles, values), sems))
    to_spectrum(plan, values, into_even, into_odd, turn, mix, spec, mid)


def conv_kernel(plan, views, count, me, filt, *refs):
    blocks, tables = refs[:count], refs[count : count + 6]
    into_even, into_odd, back_even, back_odd, turn, mix = tables
    spec, outs = refs[count + 6], refs[count + 7 : 2 * count + 7]
    values, mid, sems = refs[2 * count + 7 :]
    wait_all(start_all(views(me, blocks, values), sems))
    to_spectrum(plan, values, into_even, into_odd, turn, mix, spec, mid)
    inverse_rows(plan, False, filt, spec, turn, mix, mid)
    inverse_columns(plan, back_even, back_odd, mid, values)
    wait_all(start_all(((to, source) for source, to in views(me, outs, values)), sems))


def term_kernel(plan, views, term_views, count, me, gated, *refs):
    blocks, tables = refs[:count], refs[count : count + 6]
    into_even, into_odd, back_even, back_odd, turn, mix = tables
    spec, term, values, mid, sems, term_sems = refs[count + 6 :]
    wait_all(start_all(views(me, blocks, values), sems))
    to_spectrum(plan, values, into_even, into_odd, turn, mix, spec, mid)
    inverse_rows(plan, True, gated, spec, turn, mix, mid)
    inverse_columns(plan, back_even, back_odd, mid, values)
    wait_all(start_all(((to, source) for source, to in term_views(me, [term], values)), term_sems))


def grad_kernel(plan, views, count, me, filt, spec, back_even, back_odd, turn, mix, *refs):
    outs = refs[:count]
    values, mid, sems = refs[count:]
    inverse_rows(plan, True, filt, spec, turn, mix, mid)
    inverse_columns(plan, back_even, back_odd, mid, values)
    wait_all(start_all(((to, source) for source, to in views(me, outs, values)), sems))


def smem():
    return pl.BlockSpec(memory_space=pltpu.SMEM)


def vmem():
    return pl.BlockSpec(memory_space=pltpu.VMEM)


def anywhere():
    return pl.BlockSpec(memory_space=pl.ANY)


def kernel_cost(plan):
    return pl.CostEstimate(flops=plan.side**2, bytes_accessed=plan.side**2, transcendentals=0)


def call_kernel(plan, kernel, name, args, in_specs, out_shape, out_specs, scratch):
    return pl.pallas_call(
        kernel,
        out_shape=out_shape,
        in_specs=in_specs,
        out_specs=out_specs,
        scratch_shapes=scratch,
        compiler_params=pltpu.CompilerParams(vmem_limit_bytes=VMEM_LIMIT),
        cost_estimate=kernel_cost(plan),
        name=name,
    )(*args)


def float_array(shape):
    return jax.ShapeDtypeStruct(shape, jnp.float32)


def filter_spectrum(plan, me, tiles, views, copies):
    shape = (2, plan.rows, plan.side)
    return call_kernel(
        plan,
        functools.partial(filter_kernel, plan, views, len(tiles)),
        "filter_spectrum",
        (me, *tiles, plan.into_even, plan.into_odd, plan.turn, plan.mix),
        [smem()] + [anywhere()] * len(tiles) + [vmem()] * 4,
        float_array(shape),
        vmem(),
        [
            pltpu.VMEM((plan.side, plan.side), jnp.float32),
            pltpu.VMEM(shape, jnp.float32),
            pltpu.SemaphoreType.DMA((copies,)),
        ],
    )


def tables_of(plan):
    return (plan.into_even, plan.into_odd, plan.back_even, plan.back_odd, plan.turn, plan.mix)


def conv_of(plan, me, filt, blocks, views):
    count = len(blocks)
    shape = (2, plan.rows, plan.side)
    spec, *outs = call_kernel(
        plan,
        functools.partial(conv_kernel, plan, views, count),
        "conv_of",
        (me, filt, *blocks, *tables_of(plan)),
        [smem(), vmem()] + [vmem()] * count + [vmem()] * 6,
        [float_array(shape)] + [float_array((plan.side // count, plan.side))] * count,
        [vmem()] * (count + 1),
        [
            pltpu.VMEM((plan.side, plan.side), jnp.float32),
            pltpu.VMEM(shape, jnp.float32),
            pltpu.SemaphoreType.DMA((count,)),
        ],
    )
    return spec, outs


def term_of(plan, me, gated, blocks, views, term_shape, term_views):
    count = len(blocks)
    shape = (2, plan.rows, plan.side)
    return call_kernel(
        plan,
        functools.partial(term_kernel, plan, views, term_views, count),
        "term_of",
        (me, gated, *blocks, *tables_of(plan)),
        [smem(), vmem()] + [vmem()] * count + [vmem()] * 6,
        [float_array(shape), float_array(term_shape)],
        [vmem(), anywhere()],
        [
            pltpu.VMEM((plan.side, plan.side), jnp.float32),
            pltpu.VMEM(shape, jnp.float32),
            pltpu.SemaphoreType.DMA((count,)),
            pltpu.SemaphoreType.DMA((math.prod(term_shape[:2]),)),
        ],
    )


def grad_of(plan, me, filt, spec, count, views):
    return call_kernel(
        plan,
        functools.partial(grad_kernel, plan, views, count),
        "grad_of",
        (me, filt, spec, *tables_of(plan)[2:]),
        [smem()] + [vmem()] * 6,
        [float_array((plan.side // count, plan.side))] * count,
        [vmem()] * count,
        [
            pltpu.VMEM((plan.side, plan.side), jnp.float32),
            pltpu.VMEM((2, plan.rows, plan.side), jnp.float32),
            pltpu.SemaphoreType.DMA((count,)),
        ],
    )


def pairwise(block, axis, step):
    return lax.ppermute(block, axis, [(i, i ^ step) for i in range(lax.axis_size(axis))])


def after(first, then):
    return lax.optimization_barrier((first, then))[1]


def gate_kernel(steps, gates, me, *refs):
    count = len(steps)
    blocks = refs[:count]
    ins = refs[count : count + gates]
    outs, got, sems = refs[-gates - 2 : -2], refs[-2], refs[-1]
    here = pl.program_id(0)

    def copy_of(i):
        return pltpu.make_async_copy(blocks[i], got.at[i], sems.at[i])

    @pl.when(here == 0)
    def start():
        for i in range(count):
            copy_of(i).start()

    for i in range(count):

        @pl.when(here == i)
        def wait():
            copy_of(i).wait()

    values = got[here]
    for gate, out in zip(ins, outs):
        out[0] = (gate[0].astype(jnp.float32) * values).astype(jnp.bfloat16)


def gated_by(me, steps, blocks, gates, done=()):
    count = len(steps)
    shape = gates[0].shape

    def place(i, me):
        step = steps[-1]
        for j in range(count - 1):
            step = jnp.where(i == j, steps[j], step)
        return (me[0] ^ step, 0, 0)

    spec = pl.BlockSpec((1,) + shape[1:], place)
    size = count * shape[1] * shape[2]
    first_done = 1 + count + len(gates)
    return pl.pallas_call(
        functools.partial(gate_kernel, steps, len(gates)),
        grid_spec=pltpu.PrefetchScalarGridSpec(
            num_scalar_prefetch=1,
            grid=(count,),
            in_specs=[anywhere()] * count + [spec] * len(gates) + [anywhere()] * len(done),
            out_specs=[spec] * len(gates),
            scratch_shapes=[
                pltpu.VMEM((count,) + shape[1:], jnp.float32),
                pltpu.SemaphoreType.DMA((count,)),
            ],
        ),
        out_shape=[jax.ShapeDtypeStruct(shape, jnp.bfloat16)] * len(gates),
        input_output_aliases={first_done + i: i for i in range(len(done))},
        compiler_params=pltpu.CompilerParams(vmem_limit_bytes=VMEM_LIMIT),
        cost_estimate=pl.CostEstimate(
            flops=size * len(gates), bytes_accessed=4 * size * (1 + len(gates)), transcendentals=0
        ),
        name="gate_out",
    )(me, *blocks, *gates, *done)


def send_order(owners, cols):
    far = sorted(range(owners // 2, owners), key=lambda s: (-s // cols, -s))
    near = sorted(range(1, owners // 2), key=lambda s: (s % cols, -s))
    return far, near


def channel_shards(outer_gate, inner_gate, signal, grad_out, filter_weight):
    block, side = filter_weight.shape
    plan = Plan(side)
    parts, rows, cols = (lax.axis_size(name) for name in ("dp", "row", "col"))
    owners = rows * cols
    place = own_block()
    me = jnp.reshape(place, (1,)).astype(jnp.int32)
    far, near = send_order(owners, cols)
    order = far[:2]
    for i in range(2, len(far)):
        order = order + near[i - 2 : i - 1] + far[i : i + 1]
    order = order[:-1] + near[len(far) - 2 :] + order[-1:]
    last_order = far[:-1] + near + far[-1:]
    by_block = functools.partial(block_views, plan, owners)
    by_tile = functools.partial(tile_views, plan, (parts, rows, cols), False)
    by_row = functools.partial(tile_views, plan, (parts, rows, cols), True)

    def gated_block(left, right, step):
        at = place ^ step
        return lax.dynamic_index_in_dim(left[0], at, 0, False).astype(
            jnp.float32
        ) * lax.dynamic_index_in_dim(right[0], at, 0, False).astype(jnp.float32)

    crossed, neared = [], []

    def exchange(blocks, what, order, deep=3, near_wait=0):
        got = [blocks[0]] + [None] * (owners - 1)
        before, near_before = len(crossed), list(neared)
        neared.clear()
        for step in order:
            mine, waits = blocks[step], []
            if step in far:
                waits = crossed[max(0, len(crossed) - deep - 1) : max(0, len(crossed) - deep + 1)]
                if len(crossed) - before >= len(far) // 2:
                    waits = waits + near_before
            elif before:
                waits = crossed[before - 1 + near_wait : before + near_wait]
            if waits:
                mine = after(waits, mine)
            with jax.named_scope(f"{what}_{step}"):
                got[step] = pairwise(mine, ("row", "col"), step)
            (crossed if step in far else neared).append(got[step])
        return got

    height = block // parts
    own_part = lax.dynamic_slice_in_dim(filter_weight, lax.axis_index("dp") * height, height, 0)
    own_part = own_part * (1.0 / side)
    inner, values = inner_gate, signal
    gated = [None] * owners
    for step in order + [0]:
        gated[step] = gated_block(inner, values, step)
        if step and step % cols == 0:
            gated[step] = jnp.concatenate([gated[step], own_part])
        if step == order[0]:
            inner, values = after(gated[step], [inner_gate, signal])
    gated = exchange(gated, "gated", order)
    over_row = jnp.stack([own_part] + [gated[i * cols][block:] for i in range(1, rows)])
    grad_conv = [gated_block(grad_out, outer_gate, step) for step in range(owners)]
    over_row = after(gated + grad_conv, over_row)
    over_all = [lax.all_gather(over_row, ("dp", "col"))]
    filt = filter_spectrum(plan, me, over_all, by_tile, parts * owners)

    got = exchange(grad_conv, "grad_conv", [step for step in order if step != near[-1]], 4)
    spec, conv_out = conv_of(plan, me, filt, after([filt] + [got[step] for step in far[:1]], gated), by_block)
    with jax.named_scope(f"grad_conv_{near[-1]}"):
        got[near[-1]] = pairwise(after(conv_out[0], grad_conv[near[-1]]), ("row", "col"), near[-1])
    grad_conv = got
    conv = exchange(conv_out, "conv", order, 4)
    tile_shape = (parts * cols, rows, height, side)
    cot, term = term_of(plan, me, spec, grad_conv, by_block, tile_shape, by_row)
    back_out = grad_of(plan, me, filt, cot, owners, by_block)
    grad_gated = exchange(back_out, "grad_gated", [step for step in last_order if step != near[-1]], 3, 2)
    every = [0] + order
    (grad_outer,) = gated_by(me, every, [conv[step] for step in every], [grad_out[0]])

    term = after([conv[step] for step in far[:2]], term)
    term = lax.psum_scatter(term, ("dp", "col"), scatter_dimension=0, tiled=False)
    term = after([grad_outer] + [grad_gated[step] for step in far[:1]], term)
    total = lax.psum_scatter(term, "row", scatter_dimension=0, tiled=False) * (1.0 / side)
    with jax.named_scope("parts_gather"):
        others = [pairwise(total, "dp", i) for i in range(1, parts)]
    pieces = jnp.stack([total] + others)
    bit = 1
    while bit < parts:
        upper = (lax.axis_index("dp") & bit) != 0
        swapped = jnp.flip(pieces.reshape(parts // (2 * bit), 2, bit, height, side), 1)
        pieces = jnp.where(upper, swapped.reshape(pieces.shape), pieces)
        bit *= 2
    grad_filter = pieces.reshape(block, side)
    with jax.named_scope(f"grad_gated_{near[-1]}"):
        grad_gated[near[-1]] = pairwise(back_out[near[-1]], ("row", "col"), near[-1])

    every = [0] + near + far
    gates = [signal[0], inner_gate[0]]
    early, late = every[:-1], every[-1:]
    done = gated_by(me, early, [grad_gated[step] for step in early], gates)
    grad_inner, grad_signal = gated_by(me, late, [grad_gated[step] for step in late], gates, done)
    return (grad_outer[None], grad_inner[None], grad_signal[None], grad_filter)


def powers_of_two(*sizes):
    return all(size & (size - 1) == 0 for size in sizes)


def shards(*arrays):
    parts, rows, cols = (lax.axis_size(name) for name in ("dp", "row", "col"))
    side = arrays[0].shape[3]
    whole = arrays[0].shape[1] == rows * cols and rows >= 2 and cols == 2
    fits = powers_of_two(parts, rows, cols, side) and side // 4 % LANE_PAD == 0
    fits = fits and arrays[4].shape[0] // parts % ROW_PAD == 0
    return (channel_shards if whole and fits else spread_shards)(*arrays)


def solution(mesh):
    placed = (
        P("dp", None, ("row", "col"), None),
        P("dp", None, ("row", "col"), None),
        P("dp", None, ("row", "col"), None),
        P("dp", None, ("row", "col"), None),
        P(("row", "col"), None),
    )
    return jax.shard_map(
        shards,
        mesh=mesh,
        in_specs=placed,
        out_specs=(
            P("dp", None, ("row", "col"), None),
            P("dp", None, ("row", "col"), None),
            P("dp", None, ("row", "col"), None),
            P(("row", "col"), None),
        ),
        check_vma=False,
    )
```

```python
import functools
import math

import jax
import jax.numpy as jnp
import numpy as np
from jax import lax
from jax.experimental import pallas as pl
from jax.experimental.pallas import tpu as pltpu
from jax.sharding import PartitionSpec as P

TWO_PI = 2.0 * math.pi


def contract(form, left, right):
    return jnp.einsum(
        form, left, right, precision=lax.Precision.HIGHEST, preferred_element_type=jnp.float32
    )


def redistribute(blocks):
    return lax.all_to_all(blocks, ("row", "col"), split_axis=0, concat_axis=0, tiled=True)


def own_block():
    return lax.axis_index("row") * lax.axis_size("col") + lax.axis_index("col")


def turn_angles(first_index, second_index, total):
    product = first_index * second_index % total
    angles = product.astype(jnp.float32) * (TWO_PI / total)
    return (jnp.cos(angles), jnp.sin(angles))


def axis_dft(real, imag, sign):
    length, width = real.shape
    first = 1 << (length.bit_length() - 1) // 2
    second = length // first
    index_a = jnp.arange(first, dtype=jnp.int32)
    index_b = jnp.arange(second, dtype=jnp.int32)
    cos_a, sin_a = turn_angles(index_a[:, None], index_a[None, :], first)
    sin_a = sign * sin_a
    cos_b, sin_b = turn_angles(index_b[:, None], index_b[None, :], second)
    sin_b = sign * sin_b
    twist_cos, twist_sin = turn_angles(index_a[:, None], index_b[None, :], length)
    twist_cos = twist_cos[:, :, None]
    twist_sin = sign * twist_sin[:, :, None]
    real_three = real.reshape(first, second, width)
    step_real = contract("abm,ak->kbm", real_three, cos_a)
    step_imag = contract("abm,ak->kbm", real_three, sin_a)
    if imag is not None:
        imag_three = imag.reshape(first, second, width)
        step_real = step_real - contract("abm,ak->kbm", imag_three, sin_a)
        step_imag = step_imag + contract("abm,ak->kbm", imag_three, cos_a)
    turned_real = step_real * twist_cos - step_imag * twist_sin
    turned_imag = step_real * twist_sin + step_imag * twist_cos
    out_real = contract("kbm,bj->jkm", turned_real, cos_b) - contract(
        "kbm,bj->jkm", turned_imag, sin_b
    )
    out_imag = contract("kbm,bj->jkm", turned_real, sin_b) + contract(
        "kbm,bj->jkm", turned_imag, cos_b
    )
    return (out_real.reshape(length, width), out_imag.reshape(length, width))


def forward(stacked, order):
    count, block, grid_side = stacked.shape
    owners = grid_side // block
    total = grid_side * grid_side
    send = jnp.transpose(stacked.reshape(count, block, owners, block), (2, 1, 0, 3)).reshape(
        owners, block, count * block
    )
    columns = redistribute(send).reshape(grid_side, count * block)
    first_real, first_imag = axis_dft(columns, None, -1.0)
    first_real = first_real.reshape(grid_side, count, block)
    first_imag = first_imag.reshape(grid_side, count, block)
    col_index = own_block() * block + jnp.arange(block, dtype=jnp.int32)
    cos_turn, sin_turn = turn_angles(order[:, None, None], col_index[None, None, :], total)
    turned_real = first_real * cos_turn + first_imag * sin_turn
    turned_imag = first_imag * cos_turn - first_real * sin_turn
    send_two = jnp.concatenate([turned_real, turned_imag], axis=1).reshape(
        owners, block, 2 * count * block
    )
    gotten = redistribute(send_two).reshape(owners, block, 2 * count, block)
    flat_real = jnp.transpose(gotten[:, :, :count, :], (0, 3, 1, 2)).reshape(
        grid_side, block * count
    )
    flat_imag = jnp.transpose(gotten[:, :, count:, :], (0, 3, 1, 2)).reshape(
        grid_side, block * count
    )
    out_real, out_imag = axis_dft(flat_real, flat_imag, -1.0)
    spec_real = jnp.transpose(out_real.reshape(grid_side, block, count), (1, 2, 0))
    spec_imag = jnp.transpose(out_imag.reshape(grid_side, block, count), (1, 2, 0))
    return (spec_real, spec_imag)


def inverse(spec_real, spec_imag, order):
    block, count, grid_side = spec_real.shape
    owners = grid_side // block
    total = grid_side * grid_side
    flat_real = jnp.transpose(spec_real, (2, 0, 1)).reshape(grid_side, block * count)
    flat_imag = jnp.transpose(spec_imag, (2, 0, 1)).reshape(grid_side, block * count)
    out_real, out_imag = axis_dft(flat_real, flat_imag, 1.0)
    back_real = jnp.transpose(out_real.reshape(owners, block, block, count), (0, 2, 3, 1))
    back_imag = jnp.transpose(out_imag.reshape(owners, block, block, count), (0, 2, 3, 1))
    freq_index = lax.dynamic_slice_in_dim(order, own_block() * block, block, 0)
    col_index = (
        jnp.arange(owners, dtype=jnp.int32)[:, None] * block
        + jnp.arange(block, dtype=jnp.int32)[None, :]
    )
    cos_turn, sin_turn = turn_angles(
        freq_index[None, :, None, None], col_index[:, None, None, :], total
    )
    turned_real = back_real * cos_turn - back_imag * sin_turn
    turned_imag = back_real * sin_turn + back_imag * cos_turn
    send = jnp.concatenate([turned_real, turned_imag], axis=2).reshape(
        owners, block, 2 * count * block
    )
    gotten = redistribute(send).reshape(grid_side, 2 * count * block)
    real_part = gotten[:, : count * block]
    imag_part = gotten[:, count * block :]
    full_real, full_imag = axis_dft(real_part, imag_part, 1.0)
    values = full_real * (1.0 / total)
    returned = redistribute(values.reshape(owners, block, count * block)).reshape(
        owners, block, count, block
    )
    return jnp.transpose(returned, (2, 1, 0, 3)).reshape(count, block, grid_side)


def spread_shards(outer_gate, inner_gate, signal, grad_out, filter_weight):
    grid_side = filter_weight.shape[1]
    freq_index = jnp.arange(grid_side, dtype=jnp.int32)
    outer_f = outer_gate[0].astype(jnp.float32)
    inner_f = inner_gate[0].astype(jnp.float32)
    signal_f = signal[0].astype(jnp.float32)
    grad_f = grad_out[0].astype(jnp.float32)
    channels = inner_f.shape[0]
    gated = inner_f * signal_f
    grad_conv = grad_f * outer_f
    taps = (filter_weight * (1.0 / grid_side))[None]
    spec_real, spec_imag = forward(jnp.concatenate([gated, grad_conv], axis=0), freq_index)
    filt_real, filt_imag = forward(taps, freq_index)
    gated_real = spec_real[:, :channels]
    gated_imag = spec_imag[:, :channels]
    cot_real = spec_real[:, channels : 2 * channels]
    cot_imag = spec_imag[:, channels : 2 * channels]
    conv_real = filt_real * gated_real - filt_imag * gated_imag
    conv_imag = filt_real * gated_imag + filt_imag * gated_real
    back_real = filt_real * cot_real + filt_imag * cot_imag
    back_imag = filt_real * cot_imag - filt_imag * cot_real
    term_real = jnp.sum(gated_real * cot_real + gated_imag * cot_imag, axis=1, keepdims=True)
    term_imag = jnp.sum(gated_real * cot_imag - gated_imag * cot_real, axis=1, keepdims=True)
    values = inverse(
        jnp.concatenate([conv_real, back_real, term_real], axis=1),
        jnp.concatenate([conv_imag, back_imag, term_imag], axis=1),
        freq_index,
    )
    grad_filter = lax.psum(values[2 * channels], "dp") * (1.0 / grid_side)
    conv = values[:channels]
    grad_gated = values[channels : 2 * channels]
    grad_outer = (grad_f * conv).astype(jnp.bfloat16)[None]
    grad_inner = (grad_gated * signal_f).astype(jnp.bfloat16)[None]
    grad_signal = (grad_gated * inner_f).astype(jnp.bfloat16)[None]
    return (grad_outer, grad_inner, grad_signal, grad_filter)


VMEM_LIMIT = 18 * 1024 * 1024
ROW_PAD = 16
LANE_PAD = 128


def up_to(value, unit):
    return -(-value // unit) * unit


def high_low(table):
    high = table.astype(jnp.bfloat16)
    low = (table - high.astype(np.float64)).astype(jnp.bfloat16)
    return np.stack([high, low])


class Plan:
    def __init__(self, side):
        half = side // 2
        self.side, self.half, self.quarter = side, half, side // 4
        self.evens = up_to(half // 2 + 1, ROW_PAD)
        self.odds = half // 2
        self.rows = self.evens + self.odds
        self.even_depth = up_to(2 * self.evens, LANE_PAD)
        total = side * side
        even_k = 2 * np.arange(self.evens)
        odd_k = 2 * np.arange(self.odds) + 1
        live = (even_k <= half).astype(np.float64)
        p = np.arange(half)

        def waves(k, scale):
            angle = 2.0 * np.pi * (k[:, None] * p[None, :] % side) / side
            return np.concatenate([np.cos(angle) * scale[:, None], -np.sin(angle) * scale[:, None]])

        ones = np.ones(self.odds)
        self.into_even = high_low(waves(even_k, live))
        self.into_odd = high_low(waves(odd_k, ones))
        weight = np.where((even_k == 0) | (even_k == half), 1.0, 2.0) * live / total
        back_even = np.zeros((half, self.even_depth))
        back_even[:, : 2 * self.evens] = waves(even_k, weight).T
        self.back_even = high_low(back_even)
        self.back_odd = high_low(waves(odd_k, ones * 2.0 / total).T)
        k = np.concatenate([even_k, odd_k])
        turn = 2.0 * np.pi * (k[:, None] * np.arange(side)[None, :] % total) / total
        self.turn = np.stack([np.cos(turn), np.sin(turn)]).astype(np.float32)
        q = np.arange(self.quarter)
        mixes = []
        for r in range(4):
            angle = 2.0 * np.pi * (q[:, None] * (4 * q[None, :] + r) % side) / side
            cos, sin = np.cos(angle), np.sin(angle)
            mixes.append(np.block([[cos, -sin], [sin, cos]]))
        self.mix = high_low(np.stack(mixes))
        self.row_tile = next(t for t in (176, 264, 16, 8) if self.rows % t == 0)


def split_terms(values):
    high = values.astype(jnp.bfloat16)
    return high, (values - high.astype(jnp.float32)).astype(jnp.bfloat16)


def dot_in(table, rows, high, low):
    dot = functools.partial(jnp.dot, preferred_element_type=jnp.float32)
    first, second = table[0, rows], table[1, rows]
    return dot(first, high) + (dot(first, low) + dot(second, high))


def block_views(plan, owners, me, blocks, values):
    size = plan.side // owners
    for step in range(owners):
        at = pl.multiple_of((me[0] ^ step) * size, size)
        yield blocks[step].at[pl.ds(0, size)], values.at[pl.ds(at, size)]


def tile_views(plan, grid, me, tiles, values):
    parts, rows, cols = grid
    block = plan.side // (rows * cols)
    height = block // parts
    own_row = me[0] // cols
    for part in range(parts):
        for col in range(cols):
            for i in range(rows):
                at = ((own_row ^ i) * cols + col) * block + part * height
                yield tiles[0].at[part * cols + col, i], values.at[pl.ds(pl.multiple_of(at, height), height)]


def start_all(pairs, sems):
    copies = [pltpu.make_async_copy(source, to, sems.at[i]) for i, (source, to) in enumerate(pairs)]
    for copy in copies:
        copy.start()
    return copies


def wait_all(copies):
    for copy in copies:
        copy.wait()


def to_spectrum(plan, values, into_even, into_odd, turn, mix, spec, mid):
    side, half, quarter = plan.side, plan.half, plan.quarter

    @pl.loop(0, side // quarter)
    def columns(tile):
        cols = pl.ds(pl.multiple_of(tile * quarter, quarter), quarter)
        top, bottom = values[pl.ds(0, half), cols], values[pl.ds(half, half), cols]
        for first, count, table, part in (
            (0, plan.evens, into_even, top + bottom),
            (plan.evens, plan.odds, into_odd, top - bottom),
        ):
            out = dot_in(table, slice(None), *split_terms(part))
            real, imag = out[:count], out[count:]
            rows = pl.ds(first, count)
            cos, sin = turn[0, rows, cols], turn[1, rows, cols]
            mid[0, rows, cols] = real * cos + imag * sin
            mid[1, rows, cols] = imag * cos - real * sin

    @pl.loop(0, plan.rows // plan.row_tile)
    def rows_loop(tile):
        rows = pl.ds(pl.multiple_of(tile * plan.row_tile, plan.row_tile), plan.row_tile)
        real = [mid[0, rows, pl.ds(j * quarter, quarter)] for j in range(4)]
        imag = [mid[1, rows, pl.ds(j * quarter, quarter)] for j in range(4)]
        sum_r, sum_i = real[0] + real[2], imag[0] + imag[2]
        dif_r, dif_i = real[0] - real[2], imag[0] - imag[2]
        two_r, two_i = real[1] + real[3], imag[1] + imag[3]
        odd_r, odd_i = real[1] - real[3], imag[1] - imag[3]
        turns = (
            (sum_r + two_r, sum_i + two_i),
            (dif_r + odd_i, dif_i - odd_r),
            (sum_r - two_r, sum_i - two_i),
            (dif_r - odd_i, dif_i + odd_r),
        )
        dot = functools.partial(jnp.dot, preferred_element_type=jnp.float32)
        for r, pair in enumerate(turns):
            high, low = split_terms(jnp.concatenate(pair, axis=1))
            out = dot(high, mix[0, r]) + (dot(low, mix[0, r]) + dot(high, mix[1, r]))
            cols = pl.ds(r * quarter, quarter)
            spec[0, rows, cols] = out[:, :quarter]
            spec[1, rows, cols] = out[:, quarter:]


def inverse_rows(plan, conjugate, left, right, turn, mix, mid):
    quarter = plan.quarter

    @pl.loop(0, plan.rows // plan.row_tile)
    def rows_loop(tile):
        rows = pl.ds(pl.multiple_of(tile * plan.row_tile, plan.row_tile), plan.row_tile)
        real, imag = [], []
        for r in range(4):
            cols = pl.ds(r * quarter, quarter)
            left_r, left_i = left[0, rows, cols], left[1, rows, cols]
            right_r, right_i = right[0, rows, cols], right[1, rows, cols]
            if conjugate:
                left_i = -left_i
            pair = (left_r * right_r - left_i * right_i, left_r * right_i + left_i * right_r)
            high, low = split_terms(jnp.concatenate(pair, axis=1))

            def dot(part, table):
                return lax.dot_general(
                    part, table, (((1,), (1,)), ((), ())), preferred_element_type=jnp.float32
                )

            out = dot(high, mix[0, r]) + (dot(low, mix[0, r]) + dot(high, mix[1, r]))
            real.append(out[:, :quarter])
            imag.append(out[:, quarter:])
        sum_r, sum_i = real[0] + real[2], imag[0] + imag[2]
        dif_r, dif_i = real[0] - real[2], imag[0] - imag[2]
        two_r, two_i = real[1] + real[3], imag[1] + imag[3]
        odd_r, odd_i = real[1] - real[3], imag[1] - imag[3]
        turns = (
            (sum_r + two_r, sum_i + two_i),
            (dif_r - odd_i, dif_i + odd_r),
            (sum_r - two_r, sum_i - two_i),
            (dif_r + odd_i, dif_i - odd_r),
        )
        for j, (got_r, got_i) in enumerate(turns):
            cols = pl.ds(j * quarter, quarter)
            cos, sin = turn[0, rows, cols], turn[1, rows, cols]
            mid[0, rows, cols] = got_r * cos - got_i * sin
            mid[1, rows, cols] = got_r * sin + got_i * cos


def inverse_columns(plan, back_even, back_odd, mid, values):
    side, half, quarter = plan.side, plan.half, plan.quarter

    @pl.loop(0, side // quarter)
    def columns(tile):
        cols = pl.ds(pl.multiple_of(tile * quarter, quarter), quarter)
        even = [mid[0, pl.ds(0, plan.evens), cols], mid[1, pl.ds(0, plan.evens), cols]]
        if plan.even_depth > 2 * plan.evens:
            even.append(jnp.zeros((plan.even_depth - 2 * plan.evens, quarter), jnp.float32))
        odd = [mid[0, pl.ds(plan.evens, plan.odds), cols], mid[1, pl.ds(plan.evens, plan.odds), cols]]
        from_even = dot_in(back_even, slice(None), *split_terms(jnp.concatenate(even)))
        from_odd = dot_in(back_odd, slice(None), *split_terms(jnp.concatenate(odd)))
        values[pl.ds(0, half), cols] = from_even + from_odd
        values[pl.ds(half, half), cols] = from_even - from_odd


def filter_kernel(plan, views, count, me, *refs):
    tiles = refs[:count]
    into_even, into_odd, turn, mix, spec, values, mid, sems = refs[count:]
    wait_all(start_all(views(me, tiles, values), sems))
    to_spectrum(plan, values, into_even, into_odd, turn, mix, spec, mid)


def conv_kernel(plan, views, count, me, filt, *refs):
    blocks, tables = refs[:count], refs[count : count + 6]
    into_even, into_odd, back_even, back_odd, turn, mix = tables
    spec, outs = refs[count + 6], refs[count + 7 : 2 * count + 7]
    values, mid, sems = refs[2 * count + 7 :]
    wait_all(start_all(views(me, blocks, values), sems))
    to_spectrum(plan, values, into_even, into_odd, turn, mix, spec, mid)
    inverse_rows(plan, False, filt, spec, turn, mix, mid)
    inverse_columns(plan, back_even, back_odd, mid, values)
    wait_all(start_all(((to, source) for source, to in views(me, outs, values)), sems))


def term_kernel(plan, views, term_views, count, me, gated, *refs):
    blocks, tables = refs[:count], refs[count : count + 6]
    into_even, into_odd, back_even, back_odd, turn, mix = tables
    spec, term, values, mid, sems, term_sems = refs[count + 6 :]
    wait_all(start_all(views(me, blocks, values), sems))
    to_spectrum(plan, values, into_even, into_odd, turn, mix, spec, mid)
    inverse_rows(plan, True, gated, spec, turn, mix, mid)
    inverse_columns(plan, back_even, back_odd, mid, values)
    wait_all(start_all(((to, source) for source, to in term_views(me, [term], values)), term_sems))


def grad_kernel(plan, views, count, me, filt, spec, back_even, back_odd, turn, mix, *refs):
    outs = refs[:count]
    values, mid, sems = refs[count:]
    inverse_rows(plan, True, filt, spec, turn, mix, mid)
    inverse_columns(plan, back_even, back_odd, mid, values)
    wait_all(start_all(((to, source) for source, to in views(me, outs, values)), sems))


def smem():
    return pl.BlockSpec(memory_space=pltpu.SMEM)


def vmem():
    return pl.BlockSpec(memory_space=pltpu.VMEM)


def anywhere():
    return pl.BlockSpec(memory_space=pl.ANY)


def kernel_cost(plan):
    return pl.CostEstimate(flops=plan.side**2, bytes_accessed=plan.side**2, transcendentals=0)


def call_kernel(plan, kernel, name, args, in_specs, out_shape, out_specs, scratch):
    return pl.pallas_call(
        kernel,
        out_shape=out_shape,
        in_specs=in_specs,
        out_specs=out_specs,
        scratch_shapes=scratch,
        compiler_params=pltpu.CompilerParams(vmem_limit_bytes=VMEM_LIMIT),
        cost_estimate=kernel_cost(plan),
        name=name,
    )(*args)


def float_array(shape):
    return jax.ShapeDtypeStruct(shape, jnp.float32)


def filter_spectrum(plan, me, tiles, views, copies):
    shape = (2, plan.rows, plan.side)
    return call_kernel(
        plan,
        functools.partial(filter_kernel, plan, views, len(tiles)),
        "filter_spectrum",
        (me, *tiles, plan.into_even, plan.into_odd, plan.turn, plan.mix),
        [smem()] + [anywhere()] * len(tiles) + [vmem()] * 4,
        float_array(shape),
        vmem(),
        [
            pltpu.VMEM((plan.side, plan.side), jnp.float32),
            pltpu.VMEM(shape, jnp.float32),
            pltpu.SemaphoreType.DMA((copies,)),
        ],
    )


def tables_of(plan):
    return (plan.into_even, plan.into_odd, plan.back_even, plan.back_odd, plan.turn, plan.mix)


def conv_of(plan, me, filt, blocks, views):
    count = len(blocks)
    shape = (2, plan.rows, plan.side)
    spec, *outs = call_kernel(
        plan,
        functools.partial(conv_kernel, plan, views, count),
        "conv_of",
        (me, filt, *blocks, *tables_of(plan)),
        [smem(), vmem()] + [vmem()] * count + [vmem()] * 6,
        [float_array(shape)] + [float_array((plan.side // count, plan.side))] * count,
        [vmem()] * (count + 1),
        [
            pltpu.VMEM((plan.side, plan.side), jnp.float32),
            pltpu.VMEM(shape, jnp.float32),
            pltpu.SemaphoreType.DMA((count,)),
        ],
    )
    return spec, outs


def term_of(plan, me, gated, blocks, views, term_shape, term_views):
    count = len(blocks)
    shape = (2, plan.rows, plan.side)
    return call_kernel(
        plan,
        functools.partial(term_kernel, plan, views, term_views, count),
        "term_of",
        (me, gated, *blocks, *tables_of(plan)),
        [smem(), vmem()] + [vmem()] * count + [vmem()] * 6,
        [float_array(shape), float_array(term_shape)],
        [vmem(), anywhere()],
        [
            pltpu.VMEM((plan.side, plan.side), jnp.float32),
            pltpu.VMEM(shape, jnp.float32),
            pltpu.SemaphoreType.DMA((count,)),
            pltpu.SemaphoreType.DMA((math.prod(term_shape[:2]),)),
        ],
    )


def grad_of(plan, me, filt, spec, count, views):
    return call_kernel(
        plan,
        functools.partial(grad_kernel, plan, views, count),
        "grad_of",
        (me, filt, spec, *tables_of(plan)[2:]),
        [smem()] + [vmem()] * 6,
        [float_array((plan.side // count, plan.side))] * count,
        [vmem()] * count,
        [
            pltpu.VMEM((plan.side, plan.side), jnp.float32),
            pltpu.VMEM((2, plan.rows, plan.side), jnp.float32),
            pltpu.SemaphoreType.DMA((count,)),
        ],
    )


def pairwise(block, axis, step):
    return lax.ppermute(block, axis, [(i, i ^ step) for i in range(lax.axis_size(axis))])


def after(first, then):
    return lax.optimization_barrier((first, then))[1]


def gate_kernel(steps, gates, me, *refs):
    count = len(steps)
    blocks = refs[:count]
    ins = refs[count : count + gates]
    outs, got, sems = refs[-gates - 2 : -2], refs[-2], refs[-1]
    here = pl.program_id(0)

    def copy_of(i):
        return pltpu.make_async_copy(blocks[i], got.at[i], sems.at[i])

    @pl.when(here == 0)
    def start():
        for i in range(count):
            copy_of(i).start()

    for i in range(count):

        @pl.when(here == i)
        def wait():
            copy_of(i).wait()

    values = got[here]
    for gate, out in zip(ins, outs):
        out[0] = (gate[0].astype(jnp.float32) * values).astype(jnp.bfloat16)


def gated_by(me, steps, blocks, gates, done=()):
    count = len(steps)
    shape = gates[0].shape

    def place(i, me):
        step = steps[-1]
        for j in range(count - 1):
            step = jnp.where(i == j, steps[j], step)
        return (me[0] ^ step, 0, 0)

    spec = pl.BlockSpec((1,) + shape[1:], place)
    size = count * shape[1] * shape[2]
    first_done = 1 + count + len(gates)
    return pl.pallas_call(
        functools.partial(gate_kernel, steps, len(gates)),
        grid_spec=pltpu.PrefetchScalarGridSpec(
            num_scalar_prefetch=1,
            grid=(count,),
            in_specs=[anywhere()] * count + [spec] * len(gates) + [anywhere()] * len(done),
            out_specs=[spec] * len(gates),
            scratch_shapes=[
                pltpu.VMEM((count,) + shape[1:], jnp.float32),
                pltpu.SemaphoreType.DMA((count,)),
            ],
        ),
        out_shape=[jax.ShapeDtypeStruct(shape, jnp.bfloat16)] * len(gates),
        input_output_aliases={first_done + i: i for i in range(len(done))},
        compiler_params=pltpu.CompilerParams(vmem_limit_bytes=VMEM_LIMIT),
        cost_estimate=pl.CostEstimate(
            flops=size * len(gates), bytes_accessed=4 * size * (1 + len(gates)), transcendentals=0
        ),
        name="gate_out",
    )(me, *blocks, *gates, *done)


def send_order(owners, cols):
    far = sorted(range(owners // 2, owners), key=lambda s: (-s // cols, -s))
    near = sorted(range(1, owners // 2), key=lambda s: (s % cols, -s))
    return far, near


def channel_shards(outer_gate, inner_gate, signal, grad_out, filter_weight):
    block, side = filter_weight.shape
    plan = Plan(side)
    parts, rows, cols = (lax.axis_size(name) for name in ("dp", "row", "col"))
    owners = rows * cols
    place = own_block()
    me = jnp.reshape(place, (1,)).astype(jnp.int32)
    far, near = send_order(owners, cols)
    order = far[:2]
    for i in range(2, len(far)):
        order = order + near[i - 2 : i - 1] + far[i : i + 1]
    order = order[:-1] + near[len(far) - 2 :] + order[-1:]
    last_order = far + near
    by_block = functools.partial(block_views, plan, owners)
    by_tile = functools.partial(tile_views, plan, (parts, rows, cols))

    def gated_block(left, right, step):
        at = place ^ step
        return lax.dynamic_index_in_dim(left[0], at, 0, False).astype(
            jnp.float32
        ) * lax.dynamic_index_in_dim(right[0], at, 0, False).astype(jnp.float32)

    crossed, neared = [], []

    def exchange(blocks, what, order, deep=3, near_wait=0):
        got = [blocks[0]] + [None] * (owners - 1)
        before, near_before = len(crossed), list(neared)
        neared.clear()
        for step in order:
            mine, waits = blocks[step], []
            if step in far:
                waits = crossed[max(0, len(crossed) - deep - 1) : max(0, len(crossed) - deep + 1)]
                if len(crossed) - before >= len(far) // 2:
                    waits = waits + near_before
            elif before:
                waits = crossed[before - 1 + near_wait : before + near_wait]
            if waits:
                mine = after(waits, mine)
            with jax.named_scope(f"{what}_{step}"):
                got[step] = pairwise(mine, ("row", "col"), step)
            (crossed if step in far else neared).append(got[step])
        return got

    height = block // parts
    own_part = lax.dynamic_slice_in_dim(filter_weight, lax.axis_index("dp") * height, height, 0)
    own_part = own_part * (1.0 / side)
    inner, values = inner_gate, signal
    gated = [None] * owners
    for step in order + [0]:
        gated[step] = gated_block(inner, values, step)
        if step and step % cols == 0:
            gated[step] = jnp.concatenate([gated[step], own_part])
        if step == order[0]:
            inner, values = after(gated[step], [inner_gate, signal])
    gated = exchange(gated, "gated", order)
    over_row = jnp.stack([own_part] + [gated[i * cols][block:] for i in range(1, rows)])
    grad_conv = [gated_block(grad_out, outer_gate, step) for step in range(owners)]
    over_row = after(gated + grad_conv, over_row)
    over_all = [lax.all_gather(over_row, ("dp", "col"))]
    filt = filter_spectrum(plan, me, over_all, by_tile, parts * owners)

    got = exchange(grad_conv, "grad_conv", [step for step in order if step != near[-1]], 4)
    spec, conv_out = conv_of(plan, me, filt, after([filt] + [got[step] for step in far[:1]], gated), by_block)
    with jax.named_scope(f"grad_conv_{near[-1]}"):
        got[near[-1]] = pairwise(after(conv_out[0], grad_conv[near[-1]]), ("row", "col"), near[-1])
    grad_conv = got
    conv = exchange(conv_out, "conv", order, 4)
    tile_shape = (parts * cols, rows, height, side)
    cot, term = term_of(plan, me, spec, grad_conv, by_block, tile_shape, by_tile)
    back_out = grad_of(plan, me, filt, cot, owners, by_block)
    grad_gated = exchange(back_out, "grad_gated", last_order, 2, 3)

    term = after([conv[step] for step in far[:2]], term)
    term = lax.psum_scatter(term, ("dp", "col"), scatter_dimension=0, tiled=False)
    with jax.named_scope("rows_sum"):
        term = [term[i] for i in range(rows)]
        bit = 1
        while bit < rows:
            arrived = pairwise(jnp.stack(term[bit::2 * bit]), "row", bit)
            for j, i in enumerate(range(0, rows, 2 * bit)):
                term[i] = term[i] + arrived[j]
            bit *= 2
    total = term[0] * (1.0 / side)
    every = [0] + order
    (grad_outer,) = gated_by(me, every, [conv[step] for step in every], [grad_out[0]])
    total = after(grad_outer, total)
    with jax.named_scope("parts_gather"):
        others = [pairwise(total, "dp", i) for i in range(1, parts)]
    pieces = jnp.stack([total] + others)
    bit = 1
    while bit < parts:
        upper = (lax.axis_index("dp") & bit) != 0
        swapped = jnp.flip(pieces.reshape(parts // (2 * bit), 2, bit, height, side), 1)
        pieces = jnp.where(upper, swapped.reshape(pieces.shape), pieces)
        bit *= 2
    grad_filter = pieces.reshape(block, side)

    every = [0] + far + near[::-1]
    gates = [signal[0], inner_gate[0]]
    early, late = every[:-1], every[-1:]
    done = gated_by(me, early, [grad_gated[step] for step in early], gates)
    grad_inner, grad_signal = gated_by(me, late, [grad_gated[step] for step in late], gates, done)
    return (grad_outer[None], grad_inner[None], grad_signal[None], grad_filter)


def powers_of_two(*sizes):
    return all(size & (size - 1) == 0 for size in sizes)


def shards(*arrays):
    parts, rows, cols = (lax.axis_size(name) for name in ("dp", "row", "col"))
    side = arrays[0].shape[3]
    whole = arrays[0].shape[1] == rows * cols and rows >= 2 and cols == 2
    fits = powers_of_two(parts, rows, cols, side) and side // 4 % LANE_PAD == 0
    fits = fits and arrays[4].shape[0] // parts % ROW_PAD == 0
    return (channel_shards if whole and fits else spread_shards)(*arrays)


def solution(mesh):
    placed = (
        P("dp", None, ("row", "col"), None),
        P("dp", None, ("row", "col"), None),
        P("dp", None, ("row", "col"), None),
        P("dp", None, ("row", "col"), None),
        P(("row", "col"), None),
    )
    return jax.shard_map(
        shards,
        mesh=mesh,
        in_specs=placed,
        out_specs=(
            P("dp", None, ("row", "col"), None),
            P("dp", None, ("row", "col"), None),
            P("dp", None, ("row", "col"), None),
            P(("row", "col"), None),
        ),
        check_vma=False,
    )
```

```python
import functools
import math

import jax
import jax.numpy as jnp
import numpy as np
from jax import lax
from jax.experimental import pallas as pl
from jax.experimental.pallas import tpu as pltpu
from jax.sharding import PartitionSpec as P

TWO_PI = 2.0 * math.pi


def contract(form, left, right):
    return jnp.einsum(
        form, left, right, precision=lax.Precision.HIGHEST, preferred_element_type=jnp.float32
    )


def redistribute(blocks):
    return lax.all_to_all(blocks, ("row", "col"), split_axis=0, concat_axis=0, tiled=True)


def own_block():
    return lax.axis_index("row") * lax.axis_size("col") + lax.axis_index("col")


def turn_angles(first_index, second_index, total):
    product = first_index * second_index % total
    angles = product.astype(jnp.float32) * (TWO_PI / total)
    return (jnp.cos(angles), jnp.sin(angles))


def axis_dft(real, imag, sign):
    length, width = real.shape
    first = 1 << (length.bit_length() - 1) // 2
    second = length // first
    index_a = jnp.arange(first, dtype=jnp.int32)
    index_b = jnp.arange(second, dtype=jnp.int32)
    cos_a, sin_a = turn_angles(index_a[:, None], index_a[None, :], first)
    sin_a = sign * sin_a
    cos_b, sin_b = turn_angles(index_b[:, None], index_b[None, :], second)
    sin_b = sign * sin_b
    twist_cos, twist_sin = turn_angles(index_a[:, None], index_b[None, :], length)
    twist_cos = twist_cos[:, :, None]
    twist_sin = sign * twist_sin[:, :, None]
    real_three = real.reshape(first, second, width)
    step_real = contract("abm,ak->kbm", real_three, cos_a)
    step_imag = contract("abm,ak->kbm", real_three, sin_a)
    if imag is not None:
        imag_three = imag.reshape(first, second, width)
        step_real = step_real - contract("abm,ak->kbm", imag_three, sin_a)
        step_imag = step_imag + contract("abm,ak->kbm", imag_three, cos_a)
    turned_real = step_real * twist_cos - step_imag * twist_sin
    turned_imag = step_real * twist_sin + step_imag * twist_cos
    out_real = contract("kbm,bj->jkm", turned_real, cos_b) - contract(
        "kbm,bj->jkm", turned_imag, sin_b
    )
    out_imag = contract("kbm,bj->jkm", turned_real, sin_b) + contract(
        "kbm,bj->jkm", turned_imag, cos_b
    )
    return (out_real.reshape(length, width), out_imag.reshape(length, width))


def forward(stacked, order):
    count, block, grid_side = stacked.shape
    owners = grid_side // block
    total = grid_side * grid_side
    send = jnp.transpose(stacked.reshape(count, block, owners, block), (2, 1, 0, 3)).reshape(
        owners, block, count * block
    )
    columns = redistribute(send).reshape(grid_side, count * block)
    first_real, first_imag = axis_dft(columns, None, -1.0)
    first_real = first_real.reshape(grid_side, count, block)
    first_imag = first_imag.reshape(grid_side, count, block)
    col_index = own_block() * block + jnp.arange(block, dtype=jnp.int32)
    cos_turn, sin_turn = turn_angles(order[:, None, None], col_index[None, None, :], total)
    turned_real = first_real * cos_turn + first_imag * sin_turn
    turned_imag = first_imag * cos_turn - first_real * sin_turn
    send_two = jnp.concatenate([turned_real, turned_imag], axis=1).reshape(
        owners, block, 2 * count * block
    )
    gotten = redistribute(send_two).reshape(owners, block, 2 * count, block)
    flat_real = jnp.transpose(gotten[:, :, :count, :], (0, 3, 1, 2)).reshape(
        grid_side, block * count
    )
    flat_imag = jnp.transpose(gotten[:, :, count:, :], (0, 3, 1, 2)).reshape(
        grid_side, block * count
    )
    out_real, out_imag = axis_dft(flat_real, flat_imag, -1.0)
    spec_real = jnp.transpose(out_real.reshape(grid_side, block, count), (1, 2, 0))
    spec_imag = jnp.transpose(out_imag.reshape(grid_side, block, count), (1, 2, 0))
    return (spec_real, spec_imag)


def inverse(spec_real, spec_imag, order):
    block, count, grid_side = spec_real.shape
    owners = grid_side // block
    total = grid_side * grid_side
    flat_real = jnp.transpose(spec_real, (2, 0, 1)).reshape(grid_side, block * count)
    flat_imag = jnp.transpose(spec_imag, (2, 0, 1)).reshape(grid_side, block * count)
    out_real, out_imag = axis_dft(flat_real, flat_imag, 1.0)
    back_real = jnp.transpose(out_real.reshape(owners, block, block, count), (0, 2, 3, 1))
    back_imag = jnp.transpose(out_imag.reshape(owners, block, block, count), (0, 2, 3, 1))
    freq_index = lax.dynamic_slice_in_dim(order, own_block() * block, block, 0)
    col_index = (
        jnp.arange(owners, dtype=jnp.int32)[:, None] * block
        + jnp.arange(block, dtype=jnp.int32)[None, :]
    )
    cos_turn, sin_turn = turn_angles(
        freq_index[None, :, None, None], col_index[:, None, None, :], total
    )
    turned_real = back_real * cos_turn - back_imag * sin_turn
    turned_imag = back_real * sin_turn + back_imag * cos_turn
    send = jnp.concatenate([turned_real, turned_imag], axis=2).reshape(
        owners, block, 2 * count * block
    )
    gotten = redistribute(send).reshape(grid_side, 2 * count * block)
    real_part = gotten[:, : count * block]
    imag_part = gotten[:, count * block :]
    full_real, full_imag = axis_dft(real_part, imag_part, 1.0)
    values = full_real * (1.0 / total)
    returned = redistribute(values.reshape(owners, block, count * block)).reshape(
        owners, block, count, block
    )
    return jnp.transpose(returned, (2, 1, 0, 3)).reshape(count, block, grid_side)


def spread_shards(outer_gate, inner_gate, signal, grad_out, filter_weight):
    grid_side = filter_weight.shape[1]
    freq_index = jnp.arange(grid_side, dtype=jnp.int32)
    outer_f = outer_gate[0].astype(jnp.float32)
    inner_f = inner_gate[0].astype(jnp.float32)
    signal_f = signal[0].astype(jnp.float32)
    grad_f = grad_out[0].astype(jnp.float32)
    channels = inner_f.shape[0]
    gated = inner_f * signal_f
    grad_conv = grad_f * outer_f
    taps = (filter_weight * (1.0 / grid_side))[None]
    spec_real, spec_imag = forward(jnp.concatenate([gated, grad_conv], axis=0), freq_index)
    filt_real, filt_imag = forward(taps, freq_index)
    gated_real = spec_real[:, :channels]
    gated_imag = spec_imag[:, :channels]
    cot_real = spec_real[:, channels : 2 * channels]
    cot_imag = spec_imag[:, channels : 2 * channels]
    conv_real = filt_real * gated_real - filt_imag * gated_imag
    conv_imag = filt_real * gated_imag + filt_imag * gated_real
    back_real = filt_real * cot_real + filt_imag * cot_imag
    back_imag = filt_real * cot_imag - filt_imag * cot_real
    term_real = jnp.sum(gated_real * cot_real + gated_imag * cot_imag, axis=1, keepdims=True)
    term_imag = jnp.sum(gated_real * cot_imag - gated_imag * cot_real, axis=1, keepdims=True)
    values = inverse(
        jnp.concatenate([conv_real, back_real, term_real], axis=1),
        jnp.concatenate([conv_imag, back_imag, term_imag], axis=1),
        freq_index,
    )
    grad_filter = lax.psum(values[2 * channels], "dp") * (1.0 / grid_side)
    conv = values[:channels]
    grad_gated = values[channels : 2 * channels]
    grad_outer = (grad_f * conv).astype(jnp.bfloat16)[None]
    grad_inner = (grad_gated * signal_f).astype(jnp.bfloat16)[None]
    grad_signal = (grad_gated * inner_f).astype(jnp.bfloat16)[None]
    return (grad_outer, grad_inner, grad_signal, grad_filter)


VMEM_LIMIT = 18 * 1024 * 1024
ROW_PAD = 16
LANE_PAD = 128


def up_to(value, unit):
    return -(-value // unit) * unit


def high_low(table):
    high = table.astype(jnp.bfloat16)
    low = (table - high.astype(np.float64)).astype(jnp.bfloat16)
    return np.stack([high, low])


class Plan:
    def __init__(self, side):
        half = side // 2
        self.side, self.half, self.quarter = side, half, side // 4
        self.evens = up_to(half // 2 + 1, ROW_PAD)
        self.odds = half // 2
        self.rows = self.evens + self.odds
        self.even_depth = up_to(2 * self.evens, LANE_PAD)
        total = side * side
        even_k = 2 * np.arange(self.evens)
        odd_k = 2 * np.arange(self.odds) + 1
        live = (even_k <= half).astype(np.float64)
        p = np.arange(half)

        def waves(k, scale):
            angle = 2.0 * np.pi * (k[:, None] * p[None, :] % side) / side
            return np.concatenate([np.cos(angle) * scale[:, None], -np.sin(angle) * scale[:, None]])

        ones = np.ones(self.odds)
        self.into_even = high_low(waves(even_k, live))
        self.into_odd = high_low(waves(odd_k, ones))
        weight = np.where((even_k == 0) | (even_k == half), 1.0, 2.0) * live / total
        back_even = np.zeros((half, self.even_depth))
        back_even[:, : 2 * self.evens] = waves(even_k, weight).T
        self.back_even = high_low(back_even)
        self.back_odd = high_low(waves(odd_k, ones * 2.0 / total).T)
        k = np.concatenate([even_k, odd_k])
        turn = 2.0 * np.pi * (k[:, None] * np.arange(side)[None, :] % total) / total
        self.turn = np.stack([np.cos(turn), np.sin(turn)]).astype(np.float32)
        q = np.arange(self.quarter)
        mixes = []
        for r in range(4):
            angle = 2.0 * np.pi * (q[:, None] * (4 * q[None, :] + r) % side) / side
            cos, sin = np.cos(angle), np.sin(angle)
            mixes.append(np.block([[cos, -sin], [sin, cos]]))
        self.mix = high_low(np.stack(mixes))
        self.row_tile = next(t for t in (176, 264, 16, 8) if self.rows % t == 0)


def split_terms(values):
    high = values.astype(jnp.bfloat16)
    return high, (values - high.astype(jnp.float32)).astype(jnp.bfloat16)


def dot_in(table, rows, high, low):
    dot = functools.partial(jnp.dot, preferred_element_type=jnp.float32)
    first, second = table[0, rows], table[1, rows]
    return dot(first, high) + (dot(first, low) + dot(second, high))


def block_views(plan, owners, me, blocks, values):
    size = plan.side // owners
    for step in range(owners):
        at = pl.multiple_of((me[0] ^ step) * size, size)
        yield blocks[step].at[pl.ds(0, size)], values.at[pl.ds(at, size)]


def tile_views(plan, grid, me, tiles, values):
    parts, rows, cols = grid
    block = plan.side // (rows * cols)
    height = block // parts
    own_row = me[0] // cols
    for part in range(parts):
        for col in range(cols):
            for i in range(rows):
                at = ((own_row ^ i) * cols + col) * block + part * height
                yield tiles[0].at[part * cols + col, i], values.at[pl.ds(pl.multiple_of(at, height), height)]


def start_all(pairs, sems):
    copies = [pltpu.make_async_copy(source, to, sems.at[i]) for i, (source, to) in enumerate(pairs)]
    for copy in copies:
        copy.start()
    return copies


def wait_all(copies):
    for copy in copies:
        copy.wait()


def to_spectrum(plan, values, into_even, into_odd, turn, mix, spec, mid):
    side, half, quarter = plan.side, plan.half, plan.quarter

    @pl.loop(0, side // quarter)
    def columns(tile):
        cols = pl.ds(pl.multiple_of(tile * quarter, quarter), quarter)
        top, bottom = values[pl.ds(0, half), cols], values[pl.ds(half, half), cols]
        for first, count, table, part in (
            (0, plan.evens, into_even, top + bottom),
            (plan.evens, plan.odds, into_odd, top - bottom),
        ):
            out = dot_in(table, slice(None), *split_terms(part))
            real, imag = out[:count], out[count:]
            rows = pl.ds(first, count)
            cos, sin = turn[0, rows, cols], turn[1, rows, cols]
            mid[0, rows, cols] = real * cos + imag * sin
            mid[1, rows, cols] = imag * cos - real * sin

    @pl.loop(0, plan.rows // plan.row_tile)
    def rows_loop(tile):
        rows = pl.ds(pl.multiple_of(tile * plan.row_tile, plan.row_tile), plan.row_tile)
        real = [mid[0, rows, pl.ds(j * quarter, quarter)] for j in range(4)]
        imag = [mid[1, rows, pl.ds(j * quarter, quarter)] for j in range(4)]
        sum_r, sum_i = real[0] + real[2], imag[0] + imag[2]
        dif_r, dif_i = real[0] - real[2], imag[0] - imag[2]
        two_r, two_i = real[1] + real[3], imag[1] + imag[3]
        odd_r, odd_i = real[1] - real[3], imag[1] - imag[3]
        turns = (
            (sum_r + two_r, sum_i + two_i),
            (dif_r + odd_i, dif_i - odd_r),
            (sum_r - two_r, sum_i - two_i),
            (dif_r - odd_i, dif_i + odd_r),
        )
        dot = functools.partial(jnp.dot, preferred_element_type=jnp.float32)
        for r, pair in enumerate(turns):
            high, low = split_terms(jnp.concatenate(pair, axis=1))
            out = dot(high, mix[0, r]) + (dot(low, mix[0, r]) + dot(high, mix[1, r]))
            cols = pl.ds(r * quarter, quarter)
            spec[0, rows, cols] = out[:, :quarter]
            spec[1, rows, cols] = out[:, quarter:]


def inverse_rows(plan, conjugate, left, right, turn, mix, mid):
    quarter = plan.quarter

    @pl.loop(0, plan.rows // plan.row_tile)
    def rows_loop(tile):
        rows = pl.ds(pl.multiple_of(tile * plan.row_tile, plan.row_tile), plan.row_tile)
        real, imag = [], []
        for r in range(4):
            cols = pl.ds(r * quarter, quarter)
            left_r, left_i = left[0, rows, cols], left[1, rows, cols]
            right_r, right_i = right[0, rows, cols], right[1, rows, cols]
            if conjugate:
                left_i = -left_i
            pair = (left_r * right_r - left_i * right_i, left_r * right_i + left_i * right_r)
            high, low = split_terms(jnp.concatenate(pair, axis=1))

            def dot(part, table):
                return lax.dot_general(
                    part, table, (((1,), (1,)), ((), ())), preferred_element_type=jnp.float32
                )

            out = dot(high, mix[0, r]) + (dot(low, mix[0, r]) + dot(high, mix[1, r]))
            real.append(out[:, :quarter])
            imag.append(out[:, quarter:])
        sum_r, sum_i = real[0] + real[2], imag[0] + imag[2]
        dif_r, dif_i = real[0] - real[2], imag[0] - imag[2]
        two_r, two_i = real[1] + real[3], imag[1] + imag[3]
        odd_r, odd_i = real[1] - real[3], imag[1] - imag[3]
        turns = (
            (sum_r + two_r, sum_i + two_i),
            (dif_r - odd_i, dif_i + odd_r),
            (sum_r - two_r, sum_i - two_i),
            (dif_r + odd_i, dif_i - odd_r),
        )
        for j, (got_r, got_i) in enumerate(turns):
            cols = pl.ds(j * quarter, quarter)
            cos, sin = turn[0, rows, cols], turn[1, rows, cols]
            mid[0, rows, cols] = got_r * cos - got_i * sin
            mid[1, rows, cols] = got_r * sin + got_i * cos


def inverse_columns(plan, back_even, back_odd, mid, values):
    side, half, quarter = plan.side, plan.half, plan.quarter

    @pl.loop(0, side // quarter)
    def columns(tile):
        cols = pl.ds(pl.multiple_of(tile * quarter, quarter), quarter)
        even = [mid[0, pl.ds(0, plan.evens), cols], mid[1, pl.ds(0, plan.evens), cols]]
        if plan.even_depth > 2 * plan.evens:
            even.append(jnp.zeros((plan.even_depth - 2 * plan.evens, quarter), jnp.float32))
        odd = [mid[0, pl.ds(plan.evens, plan.odds), cols], mid[1, pl.ds(plan.evens, plan.odds), cols]]
        from_even = dot_in(back_even, slice(None), *split_terms(jnp.concatenate(even)))
        from_odd = dot_in(back_odd, slice(None), *split_terms(jnp.concatenate(odd)))
        values[pl.ds(0, half), cols] = from_even + from_odd
        values[pl.ds(half, half), cols] = from_even - from_odd


def filter_kernel(plan, views, count, me, *refs):
    tiles = refs[:count]
    into_even, into_odd, turn, mix, spec, values, mid, sems = refs[count:]
    wait_all(start_all(views(me, tiles, values), sems))
    to_spectrum(plan, values, into_even, into_odd, turn, mix, spec, mid)


def conv_kernel(plan, views, count, me, filt, *refs):
    blocks, tables = refs[:count], refs[count : count + 6]
    into_even, into_odd, back_even, back_odd, turn, mix = tables
    spec, outs = refs[count + 6], refs[count + 7 : 2 * count + 7]
    values, mid, sems = refs[2 * count + 7 :]
    wait_all(start_all(views(me, blocks, values), sems))
    to_spectrum(plan, values, into_even, into_odd, turn, mix, spec, mid)
    inverse_rows(plan, False, filt, spec, turn, mix, mid)
    inverse_columns(plan, back_even, back_odd, mid, values)
    wait_all(start_all(((to, source) for source, to in views(me, outs, values)), sems))


def term_kernel(plan, views, term_views, count, me, gated, *refs):
    blocks, tables = refs[:count], refs[count : count + 6]
    into_even, into_odd, back_even, back_odd, turn, mix = tables
    spec, term, values, mid, sems, term_sems = refs[count + 6 :]
    wait_all(start_all(views(me, blocks, values), sems))
    to_spectrum(plan, values, into_even, into_odd, turn, mix, spec, mid)
    inverse_rows(plan, True, gated, spec, turn, mix, mid)
    inverse_columns(plan, back_even, back_odd, mid, values)
    wait_all(start_all(((to, source) for source, to in term_views(me, [term], values)), term_sems))


def grad_kernel(plan, views, count, me, filt, spec, back_even, back_odd, turn, mix, *refs):
    outs = refs[:count]
    values, mid, sems = refs[count:]
    inverse_rows(plan, True, filt, spec, turn, mix, mid)
    inverse_columns(plan, back_even, back_odd, mid, values)
    wait_all(start_all(((to, source) for source, to in views(me, outs, values)), sems))


def smem():
    return pl.BlockSpec(memory_space=pltpu.SMEM)


def vmem():
    return pl.BlockSpec(memory_space=pltpu.VMEM)


def anywhere():
    return pl.BlockSpec(memory_space=pl.ANY)


def kernel_cost(plan):
    return pl.CostEstimate(flops=plan.side**2, bytes_accessed=plan.side**2, transcendentals=0)


def call_kernel(plan, kernel, name, args, in_specs, out_shape, out_specs, scratch):
    return pl.pallas_call(
        kernel,
        out_shape=out_shape,
        in_specs=in_specs,
        out_specs=out_specs,
        scratch_shapes=scratch,
        compiler_params=pltpu.CompilerParams(vmem_limit_bytes=VMEM_LIMIT),
        cost_estimate=kernel_cost(plan),
        name=name,
    )(*args)


def float_array(shape):
    return jax.ShapeDtypeStruct(shape, jnp.float32)


def filter_spectrum(plan, me, tiles, views, copies):
    shape = (2, plan.rows, plan.side)
    return call_kernel(
        plan,
        functools.partial(filter_kernel, plan, views, len(tiles)),
        "filter_spectrum",
        (me, *tiles, plan.into_even, plan.into_odd, plan.turn, plan.mix),
        [smem()] + [anywhere()] * len(tiles) + [vmem()] * 4,
        float_array(shape),
        vmem(),
        [
            pltpu.VMEM((plan.side, plan.side), jnp.float32),
            pltpu.VMEM(shape, jnp.float32),
            pltpu.SemaphoreType.DMA((copies,)),
        ],
    )


def tables_of(plan):
    return (plan.into_even, plan.into_odd, plan.back_even, plan.back_odd, plan.turn, plan.mix)


def conv_of(plan, me, filt, blocks, views):
    count = len(blocks)
    shape = (2, plan.rows, plan.side)
    spec, *outs = call_kernel(
        plan,
        functools.partial(conv_kernel, plan, views, count),
        "conv_of",
        (me, filt, *blocks, *tables_of(plan)),
        [smem(), vmem()] + [vmem()] * count + [vmem()] * 6,
        [float_array(shape)] + [float_array((plan.side // count, plan.side))] * count,
        [vmem()] * (count + 1),
        [
            pltpu.VMEM((plan.side, plan.side), jnp.float32),
            pltpu.VMEM(shape, jnp.float32),
            pltpu.SemaphoreType.DMA((count,)),
        ],
    )
    return spec, outs


def term_of(plan, me, gated, blocks, views, term_shape, term_views):
    count = len(blocks)
    shape = (2, plan.rows, plan.side)
    return call_kernel(
        plan,
        functools.partial(term_kernel, plan, views, term_views, count),
        "term_of",
        (me, gated, *blocks, *tables_of(plan)),
        [smem(), vmem()] + [vmem()] * count + [vmem()] * 6,
        [float_array(shape), float_array(term_shape)],
        [vmem(), anywhere()],
        [
            pltpu.VMEM((plan.side, plan.side), jnp.float32),
            pltpu.VMEM(shape, jnp.float32),
            pltpu.SemaphoreType.DMA((count,)),
            pltpu.SemaphoreType.DMA((math.prod(term_shape[:2]),)),
        ],
    )


def grad_of(plan, me, filt, spec, count, views):
    return call_kernel(
        plan,
        functools.partial(grad_kernel, plan, views, count),
        "grad_of",
        (me, filt, spec, *tables_of(plan)[2:]),
        [smem()] + [vmem()] * 6,
        [float_array((plan.side // count, plan.side))] * count,
        [vmem()] * count,
        [
            pltpu.VMEM((plan.side, plan.side), jnp.float32),
            pltpu.VMEM((2, plan.rows, plan.side), jnp.float32),
            pltpu.SemaphoreType.DMA((count,)),
        ],
    )


def pairwise(block, axis, step):
    return lax.ppermute(block, axis, [(i, i ^ step) for i in range(lax.axis_size(axis))])


def after(first, then):
    return lax.optimization_barrier((first, then))[1]


def gate_kernel(steps, gates, me, *refs):
    count = len(steps)
    blocks = refs[:count]
    ins = refs[count : count + gates]
    outs, got, sems = refs[-gates - 2 : -2], refs[-2], refs[-1]
    here = pl.program_id(0)

    def copy_of(i):
        return pltpu.make_async_copy(blocks[i], got.at[i], sems.at[i])

    @pl.when(here == 0)
    def start():
        for i in range(count):
            copy_of(i).start()

    for i in range(count):

        @pl.when(here == i)
        def wait():
            copy_of(i).wait()

    values = got[here]
    for gate, out in zip(ins, outs):
        out[0] = (gate[0].astype(jnp.float32) * values).astype(jnp.bfloat16)


def gated_by(me, steps, blocks, gates, done=()):
    count = len(steps)
    shape = gates[0].shape

    def place(i, me):
        step = steps[-1]
        for j in range(count - 1):
            step = jnp.where(i == j, steps[j], step)
        return (me[0] ^ step, 0, 0)

    spec = pl.BlockSpec((1,) + shape[1:], place)
    size = count * shape[1] * shape[2]
    first_done = 1 + count + len(gates)
    return pl.pallas_call(
        functools.partial(gate_kernel, steps, len(gates)),
        grid_spec=pltpu.PrefetchScalarGridSpec(
            num_scalar_prefetch=1,
            grid=(count,),
            in_specs=[anywhere()] * count + [spec] * len(gates) + [anywhere()] * len(done),
            out_specs=[spec] * len(gates),
            scratch_shapes=[
                pltpu.VMEM((count,) + shape[1:], jnp.float32),
                pltpu.SemaphoreType.DMA((count,)),
            ],
        ),
        out_shape=[jax.ShapeDtypeStruct(shape, jnp.bfloat16)] * len(gates),
        input_output_aliases={first_done + i: i for i in range(len(done))},
        compiler_params=pltpu.CompilerParams(vmem_limit_bytes=VMEM_LIMIT),
        cost_estimate=pl.CostEstimate(
            flops=size * len(gates), bytes_accessed=4 * size * (1 + len(gates)), transcendentals=0
        ),
        name="gate_out",
    )(me, *blocks, *gates, *done)


def send_order(owners, cols):
    far = sorted(range(owners // 2, owners), key=lambda s: (-s // cols, -s))
    near = sorted(range(1, owners // 2), key=lambda s: (s % cols, -s))
    return far, near


def channel_shards(outer_gate, inner_gate, signal, grad_out, filter_weight):
    block, side = filter_weight.shape
    plan = Plan(side)
    parts, rows, cols = (lax.axis_size(name) for name in ("dp", "row", "col"))
    owners = rows * cols
    place = own_block()
    me = jnp.reshape(place, (1,)).astype(jnp.int32)
    far, near = send_order(owners, cols)
    order = far[:2]
    for i in range(2, len(far)):
        order = order + near[i - 2 : i - 1] + far[i : i + 1]
    order = order[:-1] + near[len(far) - 2 :] + order[-1:]
    last_order = far + near
    by_block = functools.partial(block_views, plan, owners)
    by_tile = functools.partial(tile_views, plan, (parts, rows, cols))

    def gated_block(left, right, step):
        at = place ^ step
        return lax.dynamic_index_in_dim(left[0], at, 0, False).astype(
            jnp.float32
        ) * lax.dynamic_index_in_dim(right[0], at, 0, False).astype(jnp.float32)

    crossed, neared = [], []

    def exchange(blocks, what, order, deep=3, near_wait=0):
        got = [blocks[0]] + [None] * (owners - 1)
        before, near_before = len(crossed), list(neared)
        neared.clear()
        for step in order:
            mine, waits = blocks[step], []
            if step in far:
                waits = crossed[max(0, len(crossed) - deep - 1) : max(0, len(crossed) - deep + 1)]
                if len(crossed) - before >= len(far) // 2:
                    waits = waits + near_before
            elif before:
                waits = crossed[before - 1 + near_wait : before + near_wait]
            if waits:
                mine = after(waits, mine)
            with jax.named_scope(f"{what}_{step}"):
                got[step] = pairwise(mine, ("row", "col"), step)
            (crossed if step in far else neared).append(got[step])
        return got

    height = block // parts
    own_part = lax.dynamic_slice_in_dim(filter_weight, lax.axis_index("dp") * height, height, 0)
    own_part = own_part * (1.0 / side)
    inner, values = inner_gate, signal
    gated = [None] * owners
    for step in order + [0]:
        gated[step] = gated_block(inner, values, step)
        if step and step % cols == 0:
            gated[step] = jnp.concatenate([gated[step], own_part])
        if step == order[0]:
            inner, values = after(gated[step], [inner_gate, signal])
    gated = exchange(gated, "gated", order)
    over_row = jnp.stack([own_part] + [gated[i * cols][block:] for i in range(1, rows)])
    grad_conv = [gated_block(grad_out, outer_gate, step) for step in range(owners)]
    over_row = after(gated + grad_conv, over_row)
    over_all = [lax.all_gather(over_row, ("dp", "col"))]
    filt = filter_spectrum(plan, me, over_all, by_tile, parts * owners)

    got = exchange(grad_conv, "grad_conv", [step for step in order if step != near[-1]], 4)
    spec, conv_out = conv_of(plan, me, filt, after([filt] + [got[step] for step in far[:1]], gated), by_block)
    with jax.named_scope(f"grad_conv_{near[-1]}"):
        got[near[-1]] = pairwise(after(conv_out[0], grad_conv[near[-1]]), ("row", "col"), near[-1])
    grad_conv = got
    conv = exchange(conv_out, "conv", order, 4)
    tile_shape = (parts * cols, rows, height, side)
    cot, term = term_of(plan, me, spec, grad_conv, by_block, tile_shape, by_tile)
    back_out = grad_of(plan, me, filt, cot, owners, by_block)
    grad_gated = exchange(back_out, "grad_gated", last_order, 4, 3)

    term = after([conv[step] for step in far[:2]], term)
    term = lax.psum_scatter(term, ("dp", "col"), scatter_dimension=0, tiled=False)
    every = [0] + order
    (grad_outer,) = gated_by(me, every, [conv[step] for step in every], [grad_out[0]])
    term = after([grad_outer] + [grad_gated[step] for step in far[:2]], term)
    with jax.named_scope("rows_sum"):
        term = [term[i] for i in range(rows)]
        bit = 1
        while bit < rows:
            arrived = pairwise(jnp.stack(term[bit::2 * bit]), "row", bit)
            for j, i in enumerate(range(0, rows, 2 * bit)):
                term[i] = term[i] + arrived[j]
            bit *= 2
    total = term[0] * (1.0 / side)
    with jax.named_scope("parts_gather"):
        others = [pairwise(total, "dp", i) for i in range(1, parts)]
    pieces = jnp.stack([total] + others)
    bit = 1
    while bit < parts:
        upper = (lax.axis_index("dp") & bit) != 0
        swapped = jnp.flip(pieces.reshape(parts // (2 * bit), 2, bit, height, side), 1)
        pieces = jnp.where(upper, swapped.reshape(pieces.shape), pieces)
        bit *= 2
    grad_filter = pieces.reshape(block, side)

    every = [0] + far + near[::-1]
    gates = [signal[0], inner_gate[0]]
    early, late = every[:-1], every[-1:]
    done = gated_by(me, early, [grad_gated[step] for step in early], gates)
    grad_inner, grad_signal = gated_by(me, late, [grad_gated[step] for step in late], gates, done)
    return (grad_outer[None], grad_inner[None], grad_signal[None], grad_filter)


def powers_of_two(*sizes):
    return all(size & (size - 1) == 0 for size in sizes)


def shards(*arrays):
    parts, rows, cols = (lax.axis_size(name) for name in ("dp", "row", "col"))
    side = arrays[0].shape[3]
    whole = arrays[0].shape[1] == rows * cols and rows >= 2 and cols == 2
    fits = powers_of_two(parts, rows, cols, side) and side // 4 % LANE_PAD == 0
    fits = fits and arrays[4].shape[0] // parts % ROW_PAD == 0
    return (channel_shards if whole and fits else spread_shards)(*arrays)


def solution(mesh):
    placed = (
        P("dp", None, ("row", "col"), None),
        P("dp", None, ("row", "col"), None),
        P("dp", None, ("row", "col"), None),
        P("dp", None, ("row", "col"), None),
        P(("row", "col"), None),
    )
    return jax.shard_map(
        shards,
        mesh=mesh,
        in_specs=placed,
        out_specs=(
            P("dp", None, ("row", "col"), None),
            P("dp", None, ("row", "col"), None),
            P("dp", None, ("row", "col"), None),
            P(("row", "col"), None),
        ),
        check_vma=False,
    )
```

```python
import functools
import math

import jax
import jax.numpy as jnp
import numpy as np
from jax import lax
from jax.experimental import pallas as pl
from jax.experimental.pallas import tpu as pltpu
from jax.sharding import PartitionSpec as P

TWO_PI = 2.0 * math.pi


def contract(form, left, right):
    return jnp.einsum(
        form, left, right, precision=lax.Precision.HIGHEST, preferred_element_type=jnp.float32
    )


def redistribute(blocks):
    return lax.all_to_all(blocks, ("row", "col"), split_axis=0, concat_axis=0, tiled=True)


def own_block():
    return lax.axis_index("row") * lax.axis_size("col") + lax.axis_index("col")


def turn_angles(first_index, second_index, total):
    product = first_index * second_index % total
    angles = product.astype(jnp.float32) * (TWO_PI / total)
    return (jnp.cos(angles), jnp.sin(angles))


def axis_dft(real, imag, sign):
    length, width = real.shape
    first = 1 << (length.bit_length() - 1) // 2
    second = length // first
    index_a = jnp.arange(first, dtype=jnp.int32)
    index_b = jnp.arange(second, dtype=jnp.int32)
    cos_a, sin_a = turn_angles(index_a[:, None], index_a[None, :], first)
    sin_a = sign * sin_a
    cos_b, sin_b = turn_angles(index_b[:, None], index_b[None, :], second)
    sin_b = sign * sin_b
    twist_cos, twist_sin = turn_angles(index_a[:, None], index_b[None, :], length)
    twist_cos = twist_cos[:, :, None]
    twist_sin = sign * twist_sin[:, :, None]
    real_three = real.reshape(first, second, width)
    step_real = contract("abm,ak->kbm", real_three, cos_a)
    step_imag = contract("abm,ak->kbm", real_three, sin_a)
    if imag is not None:
        imag_three = imag.reshape(first, second, width)
        step_real = step_real - contract("abm,ak->kbm", imag_three, sin_a)
        step_imag = step_imag + contract("abm,ak->kbm", imag_three, cos_a)
    turned_real = step_real * twist_cos - step_imag * twist_sin
    turned_imag = step_real * twist_sin + step_imag * twist_cos
    out_real = contract("kbm,bj->jkm", turned_real, cos_b) - contract(
        "kbm,bj->jkm", turned_imag, sin_b
    )
    out_imag = contract("kbm,bj->jkm", turned_real, sin_b) + contract(
        "kbm,bj->jkm", turned_imag, cos_b
    )
    return (out_real.reshape(length, width), out_imag.reshape(length, width))


def forward(stacked, order):
    count, block, grid_side = stacked.shape
    owners = grid_side // block
    total = grid_side * grid_side
    send = jnp.transpose(stacked.reshape(count, block, owners, block), (2, 1, 0, 3)).reshape(
        owners, block, count * block
    )
    columns = redistribute(send).reshape(grid_side, count * block)
    first_real, first_imag = axis_dft(columns, None, -1.0)
    first_real = first_real.reshape(grid_side, count, block)
    first_imag = first_imag.reshape(grid_side, count, block)
    col_index = own_block() * block + jnp.arange(block, dtype=jnp.int32)
    cos_turn, sin_turn = turn_angles(order[:, None, None], col_index[None, None, :], total)
    turned_real = first_real * cos_turn + first_imag * sin_turn
    turned_imag = first_imag * cos_turn - first_real * sin_turn
    send_two = jnp.concatenate([turned_real, turned_imag], axis=1).reshape(
        owners, block, 2 * count * block
    )
    gotten = redistribute(send_two).reshape(owners, block, 2 * count, block)
    flat_real = jnp.transpose(gotten[:, :, :count, :], (0, 3, 1, 2)).reshape(
        grid_side, block * count
    )
    flat_imag = jnp.transpose(gotten[:, :, count:, :], (0, 3, 1, 2)).reshape(
        grid_side, block * count
    )
    out_real, out_imag = axis_dft(flat_real, flat_imag, -1.0)
    spec_real = jnp.transpose(out_real.reshape(grid_side, block, count), (1, 2, 0))
    spec_imag = jnp.transpose(out_imag.reshape(grid_side, block, count), (1, 2, 0))
    return (spec_real, spec_imag)


def inverse(spec_real, spec_imag, order):
    block, count, grid_side = spec_real.shape
    owners = grid_side // block
    total = grid_side * grid_side
    flat_real = jnp.transpose(spec_real, (2, 0, 1)).reshape(grid_side, block * count)
    flat_imag = jnp.transpose(spec_imag, (2, 0, 1)).reshape(grid_side, block * count)
    out_real, out_imag = axis_dft(flat_real, flat_imag, 1.0)
    back_real = jnp.transpose(out_real.reshape(owners, block, block, count), (0, 2, 3, 1))
    back_imag = jnp.transpose(out_imag.reshape(owners, block, block, count), (0, 2, 3, 1))
    freq_index = lax.dynamic_slice_in_dim(order, own_block() * block, block, 0)
    col_index = (
        jnp.arange(owners, dtype=jnp.int32)[:, None] * block
        + jnp.arange(block, dtype=jnp.int32)[None, :]
    )
    cos_turn, sin_turn = turn_angles(
        freq_index[None, :, None, None], col_index[:, None, None, :], total
    )
    turned_real = back_real * cos_turn - back_imag * sin_turn
    turned_imag = back_real * sin_turn + back_imag * cos_turn
    send = jnp.concatenate([turned_real, turned_imag], axis=2).reshape(
        owners, block, 2 * count * block
    )
    gotten = redistribute(send).reshape(grid_side, 2 * count * block)
    real_part = gotten[:, : count * block]
    imag_part = gotten[:, count * block :]
    full_real, full_imag = axis_dft(real_part, imag_part, 1.0)
    values = full_real * (1.0 / total)
    returned = redistribute(values.reshape(owners, block, count * block)).reshape(
        owners, block, count, block
    )
    return jnp.transpose(returned, (2, 1, 0, 3)).reshape(count, block, grid_side)


def spread_shards(outer_gate, inner_gate, signal, grad_out, filter_weight):
    grid_side = filter_weight.shape[1]
    freq_index = jnp.arange(grid_side, dtype=jnp.int32)
    outer_f = outer_gate[0].astype(jnp.float32)
    inner_f = inner_gate[0].astype(jnp.float32)
    signal_f = signal[0].astype(jnp.float32)
    grad_f = grad_out[0].astype(jnp.float32)
    channels = inner_f.shape[0]
    gated = inner_f * signal_f
    grad_conv = grad_f * outer_f
    taps = (filter_weight * (1.0 / grid_side))[None]
    spec_real, spec_imag = forward(jnp.concatenate([gated, grad_conv], axis=0), freq_index)
    filt_real, filt_imag = forward(taps, freq_index)
    gated_real = spec_real[:, :channels]
    gated_imag = spec_imag[:, :channels]
    cot_real = spec_real[:, channels : 2 * channels]
    cot_imag = spec_imag[:, channels : 2 * channels]
    conv_real = filt_real * gated_real - filt_imag * gated_imag
    conv_imag = filt_real * gated_imag + filt_imag * gated_real
    back_real = filt_real * cot_real + filt_imag * cot_imag
    back_imag = filt_real * cot_imag - filt_imag * cot_real
    term_real = jnp.sum(gated_real * cot_real + gated_imag * cot_imag, axis=1, keepdims=True)
    term_imag = jnp.sum(gated_real * cot_imag - gated_imag * cot_real, axis=1, keepdims=True)
    values = inverse(
        jnp.concatenate([conv_real, back_real, term_real], axis=1),
        jnp.concatenate([conv_imag, back_imag, term_imag], axis=1),
        freq_index,
    )
    grad_filter = lax.psum(values[2 * channels], "dp") * (1.0 / grid_side)
    conv = values[:channels]
    grad_gated = values[channels : 2 * channels]
    grad_outer = (grad_f * conv).astype(jnp.bfloat16)[None]
    grad_inner = (grad_gated * signal_f).astype(jnp.bfloat16)[None]
    grad_signal = (grad_gated * inner_f).astype(jnp.bfloat16)[None]
    return (grad_outer, grad_inner, grad_signal, grad_filter)


VMEM_LIMIT = 18 * 1024 * 1024
ROW_PAD = 16
LANE_PAD = 128


def up_to(value, unit):
    return -(-value // unit) * unit


def high_low(table):
    high = table.astype(jnp.bfloat16)
    low = (table - high.astype(np.float64)).astype(jnp.bfloat16)
    return np.stack([high, low])


class Plan:
    def __init__(self, side):
        half = side // 2
        self.side, self.half, self.quarter = side, half, side // 4
        self.evens = up_to(half // 2 + 1, ROW_PAD)
        self.odds = half // 2
        self.rows = self.evens + self.odds
        self.even_depth = up_to(2 * self.evens, LANE_PAD)
        total = side * side
        even_k = 2 * np.arange(self.evens)
        odd_k = 2 * np.arange(self.odds) + 1
        live = (even_k <= half).astype(np.float64)
        p = np.arange(half)

        def waves(k, scale):
            angle = 2.0 * np.pi * (k[:, None] * p[None, :] % side) / side
            return np.concatenate([np.cos(angle) * scale[:, None], -np.sin(angle) * scale[:, None]])

        ones = np.ones(self.odds)
        self.into_even = high_low(waves(even_k, live))
        self.into_odd = high_low(waves(odd_k, ones))
        weight = np.where((even_k == 0) | (even_k == half), 1.0, 2.0) * live / total
        back_even = np.zeros((half, self.even_depth))
        back_even[:, : 2 * self.evens] = waves(even_k, weight).T
        self.back_even = high_low(back_even)
        self.back_odd = high_low(waves(odd_k, ones * 2.0 / total).T)
        k = np.concatenate([even_k, odd_k])
        turn = 2.0 * np.pi * (k[:, None] * np.arange(side)[None, :] % total) / total
        self.turn = np.stack([np.cos(turn), np.sin(turn)]).astype(np.float32)
        q = np.arange(self.quarter)
        mixes = []
        for r in range(4):
            angle = 2.0 * np.pi * (q[:, None] * (4 * q[None, :] + r) % side) / side
            cos, sin = np.cos(angle), np.sin(angle)
            mixes.append(np.block([[cos, -sin], [sin, cos]]))
        self.mix = high_low(np.stack(mixes))
        self.row_tile = next(t for t in (176, 264, 16, 8) if self.rows % t == 0)


def split_terms(values):
    high = values.astype(jnp.bfloat16)
    return high, (values - high.astype(jnp.float32)).astype(jnp.bfloat16)


def dot_in(table, rows, high, low):
    dot = functools.partial(jnp.dot, preferred_element_type=jnp.float32)
    first, second = table[0, rows], table[1, rows]
    return dot(first, high) + (dot(first, low) + dot(second, high))


def block_views(plan, owners, me, blocks, values):
    size = plan.side // owners
    for step in range(owners):
        at = pl.multiple_of((me[0] ^ step) * size, size)
        yield blocks[step].at[pl.ds(0, size)], values.at[pl.ds(at, size)]


def tile_views(plan, grid, me, tiles, values):
    parts, rows, cols = grid
    block = plan.side // (rows * cols)
    height = block // parts
    own_row = me[0] // cols
    for part in range(parts):
        for col in range(cols):
            for i in range(rows):
                at = ((own_row ^ i) * cols + col) * block + part * height
                yield tiles[0].at[part * cols + col, i], values.at[pl.ds(pl.multiple_of(at, height), height)]


def start_all(pairs, sems):
    copies = [pltpu.make_async_copy(source, to, sems.at[i]) for i, (source, to) in enumerate(pairs)]
    for copy in copies:
        copy.start()
    return copies


def wait_all(copies):
    for copy in copies:
        copy.wait()


def to_spectrum(plan, values, into_even, into_odd, turn, mix, spec, mid):
    side, half, quarter = plan.side, plan.half, plan.quarter

    @pl.loop(0, side // quarter)
    def columns(tile):
        cols = pl.ds(pl.multiple_of(tile * quarter, quarter), quarter)
        top, bottom = values[pl.ds(0, half), cols], values[pl.ds(half, half), cols]
        for first, count, table, part in (
            (0, plan.evens, into_even, top + bottom),
            (plan.evens, plan.odds, into_odd, top - bottom),
        ):
            out = dot_in(table, slice(None), *split_terms(part))
            real, imag = out[:count], out[count:]
            rows = pl.ds(first, count)
            cos, sin = turn[0, rows, cols], turn[1, rows, cols]
            mid[0, rows, cols] = real * cos + imag * sin
            mid[1, rows, cols] = imag * cos - real * sin

    @pl.loop(0, plan.rows // plan.row_tile)
    def rows_loop(tile):
        rows = pl.ds(pl.multiple_of(tile * plan.row_tile, plan.row_tile), plan.row_tile)
        real = [mid[0, rows, pl.ds(j * quarter, quarter)] for j in range(4)]
        imag = [mid[1, rows, pl.ds(j * quarter, quarter)] for j in range(4)]
        sum_r, sum_i = real[0] + real[2], imag[0] + imag[2]
        dif_r, dif_i = real[0] - real[2], imag[0] - imag[2]
        two_r, two_i = real[1] + real[3], imag[1] + imag[3]
        odd_r, odd_i = real[1] - real[3], imag[1] - imag[3]
        turns = (
            (sum_r + two_r, sum_i + two_i),
            (dif_r + odd_i, dif_i - odd_r),
            (sum_r - two_r, sum_i - two_i),
            (dif_r - odd_i, dif_i + odd_r),
        )
        dot = functools.partial(jnp.dot, preferred_element_type=jnp.float32)
        for r, pair in enumerate(turns):
            high, low = split_terms(jnp.concatenate(pair, axis=1))
            out = dot(high, mix[0, r]) + (dot(low, mix[0, r]) + dot(high, mix[1, r]))
            cols = pl.ds(r * quarter, quarter)
            spec[0, rows, cols] = out[:, :quarter]
            spec[1, rows, cols] = out[:, quarter:]


def inverse_rows(plan, conjugate, left, right, turn, mix, mid):
    quarter = plan.quarter

    @pl.loop(0, plan.rows // plan.row_tile)
    def rows_loop(tile):
        rows = pl.ds(pl.multiple_of(tile * plan.row_tile, plan.row_tile), plan.row_tile)
        real, imag = [], []
        for r in range(4):
            cols = pl.ds(r * quarter, quarter)
            left_r, left_i = left[0, rows, cols], left[1, rows, cols]
            right_r, right_i = right[0, rows, cols], right[1, rows, cols]
            if conjugate:
                left_i = -left_i
            pair = (left_r * right_r - left_i * right_i, left_r * right_i + left_i * right_r)
            high, low = split_terms(jnp.concatenate(pair, axis=1))

            def dot(part, table):
                return lax.dot_general(
                    part, table, (((1,), (1,)), ((), ())), preferred_element_type=jnp.float32
                )

            out = dot(high, mix[0, r]) + (dot(low, mix[0, r]) + dot(high, mix[1, r]))
            real.append(out[:, :quarter])
            imag.append(out[:, quarter:])
        sum_r, sum_i = real[0] + real[2], imag[0] + imag[2]
        dif_r, dif_i = real[0] - real[2], imag[0] - imag[2]
        two_r, two_i = real[1] + real[3], imag[1] + imag[3]
        odd_r, odd_i = real[1] - real[3], imag[1] - imag[3]
        turns = (
            (sum_r + two_r, sum_i + two_i),
            (dif_r - odd_i, dif_i + odd_r),
            (sum_r - two_r, sum_i - two_i),
            (dif_r + odd_i, dif_i - odd_r),
        )
        for j, (got_r, got_i) in enumerate(turns):
            cols = pl.ds(j * quarter, quarter)
            cos, sin = turn[0, rows, cols], turn[1, rows, cols]
            mid[0, rows, cols] = got_r * cos - got_i * sin
            mid[1, rows, cols] = got_r * sin + got_i * cos


def inverse_columns(plan, back_even, back_odd, mid, values):
    side, half, quarter = plan.side, plan.half, plan.quarter

    @pl.loop(0, side // quarter)
    def columns(tile):
        cols = pl.ds(pl.multiple_of(tile * quarter, quarter), quarter)
        even = [mid[0, pl.ds(0, plan.evens), cols], mid[1, pl.ds(0, plan.evens), cols]]
        if plan.even_depth > 2 * plan.evens:
            even.append(jnp.zeros((plan.even_depth - 2 * plan.evens, quarter), jnp.float32))
        odd = [mid[0, pl.ds(plan.evens, plan.odds), cols], mid[1, pl.ds(plan.evens, plan.odds), cols]]
        from_even = dot_in(back_even, slice(None), *split_terms(jnp.concatenate(even)))
        from_odd = dot_in(back_odd, slice(None), *split_terms(jnp.concatenate(odd)))
        values[pl.ds(0, half), cols] = from_even + from_odd
        values[pl.ds(half, half), cols] = from_even - from_odd


def filter_kernel(plan, views, count, me, *refs):
    tiles = refs[:count]
    into_even, into_odd, turn, mix, spec, values, mid, sems = refs[count:]
    wait_all(start_all(views(me, tiles, values), sems))
    to_spectrum(plan, values, into_even, into_odd, turn, mix, spec, mid)


def conv_kernel(plan, views, count, me, filt, *refs):
    blocks, tables = refs[:count], refs[count : count + 6]
    into_even, into_odd, back_even, back_odd, turn, mix = tables
    spec, outs = refs[count + 6], refs[count + 7 : 2 * count + 7]
    values, mid, sems = refs[2 * count + 7 :]
    wait_all(start_all(views(me, blocks, values), sems))
    to_spectrum(plan, values, into_even, into_odd, turn, mix, spec, mid)
    inverse_rows(plan, False, filt, spec, turn, mix, mid)
    inverse_columns(plan, back_even, back_odd, mid, values)
    wait_all(start_all(((to, source) for source, to in views(me, outs, values)), sems))


def term_kernel(plan, views, term_views, count, me, gated, *refs):
    blocks, tables = refs[:count], refs[count : count + 6]
    into_even, into_odd, back_even, back_odd, turn, mix = tables
    spec, term, values, mid, sems, term_sems = refs[count + 6 :]
    wait_all(start_all(views(me, blocks, values), sems))
    to_spectrum(plan, values, into_even, into_odd, turn, mix, spec, mid)
    inverse_rows(plan, True, gated, spec, turn, mix, mid)
    inverse_columns(plan, back_even, back_odd, mid, values)
    wait_all(start_all(((to, source) for source, to in term_views(me, [term], values)), term_sems))


def grad_kernel(plan, views, count, me, filt, spec, back_even, back_odd, turn, mix, *refs):
    outs = refs[:count]
    values, mid, sems = refs[count:]
    inverse_rows(plan, True, filt, spec, turn, mix, mid)
    inverse_columns(plan, back_even, back_odd, mid, values)
    wait_all(start_all(((to, source) for source, to in views(me, outs, values)), sems))


def smem():
    return pl.BlockSpec(memory_space=pltpu.SMEM)


def vmem():
    return pl.BlockSpec(memory_space=pltpu.VMEM)


def anywhere():
    return pl.BlockSpec(memory_space=pl.ANY)


def kernel_cost(plan):
    return pl.CostEstimate(flops=plan.side**2, bytes_accessed=plan.side**2, transcendentals=0)


def call_kernel(plan, kernel, name, args, in_specs, out_shape, out_specs, scratch):
    return pl.pallas_call(
        kernel,
        out_shape=out_shape,
        in_specs=in_specs,
        out_specs=out_specs,
        scratch_shapes=scratch,
        compiler_params=pltpu.CompilerParams(vmem_limit_bytes=VMEM_LIMIT),
        cost_estimate=kernel_cost(plan),
        name=name,
    )(*args)


def float_array(shape):
    return jax.ShapeDtypeStruct(shape, jnp.float32)


def filter_spectrum(plan, me, tiles, views, copies):
    shape = (2, plan.rows, plan.side)
    return call_kernel(
        plan,
        functools.partial(filter_kernel, plan, views, len(tiles)),
        "filter_spectrum",
        (me, *tiles, plan.into_even, plan.into_odd, plan.turn, plan.mix),
        [smem()] + [anywhere()] * len(tiles) + [vmem()] * 4,
        float_array(shape),
        vmem(),
        [
            pltpu.VMEM((plan.side, plan.side), jnp.float32),
            pltpu.VMEM(shape, jnp.float32),
            pltpu.SemaphoreType.DMA((copies,)),
        ],
    )


def tables_of(plan):
    return (plan.into_even, plan.into_odd, plan.back_even, plan.back_odd, plan.turn, plan.mix)


def conv_of(plan, me, filt, blocks, views):
    count = len(blocks)
    shape = (2, plan.rows, plan.side)
    spec, *outs = call_kernel(
        plan,
        functools.partial(conv_kernel, plan, views, count),
        "conv_of",
        (me, filt, *blocks, *tables_of(plan)),
        [smem(), vmem()] + [vmem()] * count + [vmem()] * 6,
        [float_array(shape)] + [float_array((plan.side // count, plan.side))] * count,
        [vmem()] * (count + 1),
        [
            pltpu.VMEM((plan.side, plan.side), jnp.float32),
            pltpu.VMEM(shape, jnp.float32),
            pltpu.SemaphoreType.DMA((count,)),
        ],
    )
    return spec, outs


def term_of(plan, me, gated, blocks, views, term_shape, term_views):
    count = len(blocks)
    shape = (2, plan.rows, plan.side)
    return call_kernel(
        plan,
        functools.partial(term_kernel, plan, views, term_views, count),
        "term_of",
        (me, gated, *blocks, *tables_of(plan)),
        [smem(), vmem()] + [vmem()] * count + [vmem()] * 6,
        [float_array(shape), float_array(term_shape)],
        [vmem(), anywhere()],
        [
            pltpu.VMEM((plan.side, plan.side), jnp.float32),
            pltpu.VMEM(shape, jnp.float32),
            pltpu.SemaphoreType.DMA((count,)),
            pltpu.SemaphoreType.DMA((math.prod(term_shape[:2]),)),
        ],
    )


def grad_of(plan, me, filt, spec, count, views):
    return call_kernel(
        plan,
        functools.partial(grad_kernel, plan, views, count),
        "grad_of",
        (me, filt, spec, *tables_of(plan)[2:]),
        [smem()] + [vmem()] * 6,
        [float_array((plan.side // count, plan.side))] * count,
        [vmem()] * count,
        [
            pltpu.VMEM((plan.side, plan.side), jnp.float32),
            pltpu.VMEM((2, plan.rows, plan.side), jnp.float32),
            pltpu.SemaphoreType.DMA((count,)),
        ],
    )


def pairwise(block, axis, step):
    return lax.ppermute(block, axis, [(i, i ^ step) for i in range(lax.axis_size(axis))])


def after(first, then):
    return lax.optimization_barrier((first, then))[1]


def gate_kernel(steps, gates, me, *refs):
    count = len(steps)
    blocks = refs[:count]
    ins = refs[count : count + gates]
    outs, got, sems = refs[-gates - 2 : -2], refs[-2], refs[-1]
    here = pl.program_id(0)

    def copy_of(i):
        return pltpu.make_async_copy(blocks[i], got.at[i], sems.at[i])

    @pl.when(here == 0)
    def start():
        for i in range(count):
            copy_of(i).start()

    for i in range(count):

        @pl.when(here == i)
        def wait():
            copy_of(i).wait()

    values = got[here]
    for gate, out in zip(ins, outs):
        out[0] = (gate[0].astype(jnp.float32) * values).astype(jnp.bfloat16)


def gated_by(me, steps, blocks, gates, done=()):
    count = len(steps)
    shape = gates[0].shape

    def place(i, me):
        step = steps[-1]
        for j in range(count - 1):
            step = jnp.where(i == j, steps[j], step)
        return (me[0] ^ step, 0, 0)

    spec = pl.BlockSpec((1,) + shape[1:], place)
    size = count * shape[1] * shape[2]
    first_done = 1 + count + len(gates)
    return pl.pallas_call(
        functools.partial(gate_kernel, steps, len(gates)),
        grid_spec=pltpu.PrefetchScalarGridSpec(
            num_scalar_prefetch=1,
            grid=(count,),
            in_specs=[anywhere()] * count + [spec] * len(gates) + [anywhere()] * len(done),
            out_specs=[spec] * len(gates),
            scratch_shapes=[
                pltpu.VMEM((count,) + shape[1:], jnp.float32),
                pltpu.SemaphoreType.DMA((count,)),
            ],
        ),
        out_shape=[jax.ShapeDtypeStruct(shape, jnp.bfloat16)] * len(gates),
        input_output_aliases={first_done + i: i for i in range(len(done))},
        compiler_params=pltpu.CompilerParams(vmem_limit_bytes=VMEM_LIMIT),
        cost_estimate=pl.CostEstimate(
            flops=size * len(gates), bytes_accessed=4 * size * (1 + len(gates)), transcendentals=0
        ),
        name="gate_out",
    )(me, *blocks, *gates, *done)


def send_order(owners, cols):
    far = sorted(range(owners // 2, owners), key=lambda s: (-s // cols, -s))
    near = sorted(range(1, owners // 2), key=lambda s: (s % cols, -s))
    return far, near


def channel_shards(outer_gate, inner_gate, signal, grad_out, filter_weight):
    block, side = filter_weight.shape
    plan = Plan(side)
    parts, rows, cols = (lax.axis_size(name) for name in ("dp", "row", "col"))
    owners = rows * cols
    place = own_block()
    me = jnp.reshape(place, (1,)).astype(jnp.int32)
    far, near = send_order(owners, cols)
    order = far[:2]
    for i in range(2, len(far)):
        order = order + near[i - 2 : i - 1] + far[i : i + 1]
    order = order[:-1] + near[len(far) - 2 :] + order[-1:]
    last_order = far + near
    by_block = functools.partial(block_views, plan, owners)
    by_tile = functools.partial(tile_views, plan, (parts, rows, cols))

    def gated_block(left, right, step):
        at = place ^ step
        return lax.dynamic_index_in_dim(left[0], at, 0, False).astype(
            jnp.float32
        ) * lax.dynamic_index_in_dim(right[0], at, 0, False).astype(jnp.float32)

    crossed, neared = [], []

    def exchange(blocks, what, order, deep=3, near_wait=0):
        got = [blocks[0]] + [None] * (owners - 1)
        before, near_before = len(crossed), list(neared)
        neared.clear()
        for step in order:
            mine, waits = blocks[step], []
            if step in far:
                waits = crossed[max(0, len(crossed) - deep - 1) : max(0, len(crossed) - deep + 1)]
                if len(crossed) - before >= len(far) // 2:
                    waits = waits + near_before
            elif before:
                waits = crossed[before - 1 + near_wait : before + near_wait]
            if waits:
                mine = after(waits, mine)
            with jax.named_scope(f"{what}_{step}"):
                got[step] = pairwise(mine, ("row", "col"), step)
            (crossed if step in far else neared).append(got[step])
        return got

    height = block // parts
    own_part = lax.dynamic_slice_in_dim(filter_weight, lax.axis_index("dp") * height, height, 0)
    own_part = own_part * (1.0 / side)
    inner, values = inner_gate, signal
    gated = [None] * owners
    for step in order + [0]:
        gated[step] = gated_block(inner, values, step)
        if step and step % cols == 0:
            gated[step] = jnp.concatenate([gated[step], own_part])
        if step == order[0]:
            inner, values = after(gated[step], [inner_gate, signal])
    gated = exchange(gated, "gated", order)
    over_row = jnp.stack([own_part] + [gated[i * cols][block:] for i in range(1, rows)])
    grad_conv = [gated_block(grad_out, outer_gate, step) for step in range(owners)]
    over_row = after(gated + grad_conv, over_row)
    over_all = [lax.all_gather(over_row, ("dp", "col"))]
    filt = filter_spectrum(plan, me, over_all, by_tile, parts * owners)

    got = exchange(grad_conv, "grad_conv", [step for step in order if step != near[-1]], 4)
    spec, conv_out = conv_of(plan, me, filt, after([filt] + [got[step] for step in far[:1]], gated), by_block)
    with jax.named_scope(f"grad_conv_{near[-1]}"):
        got[near[-1]] = pairwise(after(conv_out[0], grad_conv[near[-1]]), ("row", "col"), near[-1])
    grad_conv = got
    conv = exchange(conv_out, "conv", order, 4)
    tile_shape = (parts * cols, rows, height, side)
    cot, term = term_of(plan, me, spec, grad_conv, by_block, tile_shape, by_tile)
    back_out = grad_of(plan, me, filt, cot, owners, by_block)
    grad_gated = exchange(back_out, "grad_gated", last_order, 3, 2)

    term = after([conv[step] for step in far[:2]], term)
    term = lax.psum_scatter(term, ("dp", "col"), scatter_dimension=0, tiled=False)
    with jax.named_scope("rows_sum"):
        arrived = [pairwise(term[i], "row", i) for i in range(1, rows)]
    total = sum(arrived, term[0]) * (1.0 / side)
    every = [0] + order
    (grad_outer,) = gated_by(me, every, [conv[step] for step in every], [grad_out[0]])
    total = after(grad_outer, total)
    with jax.named_scope("parts_gather"):
        others = [pairwise(total, "dp", i) for i in range(1, parts)]
    pieces = jnp.stack([total] + others)
    bit = 1
    while bit < parts:
        upper = (lax.axis_index("dp") & bit) != 0
        swapped = jnp.flip(pieces.reshape(parts // (2 * bit), 2, bit, height, side), 1)
        pieces = jnp.where(upper, swapped.reshape(pieces.shape), pieces)
        bit *= 2
    grad_filter = pieces.reshape(block, side)

    every = [0] + far + near[::-1]
    gates = [signal[0], inner_gate[0]]
    early, late = every[:-1], every[-1:]
    done = gated_by(me, early, [grad_gated[step] for step in early], gates)
    grad_inner, grad_signal = gated_by(me, late, [grad_gated[step] for step in late], gates, done)
    return (grad_outer[None], grad_inner[None], grad_signal[None], grad_filter)


def powers_of_two(*sizes):
    return all(size & (size - 1) == 0 for size in sizes)


def shards(*arrays):
    parts, rows, cols = (lax.axis_size(name) for name in ("dp", "row", "col"))
    side = arrays[0].shape[3]
    whole = arrays[0].shape[1] == rows * cols and rows >= 2 and cols == 2
    fits = powers_of_two(parts, rows, cols, side) and side // 4 % LANE_PAD == 0
    fits = fits and arrays[4].shape[0] // parts % ROW_PAD == 0
    return (channel_shards if whole and fits else spread_shards)(*arrays)


def solution(mesh):
    placed = (
        P("dp", None, ("row", "col"), None),
        P("dp", None, ("row", "col"), None),
        P("dp", None, ("row", "col"), None),
        P("dp", None, ("row", "col"), None),
        P(("row", "col"), None),
    )
    return jax.shard_map(
        shards,
        mesh=mesh,
        in_specs=placed,
        out_specs=(
            P("dp", None, ("row", "col"), None),
            P("dp", None, ("row", "col"), None),
            P("dp", None, ("row", "col"), None),
            P(("row", "col"), None),
        ),
        check_vma=False,
    )
```

```python
import functools
import math

import jax
import jax.numpy as jnp
import numpy as np
from jax import lax
from jax.experimental import pallas as pl
from jax.experimental.pallas import tpu as pltpu
from jax.sharding import PartitionSpec as P

TWO_PI = 2.0 * math.pi


def contract(form, left, right):
    return jnp.einsum(
        form, left, right, precision=lax.Precision.HIGHEST, preferred_element_type=jnp.float32
    )


def redistribute(blocks):
    return lax.all_to_all(blocks, ("row", "col"), split_axis=0, concat_axis=0, tiled=True)


def own_block():
    return lax.axis_index("row") * lax.axis_size("col") + lax.axis_index("col")


def turn_angles(first_index, second_index, total):
    product = first_index * second_index % total
    angles = product.astype(jnp.float32) * (TWO_PI / total)
    return (jnp.cos(angles), jnp.sin(angles))


def axis_dft(real, imag, sign):
    length, width = real.shape
    first = 1 << (length.bit_length() - 1) // 2
    second = length // first
    index_a = jnp.arange(first, dtype=jnp.int32)
    index_b = jnp.arange(second, dtype=jnp.int32)
    cos_a, sin_a = turn_angles(index_a[:, None], index_a[None, :], first)
    sin_a = sign * sin_a
    cos_b, sin_b = turn_angles(index_b[:, None], index_b[None, :], second)
    sin_b = sign * sin_b
    twist_cos, twist_sin = turn_angles(index_a[:, None], index_b[None, :], length)
    twist_cos = twist_cos[:, :, None]
    twist_sin = sign * twist_sin[:, :, None]
    real_three = real.reshape(first, second, width)
    step_real = contract("abm,ak->kbm", real_three, cos_a)
    step_imag = contract("abm,ak->kbm", real_three, sin_a)
    if imag is not None:
        imag_three = imag.reshape(first, second, width)
        step_real = step_real - contract("abm,ak->kbm", imag_three, sin_a)
        step_imag = step_imag + contract("abm,ak->kbm", imag_three, cos_a)
    turned_real = step_real * twist_cos - step_imag * twist_sin
    turned_imag = step_real * twist_sin + step_imag * twist_cos
    out_real = contract("kbm,bj->jkm", turned_real, cos_b) - contract(
        "kbm,bj->jkm", turned_imag, sin_b
    )
    out_imag = contract("kbm,bj->jkm", turned_real, sin_b) + contract(
        "kbm,bj->jkm", turned_imag, cos_b
    )
    return (out_real.reshape(length, width), out_imag.reshape(length, width))


def forward(stacked, order):
    count, block, grid_side = stacked.shape
    owners = grid_side // block
    total = grid_side * grid_side
    send = jnp.transpose(stacked.reshape(count, block, owners, block), (2, 1, 0, 3)).reshape(
        owners, block, count * block
    )
    columns = redistribute(send).reshape(grid_side, count * block)
    first_real, first_imag = axis_dft(columns, None, -1.0)
    first_real = first_real.reshape(grid_side, count, block)
    first_imag = first_imag.reshape(grid_side, count, block)
    col_index = own_block() * block + jnp.arange(block, dtype=jnp.int32)
    cos_turn, sin_turn = turn_angles(order[:, None, None], col_index[None, None, :], total)
    turned_real = first_real * cos_turn + first_imag * sin_turn
    turned_imag = first_imag * cos_turn - first_real * sin_turn
    send_two = jnp.concatenate([turned_real, turned_imag], axis=1).reshape(
        owners, block, 2 * count * block
    )
    gotten = redistribute(send_two).reshape(owners, block, 2 * count, block)
    flat_real = jnp.transpose(gotten[:, :, :count, :], (0, 3, 1, 2)).reshape(
        grid_side, block * count
    )
    flat_imag = jnp.transpose(gotten[:, :, count:, :], (0, 3, 1, 2)).reshape(
        grid_side, block * count
    )
    out_real, out_imag = axis_dft(flat_real, flat_imag, -1.0)
    spec_real = jnp.transpose(out_real.reshape(grid_side, block, count), (1, 2, 0))
    spec_imag = jnp.transpose(out_imag.reshape(grid_side, block, count), (1, 2, 0))
    return (spec_real, spec_imag)


def inverse(spec_real, spec_imag, order):
    block, count, grid_side = spec_real.shape
    owners = grid_side // block
    total = grid_side * grid_side
    flat_real = jnp.transpose(spec_real, (2, 0, 1)).reshape(grid_side, block * count)
    flat_imag = jnp.transpose(spec_imag, (2, 0, 1)).reshape(grid_side, block * count)
    out_real, out_imag = axis_dft(flat_real, flat_imag, 1.0)
    back_real = jnp.transpose(out_real.reshape(owners, block, block, count), (0, 2, 3, 1))
    back_imag = jnp.transpose(out_imag.reshape(owners, block, block, count), (0, 2, 3, 1))
    freq_index = lax.dynamic_slice_in_dim(order, own_block() * block, block, 0)
    col_index = (
        jnp.arange(owners, dtype=jnp.int32)[:, None] * block
        + jnp.arange(block, dtype=jnp.int32)[None, :]
    )
    cos_turn, sin_turn = turn_angles(
        freq_index[None, :, None, None], col_index[:, None, None, :], total
    )
    turned_real = back_real * cos_turn - back_imag * sin_turn
    turned_imag = back_real * sin_turn + back_imag * cos_turn
    send = jnp.concatenate([turned_real, turned_imag], axis=2).reshape(
        owners, block, 2 * count * block
    )
    gotten = redistribute(send).reshape(grid_side, 2 * count * block)
    real_part = gotten[:, : count * block]
    imag_part = gotten[:, count * block :]
    full_real, full_imag = axis_dft(real_part, imag_part, 1.0)
    values = full_real * (1.0 / total)
    returned = redistribute(values.reshape(owners, block, count * block)).reshape(
        owners, block, count, block
    )
    return jnp.transpose(returned, (2, 1, 0, 3)).reshape(count, block, grid_side)


def spread_shards(outer_gate, inner_gate, signal, grad_out, filter_weight):
    grid_side = filter_weight.shape[1]
    freq_index = jnp.arange(grid_side, dtype=jnp.int32)
    outer_f = outer_gate[0].astype(jnp.float32)
    inner_f = inner_gate[0].astype(jnp.float32)
    signal_f = signal[0].astype(jnp.float32)
    grad_f = grad_out[0].astype(jnp.float32)
    channels = inner_f.shape[0]
    gated = inner_f * signal_f
    grad_conv = grad_f * outer_f
    taps = (filter_weight * (1.0 / grid_side))[None]
    spec_real, spec_imag = forward(jnp.concatenate([gated, grad_conv], axis=0), freq_index)
    filt_real, filt_imag = forward(taps, freq_index)
    gated_real = spec_real[:, :channels]
    gated_imag = spec_imag[:, :channels]
    cot_real = spec_real[:, channels : 2 * channels]
    cot_imag = spec_imag[:, channels : 2 * channels]
    conv_real = filt_real * gated_real - filt_imag * gated_imag
    conv_imag = filt_real * gated_imag + filt_imag * gated_real
    back_real = filt_real * cot_real + filt_imag * cot_imag
    back_imag = filt_real * cot_imag - filt_imag * cot_real
    term_real = jnp.sum(gated_real * cot_real + gated_imag * cot_imag, axis=1, keepdims=True)
    term_imag = jnp.sum(gated_real * cot_imag - gated_imag * cot_real, axis=1, keepdims=True)
    values = inverse(
        jnp.concatenate([conv_real, back_real, term_real], axis=1),
        jnp.concatenate([conv_imag, back_imag, term_imag], axis=1),
        freq_index,
    )
    grad_filter = lax.psum(values[2 * channels], "dp") * (1.0 / grid_side)
    conv = values[:channels]
    grad_gated = values[channels : 2 * channels]
    grad_outer = (grad_f * conv).astype(jnp.bfloat16)[None]
    grad_inner = (grad_gated * signal_f).astype(jnp.bfloat16)[None]
    grad_signal = (grad_gated * inner_f).astype(jnp.bfloat16)[None]
    return (grad_outer, grad_inner, grad_signal, grad_filter)


VMEM_LIMIT = 18 * 1024 * 1024
ROW_PAD = 16
LANE_PAD = 128


def up_to(value, unit):
    return -(-value // unit) * unit


def high_low(table):
    high = table.astype(jnp.bfloat16)
    low = (table - high.astype(np.float64)).astype(jnp.bfloat16)
    return np.stack([high, low])


class Plan:
    def __init__(self, side):
        half = side // 2
        self.side, self.half, self.quarter = side, half, side // 4
        self.evens = up_to(half // 2 + 1, ROW_PAD)
        self.odds = half // 2
        self.rows = self.evens + self.odds
        self.even_depth = up_to(2 * self.evens, LANE_PAD)
        total = side * side
        even_k = 2 * np.arange(self.evens)
        odd_k = 2 * np.arange(self.odds) + 1
        live = (even_k <= half).astype(np.float64)
        p = np.arange(half)

        def waves(k, scale):
            angle = 2.0 * np.pi * (k[:, None] * p[None, :] % side) / side
            return np.concatenate([np.cos(angle) * scale[:, None], -np.sin(angle) * scale[:, None]])

        ones = np.ones(self.odds)
        self.into_even = high_low(waves(even_k, live))
        self.into_odd = high_low(waves(odd_k, ones))
        weight = np.where((even_k == 0) | (even_k == half), 1.0, 2.0) * live / total
        back_even = np.zeros((half, self.even_depth))
        back_even[:, : 2 * self.evens] = waves(even_k, weight).T
        self.back_even = high_low(back_even)
        self.back_odd = high_low(waves(odd_k, ones * 2.0 / total).T)
        k = np.concatenate([even_k, odd_k])
        turn = 2.0 * np.pi * (k[:, None] * np.arange(side)[None, :] % total) / total
        self.turn = np.stack([np.cos(turn), np.sin(turn)]).astype(np.float32)
        q = np.arange(self.quarter)
        mixes = []
        for r in range(4):
            angle = 2.0 * np.pi * (q[:, None] * (4 * q[None, :] + r) % side) / side
            cos, sin = np.cos(angle), np.sin(angle)
            mixes.append(np.block([[cos, -sin], [sin, cos]]))
        self.mix = high_low(np.stack(mixes))
        self.row_tile = next(t for t in (176, 264, 16, 8) if self.rows % t == 0)


def split_terms(values):
    high = values.astype(jnp.bfloat16)
    return high, (values - high.astype(jnp.float32)).astype(jnp.bfloat16)


def dot_in(table, rows, high, low):
    dot = functools.partial(jnp.dot, preferred_element_type=jnp.float32)
    first, second = table[0, rows], table[1, rows]
    return dot(first, high) + (dot(first, low) + dot(second, high))


def block_views(plan, owners, me, blocks, values):
    size = plan.side // owners
    for step in range(owners):
        at = pl.multiple_of((me[0] ^ step) * size, size)
        yield blocks[step].at[pl.ds(0, size)], values.at[pl.ds(at, size)]


def tile_views(plan, grid, me, tiles, values):
    parts, rows, cols = grid
    block = plan.side // (rows * cols)
    height = block // parts
    own_row = me[0] // cols
    for part in range(parts):
        for col in range(cols):
            for i in range(rows):
                at = ((own_row ^ i) * cols + col) * block + part * height
                yield tiles[0].at[part * cols + col, i], values.at[pl.ds(pl.multiple_of(at, height), height)]


def start_all(pairs, sems):
    copies = [pltpu.make_async_copy(source, to, sems.at[i]) for i, (source, to) in enumerate(pairs)]
    for copy in copies:
        copy.start()
    return copies


def wait_all(copies):
    for copy in copies:
        copy.wait()


def to_spectrum(plan, values, into_even, into_odd, turn, mix, spec, mid):
    side, half, quarter = plan.side, plan.half, plan.quarter

    @pl.loop(0, side // quarter)
    def columns(tile):
        cols = pl.ds(pl.multiple_of(tile * quarter, quarter), quarter)
        top, bottom = values[pl.ds(0, half), cols], values[pl.ds(half, half), cols]
        for first, count, table, part in (
            (0, plan.evens, into_even, top + bottom),
            (plan.evens, plan.odds, into_odd, top - bottom),
        ):
            out = dot_in(table, slice(None), *split_terms(part))
            real, imag = out[:count], out[count:]
            rows = pl.ds(first, count)
            cos, sin = turn[0, rows, cols], turn[1, rows, cols]
            mid[0, rows, cols] = real * cos + imag * sin
            mid[1, rows, cols] = imag * cos - real * sin

    @pl.loop(0, plan.rows // plan.row_tile)
    def rows_loop(tile):
        rows = pl.ds(pl.multiple_of(tile * plan.row_tile, plan.row_tile), plan.row_tile)
        real = [mid[0, rows, pl.ds(j * quarter, quarter)] for j in range(4)]
        imag = [mid[1, rows, pl.ds(j * quarter, quarter)] for j in range(4)]
        sum_r, sum_i = real[0] + real[2], imag[0] + imag[2]
        dif_r, dif_i = real[0] - real[2], imag[0] - imag[2]
        two_r, two_i = real[1] + real[3], imag[1] + imag[3]
        odd_r, odd_i = real[1] - real[3], imag[1] - imag[3]
        turns = (
            (sum_r + two_r, sum_i + two_i),
            (dif_r + odd_i, dif_i - odd_r),
            (sum_r - two_r, sum_i - two_i),
            (dif_r - odd_i, dif_i + odd_r),
        )
        dot = functools.partial(jnp.dot, preferred_element_type=jnp.float32)
        for r, pair in enumerate(turns):
            high, low = split_terms(jnp.concatenate(pair, axis=1))
            out = dot(high, mix[0, r]) + (dot(low, mix[0, r]) + dot(high, mix[1, r]))
            cols = pl.ds(r * quarter, quarter)
            spec[0, rows, cols] = out[:, :quarter]
            spec[1, rows, cols] = out[:, quarter:]


def inverse_rows(plan, conjugate, left, right, turn, mix, mid):
    quarter = plan.quarter

    @pl.loop(0, plan.rows // plan.row_tile)
    def rows_loop(tile):
        rows = pl.ds(pl.multiple_of(tile * plan.row_tile, plan.row_tile), plan.row_tile)
        real, imag = [], []
        for r in range(4):
            cols = pl.ds(r * quarter, quarter)
            left_r, left_i = left[0, rows, cols], left[1, rows, cols]
            right_r, right_i = right[0, rows, cols], right[1, rows, cols]
            if conjugate:
                left_i = -left_i
            pair = (left_r * right_r - left_i * right_i, left_r * right_i + left_i * right_r)
            high, low = split_terms(jnp.concatenate(pair, axis=1))

            def dot(part, table):
                return lax.dot_general(
                    part, table, (((1,), (1,)), ((), ())), preferred_element_type=jnp.float32
                )

            out = dot(high, mix[0, r]) + (dot(low, mix[0, r]) + dot(high, mix[1, r]))
            real.append(out[:, :quarter])
            imag.append(out[:, quarter:])
        sum_r, sum_i = real[0] + real[2], imag[0] + imag[2]
        dif_r, dif_i = real[0] - real[2], imag[0] - imag[2]
        two_r, two_i = real[1] + real[3], imag[1] + imag[3]
        odd_r, odd_i = real[1] - real[3], imag[1] - imag[3]
        turns = (
            (sum_r + two_r, sum_i + two_i),
            (dif_r - odd_i, dif_i + odd_r),
            (sum_r - two_r, sum_i - two_i),
            (dif_r + odd_i, dif_i - odd_r),
        )
        for j, (got_r, got_i) in enumerate(turns):
            cols = pl.ds(j * quarter, quarter)
            cos, sin = turn[0, rows, cols], turn[1, rows, cols]
            mid[0, rows, cols] = got_r * cos - got_i * sin
            mid[1, rows, cols] = got_r * sin + got_i * cos


def inverse_columns(plan, back_even, back_odd, mid, values):
    side, half, quarter = plan.side, plan.half, plan.quarter

    @pl.loop(0, side // quarter)
    def columns(tile):
        cols = pl.ds(pl.multiple_of(tile * quarter, quarter), quarter)
        even = [mid[0, pl.ds(0, plan.evens), cols], mid[1, pl.ds(0, plan.evens), cols]]
        if plan.even_depth > 2 * plan.evens:
            even.append(jnp.zeros((plan.even_depth - 2 * plan.evens, quarter), jnp.float32))
        odd = [mid[0, pl.ds(plan.evens, plan.odds), cols], mid[1, pl.ds(plan.evens, plan.odds), cols]]
        from_even = dot_in(back_even, slice(None), *split_terms(jnp.concatenate(even)))
        from_odd = dot_in(back_odd, slice(None), *split_terms(jnp.concatenate(odd)))
        values[pl.ds(0, half), cols] = from_even + from_odd
        values[pl.ds(half, half), cols] = from_even - from_odd


def filter_kernel(plan, views, count, me, *refs):
    tiles = refs[:count]
    into_even, into_odd, turn, mix, spec, values, mid, sems = refs[count:]
    wait_all(start_all(views(me, tiles, values), sems))
    to_spectrum(plan, values, into_even, into_odd, turn, mix, spec, mid)


def conv_kernel(plan, views, count, me, filt, *refs):
    blocks, tables = refs[:count], refs[count : count + 6]
    into_even, into_odd, back_even, back_odd, turn, mix = tables
    spec, outs = refs[count + 6], refs[count + 7 : 2 * count + 7]
    values, mid, sems = refs[2 * count + 7 :]
    wait_all(start_all(views(me, blocks, values), sems))
    to_spectrum(plan, values, into_even, into_odd, turn, mix, spec, mid)
    inverse_rows(plan, False, filt, spec, turn, mix, mid)
    inverse_columns(plan, back_even, back_odd, mid, values)
    wait_all(start_all(((to, source) for source, to in views(me, outs, values)), sems))


def term_kernel(plan, views, term_views, count, me, gated, *refs):
    blocks, tables = refs[:count], refs[count : count + 6]
    into_even, into_odd, back_even, back_odd, turn, mix = tables
    spec, term, values, mid, sems, term_sems = refs[count + 6 :]
    wait_all(start_all(views(me, blocks, values), sems))
    to_spectrum(plan, values, into_even, into_odd, turn, mix, spec, mid)
    inverse_rows(plan, True, gated, spec, turn, mix, mid)
    inverse_columns(plan, back_even, back_odd, mid, values)
    wait_all(start_all(((to, source) for source, to in term_views(me, [term], values)), term_sems))


def grad_kernel(plan, views, count, me, filt, spec, back_even, back_odd, turn, mix, *refs):
    outs = refs[:count]
    values, mid, sems = refs[count:]
    inverse_rows(plan, True, filt, spec, turn, mix, mid)
    inverse_columns(plan, back_even, back_odd, mid, values)
    wait_all(start_all(((to, source) for source, to in views(me, outs, values)), sems))


def smem():
    return pl.BlockSpec(memory_space=pltpu.SMEM)


def vmem():
    return pl.BlockSpec(memory_space=pltpu.VMEM)


def anywhere():
    return pl.BlockSpec(memory_space=pl.ANY)


def kernel_cost(plan):
    return pl.CostEstimate(flops=plan.side**2, bytes_accessed=plan.side**2, transcendentals=0)


def call_kernel(plan, kernel, name, args, in_specs, out_shape, out_specs, scratch):
    return pl.pallas_call(
        kernel,
        out_shape=out_shape,
        in_specs=in_specs,
        out_specs=out_specs,
        scratch_shapes=scratch,
        compiler_params=pltpu.CompilerParams(vmem_limit_bytes=VMEM_LIMIT),
        cost_estimate=kernel_cost(plan),
        name=name,
    )(*args)


def float_array(shape):
    return jax.ShapeDtypeStruct(shape, jnp.float32)


def filter_spectrum(plan, me, tiles, views, copies):
    shape = (2, plan.rows, plan.side)
    return call_kernel(
        plan,
        functools.partial(filter_kernel, plan, views, len(tiles)),
        "filter_spectrum",
        (me, *tiles, plan.into_even, plan.into_odd, plan.turn, plan.mix),
        [smem()] + [anywhere()] * len(tiles) + [vmem()] * 4,
        float_array(shape),
        vmem(),
        [
            pltpu.VMEM((plan.side, plan.side), jnp.float32),
            pltpu.VMEM(shape, jnp.float32),
            pltpu.SemaphoreType.DMA((copies,)),
        ],
    )


def tables_of(plan):
    return (plan.into_even, plan.into_odd, plan.back_even, plan.back_odd, plan.turn, plan.mix)


def conv_of(plan, me, filt, blocks, views):
    count = len(blocks)
    shape = (2, plan.rows, plan.side)
    spec, *outs = call_kernel(
        plan,
        functools.partial(conv_kernel, plan, views, count),
        "conv_of",
        (me, filt, *blocks, *tables_of(plan)),
        [smem(), vmem()] + [vmem()] * count + [vmem()] * 6,
        [float_array(shape)] + [float_array((plan.side // count, plan.side))] * count,
        [vmem()] * (count + 1),
        [
            pltpu.VMEM((plan.side, plan.side), jnp.float32),
            pltpu.VMEM(shape, jnp.float32),
            pltpu.SemaphoreType.DMA((count,)),
        ],
    )
    return spec, outs


def term_of(plan, me, gated, blocks, views, term_shape, term_views):
    count = len(blocks)
    shape = (2, plan.rows, plan.side)
    return call_kernel(
        plan,
        functools.partial(term_kernel, plan, views, term_views, count),
        "term_of",
        (me, gated, *blocks, *tables_of(plan)),
        [smem(), vmem()] + [vmem()] * count + [vmem()] * 6,
        [float_array(shape), float_array(term_shape)],
        [vmem(), anywhere()],
        [
            pltpu.VMEM((plan.side, plan.side), jnp.float32),
            pltpu.VMEM(shape, jnp.float32),
            pltpu.SemaphoreType.DMA((count,)),
            pltpu.SemaphoreType.DMA((math.prod(term_shape[:2]),)),
        ],
    )


def grad_of(plan, me, filt, spec, count, views):
    return call_kernel(
        plan,
        functools.partial(grad_kernel, plan, views, count),
        "grad_of",
        (me, filt, spec, *tables_of(plan)[2:]),
        [smem()] + [vmem()] * 6,
        [float_array((plan.side // count, plan.side))] * count,
        [vmem()] * count,
        [
            pltpu.VMEM((plan.side, plan.side), jnp.float32),
            pltpu.VMEM((2, plan.rows, plan.side), jnp.float32),
            pltpu.SemaphoreType.DMA((count,)),
        ],
    )


def pairwise(block, axis, step):
    return lax.ppermute(block, axis, [(i, i ^ step) for i in range(lax.axis_size(axis))])


def after(first, then):
    return lax.optimization_barrier((first, then))[1]


def gate_kernel(steps, gates, me, *refs):
    count = len(steps)
    blocks = refs[:count]
    ins = refs[count : count + gates]
    outs, got, sems = refs[-gates - 2 : -2], refs[-2], refs[-1]
    here = pl.program_id(0)

    def copy_of(i):
        return pltpu.make_async_copy(blocks[i], got.at[i], sems.at[i])

    @pl.when(here == 0)
    def start():
        for i in range(count):
            copy_of(i).start()

    for i in range(count):

        @pl.when(here == i)
        def wait():
            copy_of(i).wait()

    values = got[here]
    for gate, out in zip(ins, outs):
        out[0] = (gate[0].astype(jnp.float32) * values).astype(jnp.bfloat16)


def gated_by(me, steps, blocks, gates, done=()):
    count = len(steps)
    shape = gates[0].shape

    def place(i, me):
        step = steps[-1]
        for j in range(count - 1):
            step = jnp.where(i == j, steps[j], step)
        return (me[0] ^ step, 0, 0)

    spec = pl.BlockSpec((1,) + shape[1:], place)
    size = count * shape[1] * shape[2]
    first_done = 1 + count + len(gates)
    return pl.pallas_call(
        functools.partial(gate_kernel, steps, len(gates)),
        grid_spec=pltpu.PrefetchScalarGridSpec(
            num_scalar_prefetch=1,
            grid=(count,),
            in_specs=[anywhere()] * count + [spec] * len(gates) + [anywhere()] * len(done),
            out_specs=[spec] * len(gates),
            scratch_shapes=[
                pltpu.VMEM((count,) + shape[1:], jnp.float32),
                pltpu.SemaphoreType.DMA((count,)),
            ],
        ),
        out_shape=[jax.ShapeDtypeStruct(shape, jnp.bfloat16)] * len(gates),
        input_output_aliases={first_done + i: i for i in range(len(done))},
        compiler_params=pltpu.CompilerParams(vmem_limit_bytes=VMEM_LIMIT),
        cost_estimate=pl.CostEstimate(
            flops=size * len(gates), bytes_accessed=4 * size * (1 + len(gates)), transcendentals=0
        ),
        name="gate_out",
    )(me, *blocks, *gates, *done)


def send_order(owners, cols):
    far = sorted(range(owners // 2, owners), key=lambda s: (-s // cols, -s))
    near = sorted(range(1, owners // 2), key=lambda s: (s % cols, -s))
    return far, near


def channel_shards(outer_gate, inner_gate, signal, grad_out, filter_weight):
    block, side = filter_weight.shape
    plan = Plan(side)
    parts, rows, cols = (lax.axis_size(name) for name in ("dp", "row", "col"))
    owners = rows * cols
    place = own_block()
    me = jnp.reshape(place, (1,)).astype(jnp.int32)
    far, near = send_order(owners, cols)
    order = far[:2]
    for i in range(2, len(far)):
        order = order + near[i - 2 : i - 1] + far[i : i + 1]
    order = order[:-1] + near[len(far) - 2 :] + order[-1:]
    last_order = far[:-1] + near + far[-1:]
    by_block = functools.partial(block_views, plan, owners)
    by_tile = functools.partial(tile_views, plan, (parts, rows, cols))

    def gated_block(left, right, step):
        at = place ^ step
        return lax.dynamic_index_in_dim(left[0], at, 0, False).astype(
            jnp.float32
        ) * lax.dynamic_index_in_dim(right[0], at, 0, False).astype(jnp.float32)

    crossed, neared = [], []

    def exchange(blocks, what, order, deep=3, near_wait=0):
        got = [blocks[0]] + [None] * (owners - 1)
        before, near_before = len(crossed), list(neared)
        neared.clear()
        for step in order:
            mine, waits = blocks[step], []
            if step in far:
                waits = crossed[max(0, len(crossed) - deep - 1) : max(0, len(crossed) - deep + 1)]
                if len(crossed) - before >= len(far) // 2:
                    waits = waits + near_before
            elif before:
                waits = crossed[before - 1 + near_wait : before + near_wait]
            if waits:
                mine = after(waits, mine)
            with jax.named_scope(f"{what}_{step}"):
                got[step] = pairwise(mine, ("row", "col"), step)
            (crossed if step in far else neared).append(got[step])
        return got

    height = block // parts
    own_part = lax.dynamic_slice_in_dim(filter_weight, lax.axis_index("dp") * height, height, 0)
    own_part = own_part * (1.0 / side)
    inner, values = inner_gate, signal
    gated = [None] * owners
    for step in order + [0]:
        gated[step] = gated_block(inner, values, step)
        if step and step % cols == 0:
            gated[step] = jnp.concatenate([gated[step], own_part])
        if step == order[0]:
            inner, values = after(gated[step], [inner_gate, signal])
    gated = exchange(gated, "gated", order)
    over_row = jnp.stack([own_part] + [gated[i * cols][block:] for i in range(1, rows)])
    grad_conv = [gated_block(grad_out, outer_gate, step) for step in range(owners)]
    over_row = after(gated + grad_conv, over_row)
    over_all = [lax.all_gather(over_row, ("dp", "col"))]
    filt = filter_spectrum(plan, me, over_all, by_tile, parts * owners)

    got = exchange(grad_conv, "grad_conv", [step for step in order if step != near[-1]], 4)
    spec, conv_out = conv_of(plan, me, filt, after([filt] + [got[step] for step in far[:1]], gated), by_block)
    with jax.named_scope(f"grad_conv_{near[-1]}"):
        got[near[-1]] = pairwise(after(conv_out[0], grad_conv[near[-1]]), ("row", "col"), near[-1])
    grad_conv = got
    conv = exchange(conv_out, "conv", order, 4)
    tile_shape = (parts * cols, rows, height, side)
    cot, term = term_of(plan, me, spec, grad_conv, by_block, tile_shape, by_tile)
    back_out = grad_of(plan, me, filt, cot, owners, by_block)
    term = after([conv[step] for step in far[:2]], term)
    term = lax.psum_scatter(term, ("dp", "col"), scatter_dimension=0, tiled=False)
    with jax.named_scope("rows_sum"):
        arrived = [pairwise(term[i], "row", i) for i in range(1, rows)]
    total = sum(arrived, term[0]) * (1.0 / side)
    back_out = list(back_out)
    for step in far[3:] + near:
        back_out[step] = after(total, back_out[step])
    grad_gated = exchange(back_out, "grad_gated", last_order, 3, 1)
    every = [0] + order
    (grad_outer,) = gated_by(me, every, [conv[step] for step in every], [grad_out[0]])
    total = after(grad_outer, total)
    with jax.named_scope("parts_gather"):
        others = [pairwise(total, "dp", i) for i in range(1, parts)]
    pieces = jnp.stack([total] + others)
    bit = 1
    while bit < parts:
        upper = (lax.axis_index("dp") & bit) != 0
        swapped = jnp.flip(pieces.reshape(parts // (2 * bit), 2, bit, height, side), 1)
        pieces = jnp.where(upper, swapped.reshape(pieces.shape), pieces)
        bit *= 2
    grad_filter = pieces.reshape(block, side)

    every = [0] + near + far
    gates = [signal[0], inner_gate[0]]
    early, late = every[:-1], every[-1:]
    done = gated_by(me, early, [grad_gated[step] for step in early], gates)
    grad_inner, grad_signal = gated_by(me, late, [grad_gated[step] for step in late], gates, done)
    return (grad_outer[None], grad_inner[None], grad_signal[None], grad_filter)


def powers_of_two(*sizes):
    return all(size & (size - 1) == 0 for size in sizes)


def shards(*arrays):
    parts, rows, cols = (lax.axis_size(name) for name in ("dp", "row", "col"))
    side = arrays[0].shape[3]
    whole = arrays[0].shape[1] == rows * cols and rows >= 2 and cols == 2
    fits = powers_of_two(parts, rows, cols, side) and side // 4 % LANE_PAD == 0
    fits = fits and arrays[4].shape[0] // parts % ROW_PAD == 0
    return (channel_shards if whole and fits else spread_shards)(*arrays)


def solution(mesh):
    placed = (
        P("dp", None, ("row", "col"), None),
        P("dp", None, ("row", "col"), None),
        P("dp", None, ("row", "col"), None),
        P("dp", None, ("row", "col"), None),
        P(("row", "col"), None),
    )
    return jax.shard_map(
        shards,
        mesh=mesh,
        in_specs=placed,
        out_specs=(
            P("dp", None, ("row", "col"), None),
            P("dp", None, ("row", "col"), None),
            P("dp", None, ("row", "col"), None),
            P(("row", "col"), None),
        ),
        check_vma=False,
    )
```

```python
import functools
import math

import jax
import jax.numpy as jnp
import numpy as np
from jax import lax
from jax.experimental import pallas as pl
from jax.experimental.pallas import tpu as pltpu
from jax.sharding import PartitionSpec as P

TWO_PI = 2.0 * math.pi


def contract(form, left, right):
    return jnp.einsum(
        form, left, right, precision=lax.Precision.HIGHEST, preferred_element_type=jnp.float32
    )


def redistribute(blocks):
    return lax.all_to_all(blocks, ("row", "col"), split_axis=0, concat_axis=0, tiled=True)


def own_block():
    return lax.axis_index("row") * lax.axis_size("col") + lax.axis_index("col")


def turn_angles(first_index, second_index, total):
    product = first_index * second_index % total
    angles = product.astype(jnp.float32) * (TWO_PI / total)
    return (jnp.cos(angles), jnp.sin(angles))


def axis_dft(real, imag, sign):
    length, width = real.shape
    first = 1 << (length.bit_length() - 1) // 2
    second = length // first
    index_a = jnp.arange(first, dtype=jnp.int32)
    index_b = jnp.arange(second, dtype=jnp.int32)
    cos_a, sin_a = turn_angles(index_a[:, None], index_a[None, :], first)
    sin_a = sign * sin_a
    cos_b, sin_b = turn_angles(index_b[:, None], index_b[None, :], second)
    sin_b = sign * sin_b
    twist_cos, twist_sin = turn_angles(index_a[:, None], index_b[None, :], length)
    twist_cos = twist_cos[:, :, None]
    twist_sin = sign * twist_sin[:, :, None]
    real_three = real.reshape(first, second, width)
    step_real = contract("abm,ak->kbm", real_three, cos_a)
    step_imag = contract("abm,ak->kbm", real_three, sin_a)
    if imag is not None:
        imag_three = imag.reshape(first, second, width)
        step_real = step_real - contract("abm,ak->kbm", imag_three, sin_a)
        step_imag = step_imag + contract("abm,ak->kbm", imag_three, cos_a)
    turned_real = step_real * twist_cos - step_imag * twist_sin
    turned_imag = step_real * twist_sin + step_imag * twist_cos
    out_real = contract("kbm,bj->jkm", turned_real, cos_b) - contract(
        "kbm,bj->jkm", turned_imag, sin_b
    )
    out_imag = contract("kbm,bj->jkm", turned_real, sin_b) + contract(
        "kbm,bj->jkm", turned_imag, cos_b
    )
    return (out_real.reshape(length, width), out_imag.reshape(length, width))


def forward(stacked, order):
    count, block, grid_side = stacked.shape
    owners = grid_side // block
    total = grid_side * grid_side
    send = jnp.transpose(stacked.reshape(count, block, owners, block), (2, 1, 0, 3)).reshape(
        owners, block, count * block
    )
    columns = redistribute(send).reshape(grid_side, count * block)
    first_real, first_imag = axis_dft(columns, None, -1.0)
    first_real = first_real.reshape(grid_side, count, block)
    first_imag = first_imag.reshape(grid_side, count, block)
    col_index = own_block() * block + jnp.arange(block, dtype=jnp.int32)
    cos_turn, sin_turn = turn_angles(order[:, None, None], col_index[None, None, :], total)
    turned_real = first_real * cos_turn + first_imag * sin_turn
    turned_imag = first_imag * cos_turn - first_real * sin_turn
    send_two = jnp.concatenate([turned_real, turned_imag], axis=1).reshape(
        owners, block, 2 * count * block
    )
    gotten = redistribute(send_two).reshape(owners, block, 2 * count, block)
    flat_real = jnp.transpose(gotten[:, :, :count, :], (0, 3, 1, 2)).reshape(
        grid_side, block * count
    )
    flat_imag = jnp.transpose(gotten[:, :, count:, :], (0, 3, 1, 2)).reshape(
        grid_side, block * count
    )
    out_real, out_imag = axis_dft(flat_real, flat_imag, -1.0)
    spec_real = jnp.transpose(out_real.reshape(grid_side, block, count), (1, 2, 0))
    spec_imag = jnp.transpose(out_imag.reshape(grid_side, block, count), (1, 2, 0))
    return (spec_real, spec_imag)


def inverse(spec_real, spec_imag, order):
    block, count, grid_side = spec_real.shape
    owners = grid_side // block
    total = grid_side * grid_side
    flat_real = jnp.transpose(spec_real, (2, 0, 1)).reshape(grid_side, block * count)
    flat_imag = jnp.transpose(spec_imag, (2, 0, 1)).reshape(grid_side, block * count)
    out_real, out_imag = axis_dft(flat_real, flat_imag, 1.0)
    back_real = jnp.transpose(out_real.reshape(owners, block, block, count), (0, 2, 3, 1))
    back_imag = jnp.transpose(out_imag.reshape(owners, block, block, count), (0, 2, 3, 1))
    freq_index = lax.dynamic_slice_in_dim(order, own_block() * block, block, 0)
    col_index = (
        jnp.arange(owners, dtype=jnp.int32)[:, None] * block
        + jnp.arange(block, dtype=jnp.int32)[None, :]
    )
    cos_turn, sin_turn = turn_angles(
        freq_index[None, :, None, None], col_index[:, None, None, :], total
    )
    turned_real = back_real * cos_turn - back_imag * sin_turn
    turned_imag = back_real * sin_turn + back_imag * cos_turn
    send = jnp.concatenate([turned_real, turned_imag], axis=2).reshape(
        owners, block, 2 * count * block
    )
    gotten = redistribute(send).reshape(grid_side, 2 * count * block)
    real_part = gotten[:, : count * block]
    imag_part = gotten[:, count * block :]
    full_real, full_imag = axis_dft(real_part, imag_part, 1.0)
    values = full_real * (1.0 / total)
    returned = redistribute(values.reshape(owners, block, count * block)).reshape(
        owners, block, count, block
    )
    return jnp.transpose(returned, (2, 1, 0, 3)).reshape(count, block, grid_side)


def spread_shards(outer_gate, inner_gate, signal, grad_out, filter_weight):
    grid_side = filter_weight.shape[1]
    freq_index = jnp.arange(grid_side, dtype=jnp.int32)
    outer_f = outer_gate[0].astype(jnp.float32)
    inner_f = inner_gate[0].astype(jnp.float32)
    signal_f = signal[0].astype(jnp.float32)
    grad_f = grad_out[0].astype(jnp.float32)
    channels = inner_f.shape[0]
    gated = inner_f * signal_f
    grad_conv = grad_f * outer_f
    taps = (filter_weight * (1.0 / grid_side))[None]
    spec_real, spec_imag = forward(jnp.concatenate([gated, grad_conv], axis=0), freq_index)
    filt_real, filt_imag = forward(taps, freq_index)
    gated_real = spec_real[:, :channels]
    gated_imag = spec_imag[:, :channels]
    cot_real = spec_real[:, channels : 2 * channels]
    cot_imag = spec_imag[:, channels : 2 * channels]
    conv_real = filt_real * gated_real - filt_imag * gated_imag
    conv_imag = filt_real * gated_imag + filt_imag * gated_real
    back_real = filt_real * cot_real + filt_imag * cot_imag
    back_imag = filt_real * cot_imag - filt_imag * cot_real
    term_real = jnp.sum(gated_real * cot_real + gated_imag * cot_imag, axis=1, keepdims=True)
    term_imag = jnp.sum(gated_real * cot_imag - gated_imag * cot_real, axis=1, keepdims=True)
    values = inverse(
        jnp.concatenate([conv_real, back_real, term_real], axis=1),
        jnp.concatenate([conv_imag, back_imag, term_imag], axis=1),
        freq_index,
    )
    grad_filter = lax.psum(values[2 * channels], "dp") * (1.0 / grid_side)
    conv = values[:channels]
    grad_gated = values[channels : 2 * channels]
    grad_outer = (grad_f * conv).astype(jnp.bfloat16)[None]
    grad_inner = (grad_gated * signal_f).astype(jnp.bfloat16)[None]
    grad_signal = (grad_gated * inner_f).astype(jnp.bfloat16)[None]
    return (grad_outer, grad_inner, grad_signal, grad_filter)


VMEM_LIMIT = 18 * 1024 * 1024
ROW_PAD = 16
LANE_PAD = 128


def up_to(value, unit):
    return -(-value // unit) * unit


def high_low(table):
    high = table.astype(jnp.bfloat16)
    low = (table - high.astype(np.float64)).astype(jnp.bfloat16)
    return np.stack([high, low])


class Plan:
    def __init__(self, side):
        half = side // 2
        self.side, self.half, self.quarter = side, half, side // 4
        self.evens = up_to(half // 2 + 1, ROW_PAD)
        self.odds = half // 2
        self.rows = self.evens + self.odds
        self.even_depth = up_to(2 * self.evens, LANE_PAD)
        total = side * side
        even_k = 2 * np.arange(self.evens)
        odd_k = 2 * np.arange(self.odds) + 1
        live = (even_k <= half).astype(np.float64)
        p = np.arange(half)

        def waves(k, scale):
            angle = 2.0 * np.pi * (k[:, None] * p[None, :] % side) / side
            return np.concatenate([np.cos(angle) * scale[:, None], -np.sin(angle) * scale[:, None]])

        ones = np.ones(self.odds)
        self.into_even = high_low(waves(even_k, live))
        self.into_odd = high_low(waves(odd_k, ones))
        weight = np.where((even_k == 0) | (even_k == half), 1.0, 2.0) * live / total
        back_even = np.zeros((half, self.even_depth))
        back_even[:, : 2 * self.evens] = waves(even_k, weight).T
        self.back_even = high_low(back_even)
        self.back_odd = high_low(waves(odd_k, ones * 2.0 / total).T)
        k = np.concatenate([even_k, odd_k])
        turn = 2.0 * np.pi * (k[:, None] * np.arange(side)[None, :] % total) / total
        self.turn = np.stack([np.cos(turn), np.sin(turn)]).astype(np.float32)
        q = np.arange(self.quarter)
        mixes = []
        for r in range(4):
            angle = 2.0 * np.pi * (q[:, None] * (4 * q[None, :] + r) % side) / side
            cos, sin = np.cos(angle), np.sin(angle)
            mixes.append(np.block([[cos, -sin], [sin, cos]]))
        self.mix = high_low(np.stack(mixes))
        self.row_tile = next(t for t in (176, 264, 16, 8) if self.rows % t == 0)


def split_terms(values):
    high = values.astype(jnp.bfloat16)
    return high, (values - high.astype(jnp.float32)).astype(jnp.bfloat16)


def dot_in(table, rows, high, low):
    dot = functools.partial(jnp.dot, preferred_element_type=jnp.float32)
    first, second = table[0, rows], table[1, rows]
    return dot(first, high) + (dot(first, low) + dot(second, high))


def block_views(plan, owners, me, blocks, values):
    size = plan.side // owners
    for step in range(owners):
        at = pl.multiple_of((me[0] ^ step) * size, size)
        yield blocks[step].at[pl.ds(0, size)], values.at[pl.ds(at, size)]


def tile_views(plan, grid, me, tiles, values):
    parts, rows, cols = grid
    block = plan.side // (rows * cols)
    height = block // parts
    own_row = me[0] // cols
    for part in range(parts):
        for col in range(cols):
            for i in range(rows):
                at = ((own_row ^ i) * cols + col) * block + part * height
                yield tiles[0].at[part * cols + col, i], values.at[pl.ds(pl.multiple_of(at, height), height)]


def start_all(pairs, sems):
    copies = [pltpu.make_async_copy(source, to, sems.at[i]) for i, (source, to) in enumerate(pairs)]
    for copy in copies:
        copy.start()
    return copies


def wait_all(copies):
    for copy in copies:
        copy.wait()


def to_spectrum(plan, values, into_even, into_odd, turn, mix, spec, mid):
    side, half, quarter = plan.side, plan.half, plan.quarter

    @pl.loop(0, side // quarter)
    def columns(tile):
        cols = pl.ds(pl.multiple_of(tile * quarter, quarter), quarter)
        top, bottom = values[pl.ds(0, half), cols], values[pl.ds(half, half), cols]
        for first, count, table, part in (
            (0, plan.evens, into_even, top + bottom),
            (plan.evens, plan.odds, into_odd, top - bottom),
        ):
            out = dot_in(table, slice(None), *split_terms(part))
            real, imag = out[:count], out[count:]
            rows = pl.ds(first, count)
            cos, sin = turn[0, rows, cols], turn[1, rows, cols]
            mid[0, rows, cols] = real * cos + imag * sin
            mid[1, rows, cols] = imag * cos - real * sin

    @pl.loop(0, plan.rows // plan.row_tile)
    def rows_loop(tile):
        rows = pl.ds(pl.multiple_of(tile * plan.row_tile, plan.row_tile), plan.row_tile)
        real = [mid[0, rows, pl.ds(j * quarter, quarter)] for j in range(4)]
        imag = [mid[1, rows, pl.ds(j * quarter, quarter)] for j in range(4)]
        sum_r, sum_i = real[0] + real[2], imag[0] + imag[2]
        dif_r, dif_i = real[0] - real[2], imag[0] - imag[2]
        two_r, two_i = real[1] + real[3], imag[1] + imag[3]
        odd_r, odd_i = real[1] - real[3], imag[1] - imag[3]
        turns = (
            (sum_r + two_r, sum_i + two_i),
            (dif_r + odd_i, dif_i - odd_r),
            (sum_r - two_r, sum_i - two_i),
            (dif_r - odd_i, dif_i + odd_r),
        )
        dot = functools.partial(jnp.dot, preferred_element_type=jnp.float32)
        for r, pair in enumerate(turns):
            high, low = split_terms(jnp.concatenate(pair, axis=1))
            out = dot(high, mix[0, r]) + (dot(low, mix[0, r]) + dot(high, mix[1, r]))
            cols = pl.ds(r * quarter, quarter)
            spec[0, rows, cols] = out[:, :quarter]
            spec[1, rows, cols] = out[:, quarter:]


def inverse_rows(plan, conjugate, left, right, turn, mix, mid):
    quarter = plan.quarter

    @pl.loop(0, plan.rows // plan.row_tile)
    def rows_loop(tile):
        rows = pl.ds(pl.multiple_of(tile * plan.row_tile, plan.row_tile), plan.row_tile)
        real, imag = [], []
        for r in range(4):
            cols = pl.ds(r * quarter, quarter)
            left_r, left_i = left[0, rows, cols], left[1, rows, cols]
            right_r, right_i = right[0, rows, cols], right[1, rows, cols]
            if conjugate:
                left_i = -left_i
            pair = (left_r * right_r - left_i * right_i, left_r * right_i + left_i * right_r)
            high, low = split_terms(jnp.concatenate(pair, axis=1))

            def dot(part, table):
                return lax.dot_general(
                    part, table, (((1,), (1,)), ((), ())), preferred_element_type=jnp.float32
                )

            out = dot(high, mix[0, r]) + (dot(low, mix[0, r]) + dot(high, mix[1, r]))
            real.append(out[:, :quarter])
            imag.append(out[:, quarter:])
        sum_r, sum_i = real[0] + real[2], imag[0] + imag[2]
        dif_r, dif_i = real[0] - real[2], imag[0] - imag[2]
        two_r, two_i = real[1] + real[3], imag[1] + imag[3]
        odd_r, odd_i = real[1] - real[3], imag[1] - imag[3]
        turns = (
            (sum_r + two_r, sum_i + two_i),
            (dif_r - odd_i, dif_i + odd_r),
            (sum_r - two_r, sum_i - two_i),
            (dif_r + odd_i, dif_i - odd_r),
        )
        for j, (got_r, got_i) in enumerate(turns):
            cols = pl.ds(j * quarter, quarter)
            cos, sin = turn[0, rows, cols], turn[1, rows, cols]
            mid[0, rows, cols] = got_r * cos - got_i * sin
            mid[1, rows, cols] = got_r * sin + got_i * cos


def inverse_columns(plan, back_even, back_odd, mid, values):
    side, half, quarter = plan.side, plan.half, plan.quarter

    @pl.loop(0, side // quarter)
    def columns(tile):
        cols = pl.ds(pl.multiple_of(tile * quarter, quarter), quarter)
        even = [mid[0, pl.ds(0, plan.evens), cols], mid[1, pl.ds(0, plan.evens), cols]]
        if plan.even_depth > 2 * plan.evens:
            even.append(jnp.zeros((plan.even_depth - 2 * plan.evens, quarter), jnp.float32))
        odd = [mid[0, pl.ds(plan.evens, plan.odds), cols], mid[1, pl.ds(plan.evens, plan.odds), cols]]
        from_even = dot_in(back_even, slice(None), *split_terms(jnp.concatenate(even)))
        from_odd = dot_in(back_odd, slice(None), *split_terms(jnp.concatenate(odd)))
        values[pl.ds(0, half), cols] = from_even + from_odd
        values[pl.ds(half, half), cols] = from_even - from_odd


def filter_kernel(plan, views, count, me, *refs):
    tiles = refs[:count]
    into_even, into_odd, turn, mix, spec, values, mid, sems = refs[count:]
    wait_all(start_all(views(me, tiles, values), sems))
    to_spectrum(plan, values, into_even, into_odd, turn, mix, spec, mid)


def conv_kernel(plan, views, count, me, filt, *refs):
    blocks, tables = refs[:count], refs[count : count + 6]
    into_even, into_odd, back_even, back_odd, turn, mix = tables
    spec, outs = refs[count + 6], refs[count + 7 : 2 * count + 7]
    values, mid, sems = refs[2 * count + 7 :]
    wait_all(start_all(views(me, blocks, values), sems))
    to_spectrum(plan, values, into_even, into_odd, turn, mix, spec, mid)
    inverse_rows(plan, False, filt, spec, turn, mix, mid)
    inverse_columns(plan, back_even, back_odd, mid, values)
    wait_all(start_all(((to, source) for source, to in views(me, outs, values)), sems))


def term_kernel(plan, views, term_views, count, me, gated, *refs):
    blocks, tables = refs[:count], refs[count : count + 6]
    into_even, into_odd, back_even, back_odd, turn, mix = tables
    spec, term, values, mid, sems, term_sems = refs[count + 6 :]
    wait_all(start_all(views(me, blocks, values), sems))
    to_spectrum(plan, values, into_even, into_odd, turn, mix, spec, mid)
    inverse_rows(plan, True, gated, spec, turn, mix, mid)
    inverse_columns(plan, back_even, back_odd, mid, values)
    wait_all(start_all(((to, source) for source, to in term_views(me, [term], values)), term_sems))


def grad_kernel(plan, views, count, me, filt, spec, back_even, back_odd, turn, mix, *refs):
    outs = refs[:count]
    values, mid, sems = refs[count:]
    inverse_rows(plan, True, filt, spec, turn, mix, mid)
    inverse_columns(plan, back_even, back_odd, mid, values)
    wait_all(start_all(((to, source) for source, to in views(me, outs, values)), sems))


def smem():
    return pl.BlockSpec(memory_space=pltpu.SMEM)


def vmem():
    return pl.BlockSpec(memory_space=pltpu.VMEM)


def anywhere():
    return pl.BlockSpec(memory_space=pl.ANY)


def kernel_cost(plan):
    return pl.CostEstimate(flops=plan.side**2, bytes_accessed=plan.side**2, transcendentals=0)


def call_kernel(plan, kernel, name, args, in_specs, out_shape, out_specs, scratch):
    return pl.pallas_call(
        kernel,
        out_shape=out_shape,
        in_specs=in_specs,
        out_specs=out_specs,
        scratch_shapes=scratch,
        compiler_params=pltpu.CompilerParams(vmem_limit_bytes=VMEM_LIMIT),
        cost_estimate=kernel_cost(plan),
        name=name,
    )(*args)


def float_array(shape):
    return jax.ShapeDtypeStruct(shape, jnp.float32)


def filter_spectrum(plan, me, tiles, views, copies):
    shape = (2, plan.rows, plan.side)
    return call_kernel(
        plan,
        functools.partial(filter_kernel, plan, views, len(tiles)),
        "filter_spectrum",
        (me, *tiles, plan.into_even, plan.into_odd, plan.turn, plan.mix),
        [smem()] + [anywhere()] * len(tiles) + [vmem()] * 4,
        float_array(shape),
        vmem(),
        [
            pltpu.VMEM((plan.side, plan.side), jnp.float32),
            pltpu.VMEM(shape, jnp.float32),
            pltpu.SemaphoreType.DMA((copies,)),
        ],
    )


def tables_of(plan):
    return (plan.into_even, plan.into_odd, plan.back_even, plan.back_odd, plan.turn, plan.mix)


def conv_of(plan, me, filt, blocks, views):
    count = len(blocks)
    shape = (2, plan.rows, plan.side)
    spec, *outs = call_kernel(
        plan,
        functools.partial(conv_kernel, plan, views, count),
        "conv_of",
        (me, filt, *blocks, *tables_of(plan)),
        [smem(), vmem()] + [vmem()] * count + [vmem()] * 6,
        [float_array(shape)] + [float_array((plan.side // count, plan.side))] * count,
        [vmem()] * (count + 1),
        [
            pltpu.VMEM((plan.side, plan.side), jnp.float32),
            pltpu.VMEM(shape, jnp.float32),
            pltpu.SemaphoreType.DMA((count,)),
        ],
    )
    return spec, outs


def term_of(plan, me, gated, blocks, views, term_shape, term_views):
    count = len(blocks)
    shape = (2, plan.rows, plan.side)
    return call_kernel(
        plan,
        functools.partial(term_kernel, plan, views, term_views, count),
        "term_of",
        (me, gated, *blocks, *tables_of(plan)),
        [smem(), vmem()] + [vmem()] * count + [vmem()] * 6,
        [float_array(shape), float_array(term_shape)],
        [vmem(), anywhere()],
        [
            pltpu.VMEM((plan.side, plan.side), jnp.float32),
            pltpu.VMEM(shape, jnp.float32),
            pltpu.SemaphoreType.DMA((count,)),
            pltpu.SemaphoreType.DMA((math.prod(term_shape[:2]),)),
        ],
    )


def grad_of(plan, me, filt, spec, count, views):
    return call_kernel(
        plan,
        functools.partial(grad_kernel, plan, views, count),
        "grad_of",
        (me, filt, spec, *tables_of(plan)[2:]),
        [smem()] + [vmem()] * 6,
        [float_array((plan.side // count, plan.side))] * count,
        [vmem()] * count,
        [
            pltpu.VMEM((plan.side, plan.side), jnp.float32),
            pltpu.VMEM((2, plan.rows, plan.side), jnp.float32),
            pltpu.SemaphoreType.DMA((count,)),
        ],
    )


def pairwise(block, axis, step):
    return lax.ppermute(block, axis, [(i, i ^ step) for i in range(lax.axis_size(axis))])


def after(first, then):
    return lax.optimization_barrier((first, then))[1]


def gate_kernel(steps, gates, me, *refs):
    count = len(steps)
    blocks = refs[:count]
    ins = refs[count : count + gates]
    outs, got, sems = refs[-gates - 2 : -2], refs[-2], refs[-1]
    here = pl.program_id(0)

    def copy_of(i):
        return pltpu.make_async_copy(blocks[i], got.at[i], sems.at[i])

    @pl.when(here == 0)
    def start():
        for i in range(count):
            copy_of(i).start()

    for i in range(count):

        @pl.when(here == i)
        def wait():
            copy_of(i).wait()

    values = got[here]
    for gate, out in zip(ins, outs):
        out[0] = (gate[0].astype(jnp.float32) * values).astype(jnp.bfloat16)


def gated_by(me, steps, blocks, gates, done=()):
    count = len(steps)
    shape = gates[0].shape

    def place(i, me):
        step = steps[-1]
        for j in range(count - 1):
            step = jnp.where(i == j, steps[j], step)
        return (me[0] ^ step, 0, 0)

    spec = pl.BlockSpec((1,) + shape[1:], place)
    size = count * shape[1] * shape[2]
    first_done = 1 + count + len(gates)
    return pl.pallas_call(
        functools.partial(gate_kernel, steps, len(gates)),
        grid_spec=pltpu.PrefetchScalarGridSpec(
            num_scalar_prefetch=1,
            grid=(count,),
            in_specs=[anywhere()] * count + [spec] * len(gates) + [anywhere()] * len(done),
            out_specs=[spec] * len(gates),
            scratch_shapes=[
                pltpu.VMEM((count,) + shape[1:], jnp.float32),
                pltpu.SemaphoreType.DMA((count,)),
            ],
        ),
        out_shape=[jax.ShapeDtypeStruct(shape, jnp.bfloat16)] * len(gates),
        input_output_aliases={first_done + i: i for i in range(len(done))},
        compiler_params=pltpu.CompilerParams(vmem_limit_bytes=VMEM_LIMIT),
        cost_estimate=pl.CostEstimate(
            flops=size * len(gates), bytes_accessed=4 * size * (1 + len(gates)), transcendentals=0
        ),
        name="gate_out",
    )(me, *blocks, *gates, *done)


def send_order(owners, cols):
    far = sorted(range(owners // 2, owners), key=lambda s: (-s // cols, -s))
    near = sorted(range(1, owners // 2), key=lambda s: (s % cols, -s))
    return far, near


def channel_shards(outer_gate, inner_gate, signal, grad_out, filter_weight):
    block, side = filter_weight.shape
    plan = Plan(side)
    parts, rows, cols = (lax.axis_size(name) for name in ("dp", "row", "col"))
    owners = rows * cols
    place = own_block()
    me = jnp.reshape(place, (1,)).astype(jnp.int32)
    far, near = send_order(owners, cols)
    order = far[:2]
    for i in range(2, len(far)):
        order = order + near[i - 2 : i - 1] + far[i : i + 1]
    order = order[:-1] + near[len(far) - 2 :] + order[-1:]
    last_order = far[:-1] + near + far[-1:]
    by_block = functools.partial(block_views, plan, owners)
    by_tile = functools.partial(tile_views, plan, (parts, rows, cols))

    def gated_block(left, right, step):
        at = place ^ step
        return lax.dynamic_index_in_dim(left[0], at, 0, False).astype(
            jnp.float32
        ) * lax.dynamic_index_in_dim(right[0], at, 0, False).astype(jnp.float32)

    crossed, neared = [], []

    def exchange(blocks, what, order, deep=3, near_wait=0):
        got = [blocks[0]] + [None] * (owners - 1)
        before, near_before = len(crossed), list(neared)
        neared.clear()
        for step in order:
            mine, waits = blocks[step], []
            if step in far:
                waits = crossed[max(0, len(crossed) - deep - 1) : max(0, len(crossed) - deep + 1)]
                if len(crossed) - before >= len(far) // 2:
                    waits = waits + near_before
            elif before:
                waits = crossed[before - 1 + near_wait : before + near_wait]
            if waits:
                mine = after(waits, mine)
            with jax.named_scope(f"{what}_{step}"):
                got[step] = pairwise(mine, ("row", "col"), step)
            (crossed if step in far else neared).append(got[step])
        return got

    height = block // parts
    own_part = lax.dynamic_slice_in_dim(filter_weight, lax.axis_index("dp") * height, height, 0)
    own_part = own_part * (1.0 / side)
    inner, values = inner_gate, signal
    gated = [None] * owners
    for step in order + [0]:
        gated[step] = gated_block(inner, values, step)
        if step and step % cols == 0:
            gated[step] = jnp.concatenate([gated[step], own_part])
        if step == order[0]:
            inner, values = after(gated[step], [inner_gate, signal])
    gated = exchange(gated, "gated", order)
    over_row = jnp.stack([own_part] + [gated[i * cols][block:] for i in range(1, rows)])
    grad_conv = [gated_block(grad_out, outer_gate, step) for step in range(owners)]
    over_row = after(gated + grad_conv, over_row)
    over_all = [lax.all_gather(over_row, ("dp", "col"))]
    filt = filter_spectrum(plan, me, over_all, by_tile, parts * owners)

    got = exchange(grad_conv, "grad_conv", [step for step in order if step != near[-1]], 4)
    spec, conv_out = conv_of(plan, me, filt, after([filt] + [got[step] for step in far[:1]], gated), by_block)
    with jax.named_scope(f"grad_conv_{near[-1]}"):
        got[near[-1]] = pairwise(after(conv_out[0], grad_conv[near[-1]]), ("row", "col"), near[-1])
    grad_conv = got
    conv = exchange(conv_out, "conv", order, 4)
    tile_shape = (parts * cols, rows, height, side)
    cot, term = term_of(plan, me, spec, grad_conv, by_block, tile_shape, by_tile)
    back_out = grad_of(plan, me, filt, cot, owners, by_block)
    term = after([conv[step] for step in far[:2]], term)
    term = lax.psum_scatter(term, ("dp", "col"), scatter_dimension=0, tiled=False)
    with jax.named_scope("rows_sum"):
        arrived = [pairwise(term[i], "row", i) for i in range(1, rows)]
    total = sum(arrived, term[0]) * (1.0 / side)
    back_out = list(back_out)
    for step in far[3:] + near:
        back_out[step] = after(total, back_out[step])
    grad_gated = exchange(back_out, "grad_gated", last_order, 3, 1)
    every = [0] + order
    (grad_outer,) = gated_by(me, every, [conv[step] for step in every], [grad_out[0]])
    total = after([grad_outer, grad_gated[far[0]], grad_gated[far[2]]], total)
    with jax.named_scope("parts_gather"):
        others = [pairwise(total, "dp", i) for i in range(1, parts)]
    pieces = jnp.stack([total] + others)
    bit = 1
    while bit < parts:
        upper = (lax.axis_index("dp") & bit) != 0
        swapped = jnp.flip(pieces.reshape(parts // (2 * bit), 2, bit, height, side), 1)
        pieces = jnp.where(upper, swapped.reshape(pieces.shape), pieces)
        bit *= 2
    grad_filter = pieces.reshape(block, side)

    every = [0] + near + far
    gates = [signal[0], inner_gate[0]]
    early, late = every[:-1], every[-1:]
    done = gated_by(me, early, [grad_gated[step] for step in early], gates)
    grad_inner, grad_signal = gated_by(me, late, [grad_gated[step] for step in late], gates, done)
    return (grad_outer[None], grad_inner[None], grad_signal[None], grad_filter)


def powers_of_two(*sizes):
    return all(size & (size - 1) == 0 for size in sizes)


def shards(*arrays):
    parts, rows, cols = (lax.axis_size(name) for name in ("dp", "row", "col"))
    side = arrays[0].shape[3]
    whole = arrays[0].shape[1] == rows * cols and rows >= 2 and cols == 2
    fits = powers_of_two(parts, rows, cols, side) and side // 4 % LANE_PAD == 0
    fits = fits and arrays[4].shape[0] // parts % ROW_PAD == 0
    return (channel_shards if whole and fits else spread_shards)(*arrays)


def solution(mesh):
    placed = (
        P("dp", None, ("row", "col"), None),
        P("dp", None, ("row", "col"), None),
        P("dp", None, ("row", "col"), None),
        P("dp", None, ("row", "col"), None),
        P(("row", "col"), None),
    )
    return jax.shard_map(
        shards,
        mesh=mesh,
        in_specs=placed,
        out_specs=(
            P("dp", None, ("row", "col"), None),
            P("dp", None, ("row", "col"), None),
            P("dp", None, ("row", "col"), None),
            P(("row", "col"), None),
        ),
        check_vma=False,
    )
```
